32 devices in a mesh: dp: 8 (over z, x), mp: 4 (over y, core).
Axes of the slice: x: 2, y: 2, z: 4, core: 2. Of those that a mesh axis runs over, the one named last changes fastest.
Arguments:
- tokens: bfloat16 [8, 1024, 1024], P('dp', 'mp'), may hold values from -6 to 6
- seg_lengths: int32 [8, 2], P('dp'), may hold values from 1 to 896, 1024 in all within a row
- cotangent: bfloat16 [8, 1024, 1024], P('dp', 'mp'), may hold values from -6 to 6
- mixer_norm_gain: float32 [2, 1024], replicated, may hold values from 0.5 to 1.5
- mixer_norm_bias: float32 [2, 1024], replicated, may hold values from -3 to 3
- in_weight: bfloat16 [2, 1024, 3, 1024], P(None, None, None, 'mp'), may hold values from -0.1875 to 0.1875
- in_bias: float32 [2, 3, 1024], P(None, None, 'mp'), may hold values from -3 to 3
- conv_weight: float32 [2, 3, 3, 1024], P(None, None, None, 'mp'), may hold values from -3 to 3
- conv_bias: float32 [2, 3, 1024], P(None, None, 'mp'), may hold values from -3 to 3
- filter_in: float32 [2, 33, 64], replicated, may hold values from -1 to 1
- filter_in_bias: float32 [2, 64], replicated, may hold values from -4 to 4
- filter_in_freq: float32 [2, 64], replicated, may hold values from 0.1 to 1.9
- filter_mid: float32 [2, 64, 64], replicated, may hold values from -0.75 to 0.75
- filter_mid_bias: float32 [2, 64], replicated, may hold values from -4 to 4
- filter_mid_freq: float32 [2, 64], replicated, may hold values from 0.1 to 1.9
- filter_out: float32 [2, 64, 1024], P(None, None, 'mp'), may hold values from -0.09375 to 0.09375
- skip_bias: float32 [2, 1024], P(None, 'mp'), may hold values from -4 to 4
- out_weight: bfloat16 [2, 1024, 1024], P(None, 'mp'), may hold values from -0.1875 to 0.1875
- out_bias: float32 [2, 1024], replicated, may hold values from -3 to 3
- feed_norm_gain: float32 [2, 1024], replicated, may hold values from 0.5 to 1.5
- feed_norm_bias: float32 [2, 1024], replicated, may hold values from -3 to 3
- feed_up: bfloat16 [2, 1024, 4096], P(None, None, 'mp'), may hold values from -0.1875 to 0.1875
- feed_up_bias: float32 [2, 4096], P(None, 'mp'), may hold values from -3 to 3
- feed_down: bfloat16 [2, 4096, 1024], P(None, 'mp'), may hold values from -0.09375 to 0.09375
- feed_down_bias: float32 [2, 1024], replicated, may hold values from -3 to 3
Outputs:
- outputs: float32 [8, 1024, 1024], P('dp', 'mp')
- token_grad: float32 [8, 1024, 1024], P('dp', 'mp')
- mixer_norm_gain_grad: float32 [2, 1024], replicated
- mixer_norm_bias_grad: float32 [2, 1024], replicated
- in_weight_grad: float32 [2, 1024, 3, 1024], P(None, 'dp', None, 'mp')
- in_bias_grad: float32 [2, 3, 1024], P(None, None, 'mp')
- conv_weight_grad: float32 [2, 3, 3, 1024], P(None, None, None, 'mp')
- conv_bias_grad: float32 [2, 3, 1024], P(None, None, 'mp')
- filter_in_grad: float32 [2, 33, 64], replicated
- filter_in_bias_grad: float32 [2, 64], replicated
- filter_in_freq_grad: float32 [2, 64], replicated
- filter_mid_grad: float32 [2, 64, 64], replicated
- filter_mid_bias_grad: float32 [2, 64], replicated
- filter_mid_freq_grad: float32 [2, 64], replicated
- filter_out_grad: float32 [2, 64, 1024], P(None, None, 'mp')
- skip_bias_grad: float32 [2, 1024], P(None, 'mp')
- out_weight_grad: float32 [2, 1024, 1024], P(None, 'mp', 'dp')
- out_bias_grad: float32 [2, 1024], replicated
- feed_norm_gain_grad: float32 [2, 1024], replicated
- feed_norm_bias_grad: float32 [2, 1024], replicated
- feed_up_grad: float32 [2, 1024, 4096], P(None, 'dp', 'mp')
- feed_up_bias_grad: float32 [2, 4096], P(None, 'mp')
- feed_down_grad: float32 [2, 4096, 1024], P(None, 'mp', 'dp')
- feed_down_bias_grad: float32 [2, 1024], replicated
The draws below stay inside these ranges and needn't reach their ends.
Inputs may be any that keep to these rules, and one draw needn't show every extreme that they name: `seg_lengths`: each row's 2 segment lengths sum to 1024; none is longer than 896.
All inputs are finite; a program needn't handle non-finite values.
Results may differ from the reference program's by a relative error of at most 0.023.
Values may be sent and summed in bfloat16 or wider, within the bound.
No kernel may reach another device: no remote copies, remote signals or barrier semaphores. Data moves between devices by JAX's collectives and lax.ppermute only.
A program may use at most 256 MiB of HBM per device.

```python
import math
import jax
import jax.numpy as jnp
import numpy as np
from jax import lax

D = 1024
FF = 4096
POS = 33
FILT = 64
STREAMS = 3
SHORT = 3
ROW_LEN = 1024
SEGS = 2
LAYERS = 2
SEG_MOST = 896
ROWS = 8


def level_of(own_key, dims, cuts, least, largest):
    gain = 1.0
    for position, blocks in cuts:
        draws = jax.random.uniform(jax.random.fold_in(jax.random.fold_in(own_key, 6), position), (blocks,), jnp.float32, least / len(cuts), largest / len(cuts))
        gain = gain * jnp.repeat(jnp.exp(draws), dims[position] // blocks).reshape((-1,) + (1,) * (len(dims) - 1 - position))
    return gain


def split_up(amount, total, reach, slope):
    portions = [(1 << 20) // math.isqrt(grade ** slope) + 1 for grade in range(2, amount + 1)]
    spare, holding = total - reach - (amount - 1), [1] * (amount - 1)
    while spare > 0:
        free = [i for i in range(amount - 1) if holding[i] < reach]
        mass, budget = sum([portions[i] for i in free]), spare
        for i in free:
            addition = min(reach - holding[i], max(1, budget * portions[i] // mass), spare)
            holding[i] = holding[i] + addition
            spare = spare - addition
    return np.array([reach] + holding)


def uneven(key, amount, total, bound, lean):
    if amount == 2:
        one = jax.random.randint(key, (), max(1, total - bound), min(bound, total - 1) + 1)
        return jnp.stack([one, total - one])
    sizes = jnp.asarray(split_up(amount, total, bound, lean), jnp.int32)
    couples = (amount - 1) // 2
    giver, receiver = sizes[1:1 + 2 * couples:2], sizes[2:2 + 2 * couples:2]
    room = jnp.minimum(giver - 1, bound - receiver)
    passed = jax.random.randint(jax.random.fold_in(key, 1), (couples,), 0, 1 << 20) % (room + 1)
    sizes = sizes.at[1:1 + 2 * couples:2].set(giver - passed).at[2:2 + 2 * couples:2].set(receiver + passed)
    return sizes[jax.random.permutation(jax.random.fold_in(key, 2), amount)]


def normal_values(rng, shape, scale, bound, cuts=(), held_as=jnp.bfloat16):
    factor_of = level_of(rng, shape, cuts, -0.22, 0.18) if cuts else 1.0
    array = jax.random.normal(rng, shape, jnp.float32) * scale * factor_of
    return jnp.minimum(jnp.maximum(array, -bound), bound).astype(held_as)


def setup_inputs(seed: int = 0) -> dict:
    key_list = jax.random.split(jax.random.key(seed), 26)
    return {
        "tokens": normal_values(key_list[0], (ROWS, ROW_LEN, D), 1.0, 6.0, ((0, 8), (1, 4))),
        "seg_lengths": jax.vmap(lambda own: uneven(own, SEGS, ROW_LEN, SEG_MOST, 2))(jax.random.split(key_list[1], ROWS)).reshape((ROWS, SEGS)).astype(jnp.int32),
        "cotangent": normal_values(key_list[2], (ROWS, ROW_LEN, D), 1.0, 6.0, ((0, 8), (1, 4))),
        "mixer_norm_gain": jnp.clip(1.0 + 0.1 * jax.random.normal(key_list[3], (LAYERS, D), jnp.float32), 0.5, 1.5),
        "mixer_norm_bias": normal_values(key_list[4], (LAYERS, D), 0.3, 3.0, (), jnp.float32),
        "in_weight": normal_values(key_list[5], (LAYERS, D, STREAMS, D), D ** -0.5, 0.1875, ((3, 4),)),
        "in_bias": normal_values(key_list[6], (LAYERS, STREAMS, D), 0.3, 3.0, ((2, 4),), jnp.float32),
        "conv_weight": normal_values(key_list[7], (LAYERS, STREAMS, SHORT, D), 0.6, 3.0, ((3, 4),), jnp.float32),
        "conv_bias": normal_values(key_list[8], (LAYERS, STREAMS, D), 0.3, 3.0, ((2, 4),), jnp.float32),
        "filter_in": normal_values(key_list[9], (LAYERS, POS, FILT), POS ** -0.5, 1.0, (), jnp.float32),
        "filter_in_bias": normal_values(key_list[10], (LAYERS, FILT), 1.0, 4.0, (), jnp.float32),
        "filter_in_freq": jnp.clip(1.0 + 0.18 * jax.random.normal(key_list[11], (LAYERS, FILT), jnp.float32), 0.1, 1.9),
        "filter_mid": normal_values(key_list[12], (LAYERS, FILT, FILT), FILT ** -0.5, 0.75, (), jnp.float32),
        "filter_mid_bias": normal_values(key_list[13], (LAYERS, FILT), 1.0, 4.0, (), jnp.float32),
        "filter_mid_freq": jnp.clip(1.0 + 0.18 * jax.random.normal(key_list[14], (LAYERS, FILT), jnp.float32), 0.1, 1.9),
        "filter_out": normal_values(key_list[15], (LAYERS, FILT, D), (FILT * ROW_LEN // 16) ** -0.5, 0.09375, ((2, 4),), jnp.float32),
        "skip_bias": normal_values(key_list[16], (LAYERS, D), 1.0, 4.0, ((1, 4),), jnp.float32),
        "out_weight": normal_values(key_list[17], (LAYERS, D, D), D ** -0.5, 0.1875, ((1, 4),)),
        "out_bias": normal_values(key_list[18], (LAYERS, D), 0.3, 3.0, (), jnp.float32),
        "feed_norm_gain": jnp.clip(1.0 + 0.1 * jax.random.normal(key_list[19], (LAYERS, D), jnp.float32), 0.5, 1.5),
        "feed_norm_bias": normal_values(key_list[20], (LAYERS, D), 0.3, 3.0, (), jnp.float32),
        "feed_up": normal_values(key_list[21], (LAYERS, D, FF), D ** -0.5, 0.1875, ((2, 4),)),
        "feed_up_bias": normal_values(key_list[22], (LAYERS, FF), 0.3, 3.0, ((1, 4),), jnp.float32),
        "feed_down": normal_values(key_list[23], (LAYERS, FF, D), FF ** -0.5, 0.09375, ((1, 4),)),
        "feed_down_bias": normal_values(key_list[24], (LAYERS, D), 0.3, 3.0, (), jnp.float32),
    }


highest = lax.Precision.HIGHEST
norm_eps = 1e-05
slow_rate = math.log(100.0) / 1.5
fast_rate = math.log(100.0) / 0.3

@jax.custom_vjp
def low(v):
    return lax.optimization_barrier(v.astype(jnp.bfloat16)).astype(jnp.float32)

@jax.custom_vjp
def low_back(v):
    return v

def low_keep(v):
    return (low(v), None)

def low_pass(kept, grad):
    return (grad,)

def back_keep(v):
    return (v, None)

def back_low(kept, grad):
    return (low(grad),)
low.defvjp(low_keep, low_pass)
low_back.defvjp(back_keep, back_low)

def segment_tables(lengths, length):
    seg_ends = jnp.cumsum(lengths).astype(jnp.int32)
    starts = (seg_ends - lengths).astype(jnp.int32)
    places = jnp.arange(length, dtype=jnp.int32)
    inside = (places[None, :] >= starts[:, None]) & (places[None, :] < seg_ends[:, None])
    seg_masks = inside.astype(jnp.float32)
    seg_offset = lax.optimization_barrier(jnp.sum(jnp.where(inside, places[None, :] - starts[:, None], 0), axis=0)).astype(jnp.int32)
    return (seg_masks, seg_offset)

def position_table(length):
    places = jnp.arange(length, dtype=jnp.int32).astype(jnp.float32)
    band_count = (POS - 1) // 2
    band_index = jnp.arange(band_count, dtype=jnp.int32).astype(jnp.float32)
    band_freq = 0.0001 + band_index * ((band_count - 1 - 0.0001) / (band_count - 1))
    phases = places[:, None] * band_freq[None, :] * (2.0 * math.pi / length)
    return jnp.concatenate([places[:, None] / (length - 1), jnp.cos(phases), -jnp.sin(phases)], axis=1)

def decay_window(length, chan_index):
    places = jnp.arange(length, dtype=jnp.int32).astype(jnp.float32)
    decay_rates = slow_rate + (fast_rate - slow_rate) * chan_index / (D - 1)
    return jnp.exp(-(places[:, None] / (length - 1)) * decay_rates[None, :])

def make_taps(filter_in, filter_in_bias, filter_in_freq, filter_mid, filter_mid_bias, filter_mid_freq, filter_out, pos_table):
    hidden = jnp.sin(filter_in_freq * (jnp.dot(pos_table, filter_in, precision=highest) + filter_in_bias))
    hidden = jnp.sin(filter_mid_freq * (jnp.dot(hidden, filter_mid, precision=highest) + filter_mid_bias))
    return jnp.dot(hidden, filter_out, precision=highest)

def layer_norm(values, gain_row, shift_row):
    center = values - lax.optimization_barrier(jnp.mean(values, axis=-1, keepdims=True))
    spread = lax.optimization_barrier(jnp.mean(center * center, axis=-1, keepdims=True))
    return center * lax.rsqrt(spread + norm_eps) * gain_row + shift_row

def short_conv(proj_in, conv_weight, seg_offset):
    summed = proj_in * conv_weight[:, 0]
    for lag_index in range(1, conv_weight.shape[1]):
        shifted = jnp.pad(proj_in[:-lag_index], ((lag_index, 0), (0, 0), (0, 0)))
        kept_mask = (seg_offset >= lag_index).astype(jnp.float32)
        summed = summed + shifted * conv_weight[:, lag_index] * kept_mask[:, None, None]
    return summed

def long_conv(values, filter_taps, seg_masks):
    length = values.shape[0]
    pieces = seg_masks[:, :, None] * values[None]
    spectrum = jnp.fft.rfft(pieces, n=2 * length, axis=1) * jnp.fft.rfft(filter_taps, n=2 * length, axis=0)[None]
    results = jnp.fft.irfft(spectrum, n=2 * length, axis=1)[:, :length]
    return lax.optimization_barrier(jnp.sum(seg_masks[:, :, None] * results, axis=0))

def mixer(proj_in, conv_weight, conv_bias, filter_in, filter_in_bias, filter_in_freq, filter_mid, filter_mid_bias, filter_mid_freq, filter_out, skip_bias, pos_table, window, seg_masks, seg_offset):
    shorted = short_conv(proj_in, conv_weight, seg_offset) + conv_bias
    filter_taps = make_taps(filter_in, filter_in_bias, filter_in_freq, filter_mid, filter_mid_bias, filter_mid_freq, filter_out, pos_table) * window
    gated = shorted[:, 2] * shorted[:, 1]
    longc = long_conv(gated, filter_taps, seg_masks) + skip_bias * gated
    return longc * shorted[:, 0]

def layer_forward(residual, params, seg_masks, seg_offset, pos_table, window):
    norm_gain, norm_shift, in_weight, in_bias, conv_weight, conv_bias, filter_in, filter_in_bias, filter_in_freq, filter_mid, filter_mid_bias, filter_mid_freq, filter_out, skip_bias, out_weight, out_bias, feed_gain, feed_shift, feed_up, feed_up_bias, feed_down, feed_down_bias = params
    normed = low(layer_norm(residual, norm_gain, norm_shift))
    proj_in = low_back(jnp.einsum('td,dkc->tkc', normed, in_weight, precision=highest)) + in_bias
    mixed = low(mixer(proj_in, conv_weight, conv_bias, filter_in, filter_in_bias, filter_in_freq, filter_mid, filter_mid_bias, filter_mid_freq, filter_out, skip_bias, pos_table, window, seg_masks, seg_offset))
    middle = residual + low_back(jnp.dot(mixed, out_weight, precision=highest)) + out_bias
    feed_rows = low(layer_norm(middle, feed_gain, feed_shift))
    preact = low_back(jnp.dot(feed_rows, feed_up, precision=highest)) + feed_up_bias
    hidden = low(jax.nn.gelu(preact, approximate=True))
    return middle + low_back(jnp.dot(hidden, feed_down, precision=highest)) + feed_down_bias

def run_layers(weights, residual, seg_masks, seg_offset, pos_table, window):
    for layer_index in range(LAYERS):
        params = tuple((member[layer_index] for member in weights))
        residual = layer_forward(residual, params, seg_masks, seg_offset, pos_table, window)
    return residual

def reference(tokens, seg_lengths, cotangent, mixer_norm_gain, mixer_norm_bias, in_weight, in_bias, conv_weight, conv_bias, filter_in, filter_in_bias, filter_in_freq, filter_mid, filter_mid_bias, filter_mid_freq, filter_out, skip_bias, out_weight, out_bias, feed_norm_gain, feed_norm_bias, feed_up, feed_up_bias, feed_down, feed_down_bias):
    weights = tuple((member.astype(jnp.float32) for member in (mixer_norm_gain, mixer_norm_bias, in_weight, in_bias, conv_weight, conv_bias, filter_in, filter_in_bias, filter_in_freq, filter_mid, filter_mid_bias, filter_mid_freq, filter_out, skip_bias, out_weight, out_bias, feed_norm_gain, feed_norm_bias, feed_up, feed_up_bias, feed_down, feed_down_bias)))
    pos_table = position_table(ROW_LEN)
    window = decay_window(ROW_LEN, jnp.arange(D, dtype=jnp.int32).astype(jnp.float32))

    def one_row(totals, inputs):
        row_tokens, row_lengths, row_cot = inputs
        seg_masks, seg_offset = segment_tables(row_lengths, ROW_LEN)

        def forward(params, residual):
            return run_layers(params, residual, seg_masks, seg_offset, pos_table, window)
        results, pullback = jax.vjp(forward, weights, row_tokens.astype(jnp.float32))
        weight_grads, row_grads = pullback(row_cot.astype(jnp.float32))
        totals = jax.tree.map(jnp.add, totals, weight_grads)
        return (totals, (results, row_grads))
    zero_grads = jax.tree.map(jnp.zeros_like, weights)
    totals, (results, row_grads) = lax.scan(one_row, zero_grads, (tokens, seg_lengths, cotangent))
    return (results, row_grads, totals[0], totals[1], totals[2], totals[3], totals[4], totals[5], totals[6], totals[7], totals[8], totals[9], totals[10], totals[11], totals[12], totals[13], totals[14], totals[15], totals[16], totals[17], totals[18], totals[19], totals[20], totals[21])
```

```python
import math

import jax
import jax.numpy as jnp
import ml_dtypes
import numpy as np
from jax import lax
from jax.sharding import PartitionSpec as P

D = 1024
POS = 33
REACH = 896
WAVES = 2 * REACH
SHORT = 3

f32 = jnp.float32
bf16 = jnp.bfloat16
highest = lax.Precision.HIGHEST
norm_eps = 1e-05
slow_rate = math.log(100.0) / 1.5
fast_rate = math.log(100.0) / 0.3
GELU_A = math.sqrt(2.0 / math.pi)
GELU_B = 0.044715


def wave_table(length):
    freq = 2 * np.arange(REACH, dtype=np.int64) + 1
    phase = (freq[:, None] * np.arange(length, dtype=np.int64)[None, :]) % (2 * WAVES)
    angle = phase.astype(np.float64) * (math.pi / WAVES)
    return np.concatenate([np.cos(angle), -np.sin(angle)], axis=0).astype(ml_dtypes.bfloat16)


def position_table(length, rows):
    places = jnp.arange(rows, dtype=jnp.int32).astype(f32)
    band_count = (POS - 1) // 2
    band_index = jnp.arange(band_count, dtype=jnp.int32).astype(f32)
    band_freq = 0.0001 + band_index * ((band_count - 1 - 0.0001) / (band_count - 1))
    phases = places[:, None] * band_freq[None, :] * (2.0 * math.pi / length)
    return jnp.concatenate(
        [places[:, None] / (length - 1), jnp.cos(phases), -jnp.sin(phases)], axis=1
    )


def decay_window(length, rows, chan_index):
    places = jnp.arange(rows, dtype=jnp.int32).astype(f32)
    decay_rates = slow_rate + (fast_rate - slow_rate) * chan_index / (D - 1)
    return jnp.exp(-(places[:, None] / (length - 1)) * decay_rates[None, :])


def make_taps(w_in, b_in, f_in, w_mid, b_mid, f_mid, w_out, pos_table):
    hidden = jnp.sin(f_in * (jnp.dot(pos_table, w_in, precision=highest) + b_in))
    hidden = jnp.sin(f_mid * (jnp.dot(hidden, w_mid, precision=highest) + b_mid))
    return jnp.dot(hidden, w_out, precision=highest)


def core_swap(x):
    size = lax.axis_size("mp")
    return lax.ppermute(x, "mp", [(i, i ^ 1) for i in range(size)])


def chip_swap(x):
    size = lax.axis_size("mp")
    return lax.ppermute(x, "mp", [(i, i ^ 2) for i in range(size)])


def dot(a, b):
    return jnp.dot(a, b, preferred_element_type=f32)


def dot_rows(a, b):
    return lax.dot_general(a, b, (((0,), (0,)), ((), ())), preferred_element_type=f32)


def dot_cols(a, b):
    return lax.dot_general(a, b, (((1,), (1,)), ((), ())), preferred_element_type=f32)


def norm_parts(values):
    center = values - jnp.mean(values, axis=-1, keepdims=True)
    spread = jnp.mean(center * center, axis=-1, keepdims=True)
    rstd = lax.rsqrt(spread + norm_eps)
    return center * rstd, rstd


def layer_norm(values, gain_row, shift_row):
    unit, _ = norm_parts(values)
    return unit * gain_row + shift_row


def norm_back(grad, values, gain_row):
    unit, rstd = norm_parts(values)
    scaled = grad * gain_row
    gain_grad = jnp.sum(grad * unit, axis=0) * 0.5
    shift_grad = jnp.sum(grad, axis=0) * 0.5
    into = rstd * (
        scaled
        - jnp.mean(scaled, axis=-1, keepdims=True)
        - unit * jnp.mean(scaled * unit, axis=-1, keepdims=True)
    )
    return into, gain_grad, shift_grad


def gelu(v):
    return 0.5 * v * (1.0 + jnp.tanh(GELU_A * (v + GELU_B * v * v * v)))


def gelu_slope(v):
    t = jnp.tanh(GELU_A * (v + GELU_B * v * v * v))
    return 0.5 * (1.0 + t) + 0.5 * v * (1.0 - t * t) * (GELU_A * (1.0 + 3.0 * GELU_B * v * v))


def reduce_scatter_rows(grad, axis):
    index = lax.axis_index("dp")
    whole = lax.axis_size("dp")
    left, step = whole, 1
    while left > 1:
        shape = grad.shape
        split = grad.reshape(shape[:axis] + (left // 2, 2) + shape[axis + 1 :])
        bit = (index // step) % 2
        kept = lax.dynamic_index_in_dim(split, bit, axis + 1, keepdims=False)
        sent = lax.dynamic_index_in_dim(split, 1 - bit, axis + 1, keepdims=False)
        got = lax.ppermute(sent, "dp", [(i, i ^ step) for i in range(whole)])
        grad = kept.astype(f32) + got.astype(f32)
        left, step = left // 2, step * 2
        if left > 1:
            grad = grad.astype(bf16)
    return jnp.squeeze(grad, axis)


def sum_over(values, axis_name):
    size, step = lax.axis_size(axis_name), 1
    while step < size:
        perm = [(i, i ^ step) for i in range(size)]
        got = [lax.ppermute(v, axis_name, perm) for v in values]
        values = [a + b for a, b in zip(values, got)]
        step *= 2
    return values


def shards(
    tokens,
    seg_lengths,
    cotangent,
    mixer_norm_gain,
    mixer_norm_bias,
    in_weight,
    in_bias,
    conv_weight,
    conv_bias,
    filter_in,
    filter_in_bias,
    filter_in_freq,
    filter_mid,
    filter_mid_bias,
    filter_mid_freq,
    filter_out,
    skip_bias,
    out_weight,
    out_bias,
    feed_norm_gain,
    feed_norm_bias,
    feed_up,
    feed_up_bias,
    feed_down,
    feed_down_bias,
):
    block = tokens.shape[1]
    length = block * lax.axis_size("mp")
    channels = in_weight.shape[3]
    layers = in_weight.shape[0]
    spot = lax.axis_index("mp")
    core, chip = spot % 2, spot // 2
    chan_index = (spot * channels + jnp.arange(channels, dtype=jnp.int32)).astype(f32)
    pos_table = position_table(length, REACH)
    window = decay_window(length, REACH, chan_index)
    table = wave_table(length)
    waves = jnp.asarray(table)
    waves_t = jnp.asarray(np.ascontiguousarray(table.T))
    taps_waves = jnp.asarray(np.ascontiguousarray(table[:, :REACH]))
    taps_waves_t = jnp.asarray(np.ascontiguousarray(table[:, :REACH].T))

    first = seg_lengths[0, 0]
    places = jnp.arange(length, dtype=jnp.int32)
    in_first = (places < first)[:, None]
    seg_offset = jnp.where(places < first, places, places - first)
    lag_kept = [(seg_offset >= lag).astype(f32)[:, None, None] for lag in range(SHORT)]

    def own_rows(mine):
        other = chip_swap(mine)
        return jnp.concatenate(
            [jnp.where(chip == 0, mine, other), jnp.where(chip == 0, other, mine)], axis=0
        )

    def in_order(own, got):
        a = own.reshape(2, block, -1)
        b = got.reshape(2, block, -1)
        lo = jnp.where(core == 0, a, b)
        hi = jnp.where(core == 0, b, a)
        return jnp.stack([lo, hi], axis=1).reshape(4 * block, -1)

    def core_part(rows, which):
        split = rows.reshape(2, 2, block, -1)
        return lax.dynamic_index_in_dim(split, which, 1, keepdims=False).reshape(2 * block, -1)

    def reduce_pair(keep, got):
        here = keep + got.astype(f32)
        there = chip_swap(here.astype(bf16))
        return here + there.astype(f32)

    def split_spectrum(spec):
        return spec[:REACH], spec[REACH:]

    def pieces_of(values):
        return jnp.concatenate(
            [jnp.where(in_first, values, 0.0), jnp.where(in_first, 0.0, values)], axis=1
        ).astype(bf16)

    def merge(pieces):
        return jnp.where(in_first, pieces[:, :channels], pieces[:, channels:])

    def twice(spec):
        return jnp.concatenate([spec, spec], axis=1)

    filt = []
    for layer in range(layers):
        taps, pull = jax.vjp(
            lambda *args: make_taps(*args, pos_table) * window,
            filter_in[layer],
            filter_in_bias[layer],
            filter_in_freq[layer],
            filter_mid[layer],
            filter_mid_bias[layer],
            filter_mid_freq[layer],
            filter_out[layer],
        )
        spec = dot(taps_waves, taps.astype(bf16)) * (2.0 / WAVES)
        filt.append((spec, pull))

    def short(proj, layer):
        total = conv_bias[layer] + proj * conv_weight[layer][:, 0]
        for lag in range(1, SHORT):
            moved = jnp.pad(proj[:-lag], ((lag, 0), (0, 0), (0, 0)))
            total = total + moved * conv_weight[layer][:, lag] * lag_kept[lag]
        return total

    residual = own_rows(tokens[0]).astype(f32)
    stored = []
    for layer in range(layers):
        entry = residual
        normed_own = layer_norm(
            residual, mixer_norm_gain[layer], mixer_norm_bias[layer]
        ).astype(bf16)
        normed = in_order(normed_own, core_swap(normed_own))
        proj = (
            dot(normed, in_weight[layer].reshape(D, -1)).reshape(length, 3, channels)
            + in_bias[layer]
        )
        shorted = short(proj, layer)
        gated = shorted[:, 2] * shorted[:, 1]
        gate_spec = dot(waves, pieces_of(gated))
        taps_re, taps_im = split_spectrum(twice(filt[layer][0]))
        gate_re, gate_im = split_spectrum(gate_spec)
        prod = jnp.concatenate(
            [gate_re * taps_re - gate_im * taps_im, gate_re * taps_im + gate_im * taps_re], axis=0
        ).astype(bf16)
        longc = merge(dot(waves_t, prod)) + skip_bias[layer] * gated
        mixed = (longc * shorted[:, 0]).astype(bf16)
        sent = dot(core_part(mixed, 1 - core), out_weight[layer]).astype(bf16)
        got = core_swap(sent)
        keep = dot(core_part(mixed, core), out_weight[layer])
        middle = residual + reduce_pair(keep, got) + out_bias[layer]
        feed_own = layer_norm(middle, feed_norm_gain[layer], feed_norm_bias[layer]).astype(bf16)
        feed_got = core_swap(feed_own)
        pre_own = dot(feed_own, feed_up[layer]) + feed_up_bias[layer]
        hid_own = gelu(pre_own).astype(bf16)
        pre_got = dot(feed_got, feed_up[layer]) + feed_up_bias[layer]
        hid_got = gelu(pre_got).astype(bf16)
        got = core_swap(dot(hid_got, feed_down[layer]).astype(bf16))
        keep = dot(hid_own, feed_down[layer])
        branch = reduce_pair(keep, got)
        stored.append(
            (
                entry,
                normed,
                proj,
                gate_spec.astype(bf16),
                longc,
                mixed,
                middle,
                feed_own,
                feed_got,
                pre_own,
                pre_got,
                hid_own,
                hid_got,
            )
        )
        residual = middle + branch + feed_down_bias[layer]
    outputs = lax.dynamic_slice_in_dim(residual, chip * block, block, 0)

    gradient = own_rows(cotangent[0]).astype(f32)
    big = [None] * layers
    small = [None] * layers
    shared = [None] * layers
    chunks = lax.axis_size("dp")

    def by_rows(grad):
        return reduce_scatter_rows(
            grad.astype(bf16).reshape(chunks, grad.shape[0] // chunks, grad.shape[1]), 0
        )

    def by_cols(grad):
        return reduce_scatter_rows(
            grad.astype(bf16).reshape(grad.shape[0], chunks, grad.shape[1] // chunks), 1
        )

    for layer in reversed(range(layers)):
        (
            entry,
            normed,
            proj,
            gate_spec,
            longc,
            mixed,
            middle,
            feed_own,
            feed_got,
            pre_own,
            pre_got,
            hid_own,
            hid_got,
        ) = stored[layer]
        down_bias_grad = jnp.sum(gradient, axis=0) * 0.5
        low_own = gradient.astype(bf16)
        low_got = core_swap(low_own)
        pg_own = dot_cols(low_own, feed_down[layer]) * gelu_slope(pre_own)
        up_own = pg_own.astype(bf16)
        pg_got = dot_cols(low_got, feed_down[layer]) * gelu_slope(pre_got)
        up_got = pg_got.astype(bf16)
        got = core_swap(dot_cols(up_got, feed_up[layer]).astype(bf16))
        keep = dot_cols(up_own, feed_up[layer])
        feed_grad = reduce_pair(keep, got)
        up_bias_grad = jnp.sum(pg_own, axis=0) + jnp.sum(pg_got, axis=0)
        down_grad = dot_rows(
            jnp.concatenate([hid_own, hid_got], axis=0), jnp.concatenate([low_own, low_got], axis=0)
        )
        up_grad = dot_rows(
            jnp.concatenate([feed_own, feed_got], axis=0), jnp.concatenate([up_own, up_got], axis=0)
        )
        down_big = by_cols(down_grad)
        up_big = by_rows(up_grad)
        into, feed_gain_grad, feed_shift_grad = norm_back(
            feed_grad, middle, feed_norm_gain[layer]
        )
        gradient = gradient + into
        out_bias_grad = jnp.sum(gradient, axis=0) * 0.5
        out_own = gradient.astype(bf16)
        out_low = in_order(out_own, core_swap(out_own))
        mixed_grad = dot_cols(out_low, out_weight[layer])
        out_big = by_cols(dot_rows(mixed, out_low))

        shorted = short(proj, layer)
        gated = shorted[:, 2] * shorted[:, 1]
        long_grad = mixed_grad * shorted[:, 0]
        first_grad = mixed_grad * longc
        skip_grad = jnp.sum(long_grad * gated, axis=0)
        long_spec = dot(waves, pieces_of(long_grad))
        taps_re, taps_im = split_spectrum(twice(filt[layer][0]))
        long_re, long_im = split_spectrum(long_spec)
        gate_re, gate_im = split_spectrum(gate_spec.astype(f32))
        prod = jnp.concatenate(
            [long_re * taps_re + long_im * taps_im, long_im * taps_re - long_re * taps_im], axis=0
        ).astype(bf16)
        gated_grad = merge(dot(waves_t, prod)) + skip_bias[layer] * long_grad
        corr_re = gate_re * long_re + gate_im * long_im
        corr_im = gate_re * long_im - gate_im * long_re
        corr = jnp.concatenate([corr_re, corr_im], axis=0)
        corr = (corr[:, :channels] + corr[:, channels:]).astype(bf16)
        taps_grad = dot(taps_waves_t, corr) * (2.0 / WAVES)
        filter_grads = filt[layer][1](taps_grad)
        short_grad = jnp.stack(
            [first_grad, gated_grad * shorted[:, 2], gated_grad * shorted[:, 1]], axis=1
        )
        conv_bias_grad = jnp.sum(short_grad, axis=0)
        proj_grad = short_grad * conv_weight[layer][:, 0]
        conv_grads = [jnp.sum(short_grad * proj, axis=0)]
        for lag in range(1, SHORT):
            kept = short_grad * lag_kept[lag]
            moved = jnp.pad(kept[lag:], ((0, lag), (0, 0), (0, 0)))
            proj_grad = proj_grad + moved * conv_weight[layer][:, lag]
            conv_grads.append(jnp.sum(moved * proj, axis=0))
        conv_weight_grad = jnp.stack(conv_grads, axis=1)
        in_bias_grad = jnp.sum(proj_grad, axis=0)
        in_low = proj_grad.astype(bf16).reshape(length, -1)
        flat_in = in_weight[layer].reshape(D, -1)
        in_big = by_rows(dot_rows(normed, in_low))
        got = core_swap(dot_cols(core_part(in_low, 1 - core), flat_in).astype(bf16))
        keep = dot_cols(core_part(in_low, core), flat_in)
        into, mixer_gain_grad, mixer_shift_grad = norm_back(
            reduce_pair(keep, got), entry, mixer_norm_gain[layer]
        )
        gradient = gradient + into

        big[layer] = (in_big.reshape(-1, 3, channels), out_big, up_big, down_big)
        small[layer] = jnp.concatenate(
            [
                in_bias_grad,
                conv_weight_grad.reshape(-1, channels),
                conv_bias_grad,
                filter_grads[6],
                skip_grad[None],
                up_bias_grad.reshape(-1, channels),
            ],
            axis=0,
        )
        shared[layer] = (
            jnp.stack(
                [
                    mixer_gain_grad,
                    mixer_shift_grad,
                    out_bias_grad,
                    feed_gain_grad,
                    feed_shift_grad,
                    down_bias_grad,
                ]
            ),
            jnp.concatenate(
                [
                    filter_grads[0],
                    filter_grads[1][None],
                    filter_grads[2][None],
                    filter_grads[3],
                    filter_grads[4][None],
                    filter_grads[5][None],
                ],
                axis=0,
            ),
        )
    token_grad = lax.dynamic_slice_in_dim(gradient, chip * block, block, 0)

    sums = []
    for layer in range(layers):
        by_chan, wide, narrow = sum_over([small[layer], *shared[layer]], "dp")
        wide, narrow = sum_over([wide, narrow], "mp")
        sums.append((by_chan, wide, narrow))

    def both(pick):
        return jnp.stack([pick(layer) for layer in range(layers)])

    def chan(lo, hi):
        return both(lambda layer: sums[layer][0][lo:hi])

    def wide(row):
        return both(lambda layer: sums[layer][1][row])

    def narrow(lo, hi):
        return both(lambda layer: sums[layer][2][lo:hi])

    filt_width = filter_mid.shape[1]
    at = np.cumsum([0, 3, 3 * SHORT, 3, filt_width, 1, feed_up.shape[2] // channels])
    return (
        outputs[None],
        token_grad[None],
        wide(0),
        wide(1),
        both(lambda layer: big[layer][0]),
        chan(at[0], at[1]),
        chan(at[1], at[2]).reshape(layers, 3, SHORT, channels),
        chan(at[2], at[3]),
        narrow(0, POS),
        narrow(POS, POS + 1)[:, 0],
        narrow(POS + 1, POS + 2)[:, 0],
        narrow(POS + 2, POS + 2 + filt_width),
        narrow(POS + 2 + filt_width, POS + 3 + filt_width)[:, 0],
        narrow(POS + 3 + filt_width, POS + 4 + filt_width)[:, 0],
        chan(at[3], at[4]),
        chan(at[4], at[5])[:, 0],
        both(lambda layer: big[layer][1]),
        wide(2),
        wide(3),
        wide(4),
        both(lambda layer: big[layer][2]),
        chan(at[5], at[6]).reshape(layers, -1),
        both(lambda layer: big[layer][3]),
        wide(5),
    )


def solution(mesh):
    in_specs = (
        P("dp", "mp", None),
        P("dp", None),
        P("dp", "mp", None),
        P(),
        P(),
        P(None, None, None, "mp"),
        P(None, None, "mp"),
        P(None, None, None, "mp"),
        P(None, None, "mp"),
        P(),
        P(),
        P(),
        P(),
        P(),
        P(),
        P(None, None, "mp"),
        P(None, "mp"),
        P(None, "mp", None),
        P(),
        P(),
        P(),
        P(None, None, "mp"),
        P(None, "mp"),
        P(None, "mp", None),
        P(),
    )
    out_specs = (
        P("dp", "mp", None),
        P("dp", "mp", None),
        P(),
        P(),
        P(None, "dp", None, "mp"),
        P(None, None, "mp"),
        P(None, None, None, "mp"),
        P(None, None, "mp"),
        P(),
        P(),
        P(),
        P(),
        P(),
        P(),
        P(None, None, "mp"),
        P(None, "mp"),
        P(None, "mp", "dp"),
        P(),
        P(),
        P(),
        P(None, "dp", "mp"),
        P(None, "mp"),
        P(None, "mp", "dp"),
        P(),
    )
    return jax.shard_map(shards, mesh=mesh, in_specs=in_specs, out_specs=out_specs, check_vma=False)
```

```python
import functools
import math

import jax
import jax.numpy as jnp
import ml_dtypes
import numpy as np
from jax import lax
from jax.experimental import pallas as pl
from jax.experimental.pallas import tpu as pltpu
from jax.sharding import PartitionSpec as P

D = 1024
POS = 33
FILT = 64
REACH = 896
WAVES = 2 * REACH
SHORT = 3
STREAMS = 3
TILE = 128
CHUNK = 128
PARTS = D // CHUNK

f32 = jnp.float32
bf16 = jnp.bfloat16
highest = lax.Precision.HIGHEST
norm_eps = 1e-05
slow_rate = math.log(100.0) / 1.5
fast_rate = math.log(100.0) / 0.3
GELU_A = math.sqrt(2.0 / math.pi)
GELU_B = 0.044715
SPARE_MB = 3

ROW_IN_BIAS = 0
ROW_CONV_W = 3
ROW_CONV_B = 12
ROW_SKIP = 15
ROW_FILTER = 16
ROW_UP_BIAS = 80
ROW_WIDE = 84
ROW_NARROW = 116
PACK_ROWS = 144
NARROW_ROWS = 112
NARROW_GROUP = 28
NB_IN, NF_IN, NW_MID, NB_MID, NF_MID = 33, 34, 35, 99, 100


def wave_table(length):
    freq = 2 * np.arange(REACH, dtype=np.int64) + 1
    phase = (freq[:, None] * np.arange(length, dtype=np.int64)[None, :]) % (2 * WAVES)
    angle = phase.astype(np.float64) * (math.pi / WAVES)
    return np.concatenate([np.cos(angle), -np.sin(angle)], axis=0).astype(ml_dtypes.bfloat16)


def position_table(length):
    places = np.arange(REACH, dtype=np.float64)
    count = (POS - 1) // 2
    bands = 0.0001 + np.arange(count, dtype=np.float64) * ((count - 1 - 0.0001) / (count - 1))
    phases = bands[:, None] * places[None, :] * (2.0 * math.pi / length)
    table = np.zeros((64, REACH), np.float32)
    table[0] = places / (length - 1)
    table[1 : 1 + count] = np.cos(phases)
    table[1 + count : POS] = -np.sin(phases)
    return table


def core_swap(x):
    size = lax.axis_size("mp")
    return lax.ppermute(x, "mp", [(i, i ^ 1) for i in range(size)])


def chip_swap(x):
    size = lax.axis_size("mp")
    return lax.ppermute(x, "mp", [(i, i ^ 2) for i in range(size)])


def dot(a, b):
    return jnp.dot(a, b, preferred_element_type=f32)


def dot_rows(a, b):
    return lax.dot_general(a, b, (((0,), (0,)), ((), ())), preferred_element_type=f32)


def dot_cols(a, b):
    return lax.dot_general(a, b, (((1,), (1,)), ((), ())), preferred_element_type=f32)


def fine(a, b, dims):
    return lax.dot_general(a, b, (dims, ((), ())), precision=highest, preferred_element_type=f32)


def whole(shape):
    return pl.BlockSpec(tuple(shape), lambda *_: (0,) * len(shape))


def layer_of(stacked, layer):
    shape = stacked.shape[1:]
    return pl.BlockSpec((None, *shape), lambda *_: (layer,) + (0,) * len(shape))


SMALL = pl.BlockSpec(memory_space=pltpu.SMEM)
FAR = pl.BlockSpec(memory_space=pl.ANY)
MAIN = pl.BlockSpec(memory_space=pltpu.HBM)


def struct(shape, dtype):
    return jax.ShapeDtypeStruct(tuple(shape), dtype)


class Chain:
    def __init__(self):
        self.token = None

    def __call__(self, kernel, operands, outs, scratch=(), far=0, spill=0, name=None, after=()):
        arrays = [a for a, _ in operands]
        specs = [whole(a.shape) if s is None else s for a, s in operands]
        main = far + spill
        out_specs = [MAIN if i < main else whole(o.shape) for i, o in enumerate(outs)]
        spilled = [pltpu.VMEM(o.shape, o.dtype) for o in outs[far:main]]
        scratch = [*scratch, *spilled] + ([pltpu.SemaphoreType.DMA((spill,))] if spill else [])
        held = 0
        for a, s in list(zip(arrays, specs)) + list(zip(outs, out_specs)):
            if s is not SMALL and s is not FAR and s is not MAIN:
                held += math.prod(x for x in s.block_shape if x is not None) * a.dtype.itemsize
        for s in scratch:
            if getattr(s, "memory_space", None) == pltpu.VMEM:
                held += math.prod(s.shape) * jnp.dtype(s.dtype).itemsize
        count, given = len(arrays), len(outs)
        tokens = ([] if self.token is None else [self.token]) + list(after)

        def body(*refs):
            ins, refs = refs[:count], refs[count + len(tokens) :]
            results, rest = refs[:given], refs[given + 1 :]
            if spill:
                rest, buffers, sems = rest[: -spill - 1], rest[-spill - 1 : -1], rest[-1]
                kernel(*ins, *results[:far], *buffers, *results[main:], *rest)
                copies = [
                    pltpu.make_async_copy(buffers[i], results[far + i], sems.at[i]) for i in range(spill)
                ]
                for copy in copies:
                    copy.start()
                for copy in copies:
                    copy.wait()
            else:
                kernel(*ins, *results, *rest)

        *results, self.token = pl.pallas_call(
            body,
            grid=(1,),
            out_shape=[pltpu.HBM(o.shape, o.dtype) if i < main else o for i, o in enumerate(outs)]
            + [struct((8, 128), f32)],
            in_specs=specs + [FAR] * len(tokens),
            out_specs=out_specs + [FAR],
            scratch_shapes=scratch,
            compiler_params=pltpu.CompilerParams(vmem_limit_bytes=held + SPARE_MB * 1024 * 1024),
            cost_estimate=pl.CostEstimate(flops=1, bytes_accessed=1, transcendentals=0),
            name=name,
        )(*arrays, *tokens)
        return results


def unit_of(values):
    center = values - jnp.mean(values, axis=-1, keepdims=True)
    spread = jnp.mean(center * center, axis=-1, keepdims=True)
    rstd = lax.rsqrt(spread + norm_eps)
    return center * rstd, rstd


def row_tiles(count, size=32):
    return [slice(i * size, (i + 1) * size) for i in range(count // size)]


def stay(x):
    return pltpu.with_memory_space_constraint(x, pltpu.HBM)


def first_norm_kernel(scal, mine, other, gain, shift, cot, low_a, low_b, res_a, res_b, cot_out):
    chip = scal[2]
    cot_out[...] = cot[...]
    for rows in row_tiles(mine.shape[0]):
        a, b = mine[rows, :].astype(f32), other[rows, :].astype(f32)
        for values, res, low in (
            (jnp.where(chip == 0, a, b), res_a, low_a),
            (jnp.where(chip == 0, b, a), res_b, low_b),
        ):
            res[rows, :] = values
            unit, _ = unit_of(values)
            low[rows, :] = (unit * gain[0:1, :] + shift[0:1, :]).astype(bf16)


def first_norm(run, scal, mine, other, gain, shift, cot):
    block = mine.shape[0]
    return run(
        first_norm_kernel,
        [(scal, SMALL)] + [(a, None) for a in (mine, other, gain, shift, cot)],
        [struct((block, D), bf16)] * 2 + [struct((block, D), f32)] * 2 + [struct((block, D), bf16)],
        spill=2,
        name="first_norm",
    )


def first_grad_kernel(scal, mine, other, low_a, low_b, sums):
    chip = scal[2]
    total = jnp.zeros((8, D), f32)
    for rows in row_tiles(mine.shape[0]):
        a, b = mine[rows, :], other[rows, :]
        low_a[rows, :] = jnp.where(chip == 0, a, b)
        low_b[rows, :] = jnp.where(chip == 0, b, a)
        total = total + fold(a.astype(f32)) + fold(b.astype(f32))
    sums[...] = 0.5 * jnp.sum(total, axis=0, keepdims=True)


def first_grad(run, scal, mine, other):
    block = mine.shape[0]
    return run(
        first_grad_kernel,
        [(scal, SMALL), (mine, None), (other, None)],
        [struct((block, D), bf16)] * 2 + [struct((1, D), f32)],
        name="first_grad",
    )


def add_kernel(keep, got, out):
    for rows in row_tiles(keep.shape[0], 64):
        out[rows, :] = (keep[rows, :] + got[rows, :].astype(f32)).astype(out.dtype)


def add_low(run, keep, got, after=()):
    out = [struct(keep.shape, bf16)]
    return run(add_kernel, [(keep, None), (got, None)], out, name="add_low", after=after)[0]


def last_pick_kernel(scal, keep_a, got_a, val_a, keep_b, got_b, val_b, send, mine, sums):
    totals = [jnp.zeros((8, D), f32) for _ in range(2)]
    near_a = scal[2] == 0
    for rows in row_tiles(mine.shape[0]):
        parts = []
        for keep, got, values in ((keep_a, got_a, val_a), (keep_b, got_b, val_b)):
            total = keep[rows, :] + got[rows, :].astype(f32)
            unit, _ = unit_of(values[rows, :])
            totals[0] = totals[0] + fold(total * unit)
            totals[1] = totals[1] + fold(total)
            parts.append(total)
        mine[rows, :] = jnp.where(near_a, parts[0], parts[1])
        send[rows, :] = jnp.where(near_a, parts[1], parts[0]).astype(bf16)
    for i, total in enumerate(totals):
        sums[i : i + 1, :] = jnp.sum(total, axis=0, keepdims=True)
    sums[2:8, :] = jnp.zeros((6, D), f32)


def last_pick(run, scal, keeps, gots, entry):
    shape = keeps[0].shape
    operands = [a for i in range(2) for a in (keeps[i], gots[i], entry[i])]
    return run(
        last_pick_kernel,
        [(scal, SMALL)] + [(a, None) for a in operands],
        [struct(shape, bf16), struct(shape, f32), struct((8, D), f32)],
        name="last_pick",
    )


def add_norm_kernel(layer, norm_layer, here, there, residual, bias, gain, shift, low, out):
    for rows in row_tiles(here.shape[0]):
        values = residual[rows, :] + here[rows, :].astype(f32) + there[rows, :].astype(f32)
        values = values + bias[layer : layer + 1, :]
        out[rows, :] = values
        unit, _ = unit_of(values)
        low[rows, :] = (
            unit * gain[norm_layer : norm_layer + 1, :] + shift[norm_layer : norm_layer + 1, :]
        ).astype(bf16)


def add_norm(run, layer, norm_layer, here, there, residual, bias, gain, shift, spill=0):
    shape = here.shape
    return run(
        functools.partial(add_norm_kernel, layer, norm_layer),
        [(a, None) for a in (here, there, residual, bias, gain, shift)],
        [struct(shape, bf16), struct(shape, f32)],
        spill=spill,
        name="add_norm",
    )


def pick_kernel(layer, scal, keep_a, got_a, keep_b, got_b, mid_a, mid_b, bias, send, mine):
    def pick(near, far_away):
        keep, got, middle = near
        for rows in row_tiles(mine.shape[0]):
            values = keep[rows, :] + got[rows, :].astype(f32) + middle[rows, :]
            mine[rows, :] = values + bias[layer : layer + 1, :]
            send[rows, :] = (far_away[0][rows, :] + far_away[1][rows, :].astype(f32)).astype(bf16)

    @pl.when(scal[2] == 0)
    def _():
        pick((keep_a, got_a, mid_a), (keep_b, got_b))

    @pl.when(scal[2] != 0)
    def _():
        pick((keep_b, got_b, mid_b), (keep_a, got_a))


def pick_outputs(run, layer, scal, keeps, gots, middles, bias):
    shape = keeps[0].shape
    operands = (keeps[0], gots[0], keeps[1], gots[1], *middles, bias)
    return run(
        functools.partial(pick_kernel, layer),
        [(scal, SMALL)] + [(a, None) for a in operands],
        [struct(shape, bf16), struct(shape, f32)],
        name="pick_outputs",
    )


def last_add_kernel(mine, there, out):
    for rows in row_tiles(out.shape[0], 64):
        out[rows, :] = mine[rows, :] + there[rows, :].astype(f32)


def last_add(run, mine, there):
    return run(last_add_kernel, [(mine, None), (there, None)], [struct(mine.shape, f32)], name="last_add")[0]


def fold(x):
    return sum(x[8 * i : 8 * i + 8, :] for i in range(x.shape[0] // 8))


def norm_back_kernel(layer, here, there, values, grad, gain, low, out, sums):
    totals = [jnp.zeros((8, D), f32) for _ in range(3)]
    for rows in row_tiles(here.shape[0], 16):
        dy = here[rows, :].astype(f32) + there[rows, :].astype(f32)
        unit, rstd = unit_of(values[rows, :])
        scaled = dy * gain[layer : layer + 1, :]
        into = rstd * (
            scaled
            - jnp.mean(scaled, axis=-1, keepdims=True)
            - unit * jnp.mean(scaled * unit, axis=-1, keepdims=True)
        )
        new = grad[rows, :].astype(f32) + into
        out[rows, :] = new
        low[rows, :] = new.astype(bf16)
        for k, part in enumerate((dy * unit, dy, new)):
            totals[k] = totals[k] + fold(part)
    for k, total in enumerate(totals):
        sums[k : k + 1, :] = 0.5 * jnp.sum(total, axis=0, keepdims=True)
    sums[3:8, :] = jnp.zeros((5, D), f32)


def norm_back(run, layer, here, there, values, grad, gain, spill=0):
    shape = here.shape
    return run(
        functools.partial(norm_back_kernel, layer),
        [(a, None) for a in (here, there, values, grad, gain)],
        [struct(shape, bf16), struct(shape, f32), struct((8, D), f32)],
        spill=spill,
        name="norm_back",
    )


def last_back_kernel(layer, scal, mine, there, val_a, val_b, grad_a, grad_b, gain, out):
    near_a = scal[2] == 0
    for rows in row_tiles(out.shape[0], 16):
        dy = mine[rows, :] + there[rows, :].astype(f32)
        unit, rstd = unit_of(jnp.where(near_a, val_a[rows, :], val_b[rows, :]))
        scaled = dy * gain[layer : layer + 1, :]
        into = rstd * (
            scaled
            - jnp.mean(scaled, axis=-1, keepdims=True)
            - unit * jnp.mean(scaled * unit, axis=-1, keepdims=True)
        )
        out[rows, :] = jnp.where(near_a, grad_a[rows, :], grad_b[rows, :]) + into


def last_back(run, layer, scal, mine, there, entry, grad, gain):
    return run(
        functools.partial(last_back_kernel, layer),
        [(scal, SMALL)] + [(a, None) for a in (mine, there, *entry, *grad, gain)],
        [struct(mine.shape, f32)],
        name="last_back",
    )[0]


def ffn_fwd_kernel(
    layer, own, got, up_far, up_bias, down_far, pre_far, hid_far, sent, keep, both, pre, hid, up, down, sems
):
    copy_up = pltpu.make_async_copy(up_far.at[layer], up, sems.at[2])
    copy_down = pltpu.make_async_copy(down_far.at[layer], down, sems.at[3])
    copy_up.start()
    copy_down.start()
    half = own.shape[0]
    both[:half, :] = own[...]
    both[half:, :] = got[...]
    copy_up.wait()
    v = dot(both[...], up[...]) + up_bias[layer : layer + 1, :]
    pre[...] = v.astype(bf16)
    hid[...] = (0.5 * v * (1.0 + jnp.tanh(GELU_A * (v + GELU_B * v * v * v)))).astype(bf16)
    copies = [
        pltpu.make_async_copy(a, b, sems.at[i]) for i, (a, b) in enumerate(((pre, pre_far), (hid, hid_far)))
    ]
    for copy in copies:
        copy.start()
    copy_down.wait()
    total = dot(hid[...], down[...])
    keep[...] = total[:half, :]
    sent[...] = total[half:, :].astype(bf16)
    for copy in copies:
        copy.wait()


def ffn_fwd(run, layer, own, got, up, up_bias, down):
    half, width = own.shape[0], up.shape[2]
    return run(
        functools.partial(ffn_fwd_kernel, layer),
        [(own, None), (got, None), (up, FAR), (up_bias, None), (down, FAR)],
        [
            struct((2 * half, width), bf16),
            struct((2 * half, width), bf16),
            struct((half, D), bf16),
            struct((half, D), f32),
        ],
        scratch=[
            pltpu.VMEM((2 * half, D), bf16),
            pltpu.VMEM((2 * half, width), bf16),
            pltpu.VMEM((2 * half, width), bf16),
            pltpu.VMEM((D, width), bf16),
            pltpu.VMEM((width, D), bf16),
            pltpu.SemaphoreType.DMA((4,)),
        ],
        far=2,
        name="ffn_fwd",
    )


def ffn_bwd_kernel(
    layer, own, got, up_far, down_far, pre_far, up_low, bias_sum, sent, keep, both, up, down, pre, sems
):
    ins = ((down_far.at[layer], down), (pre_far, pre), (up_far.at[layer], up))
    copies = [pltpu.make_async_copy(a, b, sems.at[i]) for i, (a, b) in enumerate(ins)]
    for copy in copies:
        copy.start()
    half = own.shape[0]
    both[:half, :] = own[...]
    both[half:, :] = got[...]
    copies[0].wait()
    copies[1].wait()
    v = pre[...].astype(f32)
    t = jnp.tanh(GELU_A * (v + GELU_B * v * v * v))
    slope = 0.5 * (1.0 + t) + 0.5 * v * (1.0 - t * t) * (GELU_A * (1.0 + 3.0 * GELU_B * v * v))
    g = dot_cols(both[...], down[...]) * slope
    bias_sum[...] = jnp.sum(g, axis=0, keepdims=True)
    up_low[...] = g.astype(bf16)
    copies[2].wait()
    total = dot_cols(up_low[...], up[...])
    keep[...] = total[:half, :]
    sent[...] = total[half:, :].astype(bf16)


def ffn_bwd(run, layer, own, got, up, down, pre):
    half, width = own.shape[0], up.shape[2]
    return run(
        functools.partial(ffn_bwd_kernel, layer),
        [(own, None), (got, None), (up, FAR), (down, FAR), (pre, FAR)],
        [
            struct((2 * half, width), bf16),
            struct((1, width), f32),
            struct((half, D), bf16),
            struct((half, D), f32),
        ],
        scratch=[
            pltpu.VMEM((2 * half, D), bf16),
            pltpu.VMEM((D, width), bf16),
            pltpu.VMEM((width, D), bf16),
            pltpu.VMEM((2 * half, width), bf16),
            pltpu.SemaphoreType.DMA((3,)),
        ],
        name="ffn_bwd",
    )


def sine(x, both=False):
    turns = jnp.floor(x * (1.0 / math.pi) + 0.5)
    rest = (x - turns * 3.140625) - turns * 9.67653589793e-4
    sign = 1.0 - 2.0 * (turns - 2.0 * jnp.floor(turns * 0.5))
    sq = rest * rest
    odd = -1.0 / 39916800.0
    for c in (1.0 / 362880.0, -1.0 / 5040.0, 1.0 / 120.0, -1.0 / 6.0, 1.0):
        odd = odd * sq + c
    value = sign * rest * odd
    if not both:
        return value
    even = 1.0 / 479001600.0
    for c in (-1.0 / 3628800.0, 1.0 / 40320.0, -1.0 / 720.0, 1.0 / 24.0, -0.5, 1.0):
        even = even * sq + c
    return value, sign * even


def decay(spot, channels, length):
    lane = lax.broadcasted_iota(jnp.int32, (1, channels), 1) + spot * channels
    row = lax.broadcasted_iota(jnp.int32, (REACH, channels), 0).astype(f32)
    rate = slow_rate + (fast_rate - slow_rate) * lane.astype(f32) / (D - 1)
    return jnp.exp(-(row * (1.0 / (length - 1))) * rate)


def columns(layer, *refs):
    rows = [r[layer : layer + 1, :] for r in refs] + [jnp.zeros((8 - len(refs), FILT), f32)]
    wide = jnp.concatenate([jnp.concatenate(rows, axis=0), jnp.zeros((8, 128 - FILT), f32)], axis=1).T
    return [wide[:FILT, i : i + 1] for i in range(len(refs))]


def filter_fwd_kernel(
    layer, length, scal, pos, w_in, b_in, f_in, w_mid, b_mid, f_mid, w_out, waves, spec, kept
):
    channels = w_out.shape[1]
    b_in, f_in, b_mid, f_mid = columns(layer, b_in, f_in, b_mid, f_mid)
    z = fine(w_in[...], pos[:POS, :], ((0,), (0,))) + b_in
    h, c = sine(f_in * z, both=True)
    kept[0] = z
    kept[1] = h
    kept[2] = c
    z = fine(w_mid[...], h, ((0,), (0,))) + b_mid
    h, c = sine(f_mid * z, both=True)
    kept[3] = z
    kept[4] = h
    kept[5] = c
    taps = fine(h, w_out[...], ((0,), (0,))) * decay(scal[4], channels, length)
    spec[...] = dot(waves[:, :REACH], taps.astype(bf16)) * (2.0 / WAVES)


def filter_fwd(run, layer, length, scal, pos, weights, waves):
    channels = weights[-1].shape[2]
    return run(
        functools.partial(filter_fwd_kernel, layer, length),
        [(scal, SMALL), (pos, None)]
        + [(a, layer_of(a, layer) if a.ndim == 3 else None) for a in weights]
        + [(waves, None)],
        [struct((WAVES, channels), f32), struct((6, FILT, REACH), f32)],
        spill=2,
        name="filter_fwd",
    )


def filter_bwd_kernel(layer, length, scal, taps_grad, pos, f_in, w_mid, f_mid, w_out, kept, by_chan, narrow):
    channels = w_out.shape[1]
    dt = taps_grad[...] * decay(scal[4], channels, length)
    by_chan[...] = fine(kept[4], dt, ((1,), (0,)))
    f_in, f_mid = columns(layer, f_in, f_mid)
    dh = fine(w_out[...], dt, ((1,), (1,)))
    c = kept[5] * dh
    dz = c * f_mid
    narrow[NW_MID : NW_MID + FILT, :] = fine(kept[1], dz, ((1,), (1,)))
    mid_sums = jnp.concatenate(
        [jnp.sum(dz, axis=1, keepdims=True), jnp.sum(c * kept[3], axis=1, keepdims=True)], axis=1
    )
    dh = fine(w_mid[...], dz, ((1,), (0,)))
    c = kept[2] * dh
    dz = c * f_in
    narrow[:POS, :] = fine(pos[...], dz, ((1,), (1,)))[:POS, :]
    in_sums = jnp.concatenate(
        [jnp.sum(dz, axis=1, keepdims=True), jnp.sum(c * kept[0], axis=1, keepdims=True)], axis=1
    )
    sums = jnp.concatenate([in_sums, mid_sums, jnp.zeros((FILT, 124), f32)], axis=1).T
    narrow[NB_IN : NB_IN + 2, :] = sums[0:2, :]
    narrow[NB_MID : NB_MID + 2, :] = sums[2:4, :]
    narrow[NF_MID + 1 :, :] = jnp.zeros((NARROW_ROWS - NF_MID - 1, FILT), f32)


def filter_bwd(run, layer, length, scal, taps_grad, pos, weights, kept):
    _, _, f_in, w_mid, _, f_mid, w_out = weights
    return run(
        functools.partial(filter_bwd_kernel, layer, length),
        [(scal, SMALL), (taps_grad, None), (pos, None)]
        + [(a, layer_of(a, layer) if a.ndim == 3 else None) for a in (f_in, w_mid, f_mid, w_out)]
        + [(kept, None)],
        [struct((FILT, w_out.shape[2]), f32), struct((NARROW_ROWS, FILT), f32)],
        name="filter_bwd",
    )


def lagged(ref, tile, cols, lag):
    if tile:
        return ref[tile * TILE - lag : (tile + 1) * TILE - lag, cols]
    empty = jnp.zeros((lag, cols.stop - cols.start), f32)
    return jnp.concatenate([empty, ref[: TILE - lag, cols]], axis=0)


def ahead(ref, tile, cols, lag, last):
    if tile < last:
        return ref[tile * TILE + lag : (tile + 1) * TILE + lag, cols]
    empty = jnp.zeros((lag, cols.stop - cols.start), f32)
    return jnp.concatenate([ref[tile * TILE + lag : (tile + 1) * TILE, cols], empty], axis=0)


def place(tile, first, shift=0):
    row = lax.broadcasted_iota(jnp.int32, (TILE, 1), 0) + (tile * TILE + shift)
    in_first = row < first
    return in_first, jnp.where(in_first, row, row - first)


def short_tile(proj, conv_w, conv_b, layer, tile, stream, offset, channels):
    cols = slice(stream * channels, (stream + 1) * channels)
    row = slice(layer, layer + 1)
    total = proj[tile * TILE : (tile + 1) * TILE, cols] * conv_w[stream, 0, row, :]
    total = total + conv_b[stream, row, :]
    for lag in range(1, SHORT):
        weight = conv_w[stream, lag, row, :]
        total = total + jnp.where(offset >= lag, lagged(proj, tile, cols, lag) * weight, 0.0)
    return total


def tile_rows(tile):
    return slice(tile * TILE, (tile + 1) * TILE)


def halves(own_a, own_b, got_a, got_b, core):
    block = own_a.shape[0]
    out = []
    for half, (own, got) in enumerate(((own_a, got_a), (own_b, got_b))):
        for rows, side in ((own, core), (got, 1 - core)):
            out.append((rows, pl.multiple_of(2 * block * half + side * block, block)))
    return out


def mix_fwd_kernel(
    layer, scal, own_a, own_b, got_a, got_b, in_w, in_b, conv_w, conv_b, skip, taps_far, out_w_far, waves_far, waves_t_far,
    proj_far, spec_far, longc_far, mixed_far, sent_a, sent_b, keep_a, keep_b,
    waves, waves_t, taps, out_w, proj, spec, gated, mixed, s0, pieces, prod, sems,
):
    ins = ((waves_far, waves), (taps_far, taps), (waves_t_far, waves_t), (out_w_far.at[layer], out_w))
    copy_f, copy_taps, copy_t, copy_out = [
        pltpu.make_async_copy(a, b, sems.at[i]) for i, (a, b) in enumerate(ins)
    ]
    outs = ((proj, proj_far), (spec, spec_far), (gated, longc_far), (mixed, mixed_far))
    copy_proj, copy_spec, copy_long, copy_mixed = [
        pltpu.make_async_copy(a, b, sems.at[4 + i]) for i, (a, b) in enumerate(outs)
    ]
    for copy in (copy_f, copy_taps, copy_t, copy_out):
        copy.start()
    first, core = scal[0], scal[1]
    block = own_a.shape[0]
    channels = skip.shape[1]
    row = slice(layer, layer + 1)
    length = 4 * block
    for rows, at in halves(own_a, own_b, got_a, got_b, core):
        for stream in range(STREAMS):
            cols = slice(stream * channels, (stream + 1) * channels)
            proj[pl.ds(at, block), cols] = dot(rows[...], in_w[stream]) + in_b[stream, row, :]
    copy_proj.start()
    for tile in range(length // TILE):
        rows = tile_rows(tile)
        in_first, offset = place(tile, first)
        g = short_tile(proj, conv_w, conv_b, layer, tile, 1, offset, channels) * short_tile(
            proj, conv_w, conv_b, layer, tile, 2, offset, channels
        )
        gated[rows, :] = g
        s0[rows, :] = short_tile(proj, conv_w, conv_b, layer, tile, 0, offset, channels)
        pieces[rows, :channels] = jnp.where(in_first, g, 0.0).astype(bf16)
        pieces[rows, channels:] = jnp.where(in_first, 0.0, g).astype(bf16)
    copy_f.wait()
    copy_taps.wait()
    steps = 2
    part = REACH // steps
    for step in range(steps):
        lo = slice(step * part, (step + 1) * part)
        hi = slice(REACH + step * part, REACH + (step + 1) * part)
        for seg in range(2):
            cols = slice(seg * channels, (seg + 1) * channels)
            re = dot(waves[lo, :], pieces[:, cols])
            im = dot(waves[hi, :], pieces[:, cols])
            t_re, t_im = taps[lo, :], taps[hi, :]
            spec[lo, cols] = re.astype(bf16)
            spec[hi, cols] = im.astype(bf16)
            prod[lo, cols] = (re * t_re - im * t_im).astype(bf16)
            prod[hi, cols] = (re * t_im + im * t_re).astype(bf16)
    copy_spec.start()
    copy_t.wait()
    big = 512
    for r in range(length // big):
        rows = slice(r * big, (r + 1) * big)
        in_first = lax.broadcasted_iota(jnp.int32, (big, 1), 0) + r * big < first
        a = dot(waves_t[rows, :], prod[:, :channels])
        b = dot(waves_t[rows, :], prod[:, channels:])
        total = jnp.where(in_first, a, b) + skip[row, :] * gated[rows, :]
        gated[rows, :] = total
        mixed[rows, :] = (total * s0[rows, :]).astype(bf16)
    copy_long.start()
    copy_mixed.start()
    copy_out.wait()
    for half, (sent, keep) in enumerate(((sent_a, keep_a), (sent_b, keep_b))):
        at = pl.multiple_of(2 * block * half + (1 - core) * block, block)
        sent[...] = dot(mixed[pl.ds(at, block), :], out_w[...]).astype(bf16)
        at = pl.multiple_of(2 * block * half + core * block, block)
        keep[...] = dot(mixed[pl.ds(at, block), :], out_w[...])
    copy_proj.wait()
    copy_spec.wait()
    copy_long.wait()
    copy_mixed.wait()


def mix_fwd(run, layer, scal, rows, in_w, in_b, conv_w, conv_b, skip, taps, out_w, waves, waves_t):
    block, channels = rows[0].shape[0], skip.shape[1]
    length = 4 * block
    return run(
        functools.partial(mix_fwd_kernel, layer),
        [(scal, SMALL)]
        + [(stay(a), None) for a in rows]
        + [(stay(in_w), layer_of(in_w, layer))]
        + [(a, None) for a in (in_b, conv_w, conv_b, skip)]
        + [(stay(a), FAR) for a in (taps, out_w, waves, waves_t)],
        [
            struct((length, STREAMS * channels), f32),
            struct((WAVES, 2 * channels), bf16),
            struct((length, channels), f32),
            struct((length, channels), bf16),
            struct((block, D), bf16),
            struct((block, D), bf16),
            struct((block, D), f32),
            struct((block, D), f32),
        ],
        scratch=[
            pltpu.VMEM((WAVES, length), bf16),
            pltpu.VMEM((length, WAVES), bf16),
            pltpu.VMEM((WAVES, channels), f32),
            pltpu.VMEM((channels, D), bf16),
            pltpu.VMEM((length, STREAMS * channels), f32),
            pltpu.VMEM((WAVES, 2 * channels), bf16),
            pltpu.VMEM((length, channels), f32),
            pltpu.VMEM((length, channels), bf16),
            pltpu.VMEM((length, channels), f32),
            pltpu.VMEM((length, 2 * channels), bf16),
            pltpu.VMEM((WAVES, 2 * channels), bf16),
            pltpu.SemaphoreType.DMA((8,)),
        ],
        far=4,
        name="mix_fwd",
    )


def mix_bwd_kernel(
    layer, scal, own_a, own_b, got_a, got_b, out_w, conv_w, conv_b, skip,
    proj_far, longc_far, waves_far, spec_far, taps_far, waves_t_far, in_w_far,
    in_low, taps_grad, sums, sent_a, sent_b, keep_a, keep_b,
    proj, longc, waves, spec, taps, waves_t, in_w, mgrad, ds, pieces, prod, corr, sems,
):
    ins = (
        (proj_far, proj),
        (longc_far, longc),
        (waves_far, waves),
        (spec_far, spec),
        (taps_far, taps),
        (waves_t_far, waves_t),
        (in_w_far.at[layer], in_w),
    )
    copies = [pltpu.make_async_copy(a, b, sems.at[i]) for i, (a, b) in enumerate(ins)]
    for copy in copies:
        copy.start()
    first, core = scal[0], scal[1]
    block = own_a.shape[0]
    channels = skip.shape[1]
    row = slice(layer, layer + 1)
    length = 4 * block
    tiles = length // TILE
    for rows, at in halves(own_a, own_b, got_a, got_b, core):
        mgrad[pl.ds(at, block), :] = dot_cols(rows[...], out_w[...])
    skip_sum = jnp.zeros((1, channels), f32)
    copies[0].wait()
    copies[1].wait()
    mid, end = slice(channels, 2 * channels), slice(2 * channels, 3 * channels)
    for tile in range(tiles):
        rows = tile_rows(tile)
        in_first, offset = place(tile, first)
        one = short_tile(proj, conv_w, conv_b, layer, tile, 1, offset, channels)
        two = short_tile(proj, conv_w, conv_b, layer, tile, 2, offset, channels)
        ds[rows, mid] = one
        ds[rows, end] = two
        m = mgrad[rows, :]
        r = m * short_tile(proj, conv_w, conv_b, layer, tile, 0, offset, channels)
        mgrad[rows, :] = r
        ds[rows, :channels] = m * longc[rows, :]
        skip_sum = skip_sum + jnp.sum(r * one * two, axis=0, keepdims=True)
        pieces[rows, :channels] = jnp.where(in_first, r, 0.0).astype(bf16)
        pieces[rows, channels:] = jnp.where(in_first, 0.0, r).astype(bf16)
    sums[ROW_SKIP : ROW_SKIP + 1, :] = skip_sum
    for copy in copies[2:5]:
        copy.wait()
    steps = 2
    part = REACH // steps
    for step in range(steps):
        lo = slice(step * part, (step + 1) * part)
        hi = slice(REACH + step * part, REACH + (step + 1) * part)
        corr_re, corr_im = None, None
        for seg in range(2):
            cols = slice(seg * channels, (seg + 1) * channels)
            re = dot(waves[lo, :], pieces[:, cols])
            im = dot(waves[hi, :], pieces[:, cols])
            t_re, t_im = taps[lo, :], taps[hi, :]
            prod[lo, cols] = (re * t_re + im * t_im).astype(bf16)
            prod[hi, cols] = (im * t_re - re * t_im).astype(bf16)
            g_re, g_im = spec[lo, cols].astype(f32), spec[hi, cols].astype(f32)
            c_re = g_re * re + g_im * im
            c_im = g_re * im - g_im * re
            corr_re = c_re if corr_re is None else corr_re + c_re
            corr_im = c_im if corr_im is None else corr_im + c_im
        corr[lo, :] = corr_re.astype(bf16)
        corr[hi, :] = corr_im.astype(bf16)
    copies[5].wait()
    big = 512
    for r in range(length // big):
        rows = slice(r * big, (r + 1) * big)
        in_first = lax.broadcasted_iota(jnp.int32, (big, 1), 0) + r * big < first
        a = dot(waves_t[rows, :], prod[:, :channels])
        b = dot(waves_t[rows, :], prod[:, channels:])
        total = jnp.where(in_first, a, b) + skip[row, :] * mgrad[rows, :]
        one, two = ds[rows, mid], ds[rows, end]
        ds[rows, mid] = total * two
        ds[rows, end] = total * one
    for stream in range(STREAMS):
        cols = slice(stream * channels, (stream + 1) * channels)
        at = stream * SHORT
        bias_sum = jnp.zeros((1, channels), f32)
        in_sum = jnp.zeros((1, channels), f32)
        lag_sums = [jnp.zeros((1, channels), f32) for _ in range(SHORT)]
        for tile in range(tiles):
            rows = tile_rows(tile)
            _, offset = place(tile, first)
            d = ds[rows, cols]
            p = proj[rows, cols]
            total = d * conv_w[stream, 0, row, :]
            bias_sum = bias_sum + jnp.sum(d, axis=0, keepdims=True)
            lag_sums[0] = lag_sums[0] + jnp.sum(d * p, axis=0, keepdims=True)
            for lag in range(1, SHORT):
                _, later = place(tile, first, lag)
                moved = jnp.where(later >= lag, ahead(ds, tile, cols, lag, tiles - 1), 0.0)
                total = total + moved * conv_w[stream, lag, row, :]
                lag_sums[lag] = lag_sums[lag] + jnp.sum(moved * p, axis=0, keepdims=True)
            in_sum = in_sum + jnp.sum(total, axis=0, keepdims=True)
            in_low[rows, cols] = total.astype(bf16)
        sums[ROW_IN_BIAS + stream : ROW_IN_BIAS + stream + 1, :] = in_sum
        sums[ROW_CONV_B + stream : ROW_CONV_B + stream + 1, :] = bias_sum
        for lag in range(SHORT):
            sums[ROW_CONV_W + at + lag : ROW_CONV_W + at + lag + 1, :] = lag_sums[lag]

    def into(at):
        rows = pl.ds(at, block)
        total = dot_cols(in_low[rows, :channels], in_w[0])
        for stream in range(1, STREAMS):
            cols = slice(stream * channels, (stream + 1) * channels)
            total = total + dot_cols(in_low[rows, cols], in_w[stream])
        return total

    copies[6].wait()
    for half, (sent, keep) in enumerate(((sent_a, keep_a), (sent_b, keep_b))):
        at = pl.multiple_of(2 * block * half + (1 - core) * block, block)
        sent[...] = into(at).astype(bf16)
        at = pl.multiple_of(2 * block * half + core * block, block)
        keep[...] = into(at)
    taps_grad[...] = dot(waves_t[:REACH, :], corr[...]) * (2.0 / WAVES)


def mix_bwd(run, layer, scal, rows, out_w, proj, spec, longc, in_w, conv_w, conv_b, skip, taps, waves, waves_t):
    block, channels = rows[0].shape[0], skip.shape[1]
    length = 4 * block
    return run(
        functools.partial(mix_bwd_kernel, layer),
        [(scal, SMALL)]
        + [(stay(a), None) for a in rows]
        + [(stay(out_w), layer_of(out_w, layer))]
        + [(a, None) for a in (conv_w, conv_b, skip)]
        + [(stay(a), FAR) for a in (proj, longc, waves, spec, taps, waves_t, in_w)],
        [
            struct((length, STREAMS * channels), bf16),
            struct((REACH, channels), f32),
            struct((16, channels), f32),
            struct((block, D), bf16),
            struct((block, D), bf16),
            struct((block, D), f32),
            struct((block, D), f32),
        ],
        scratch=[
            pltpu.VMEM((length, STREAMS * channels), f32),
            pltpu.VMEM((length, channels), f32),
            pltpu.VMEM((WAVES, length), bf16),
            pltpu.VMEM((WAVES, 2 * channels), bf16),
            pltpu.VMEM((WAVES, channels), f32),
            pltpu.VMEM((length, WAVES), bf16),
            pltpu.VMEM((STREAMS, D, channels), bf16),
            pltpu.VMEM((length, channels), f32),
            pltpu.VMEM((length, STREAMS * channels), f32),
            pltpu.VMEM((length, 2 * channels), bf16),
            pltpu.VMEM((WAVES, 2 * channels), bf16),
            pltpu.VMEM((WAVES, channels), bf16),
            pltpu.SemaphoreType.DMA((7,)),
        ],
        name="mix_bwd",
    )


def parts_order(strides):
    bits = len(strides)
    return [sum(((part >> (bits - 1 - i)) & 1) * s for i, s in enumerate(strides)) for part in range(1 << bits)]


def spread_columns(source, target, at, index, order):
    for part, step in enumerate(order):
        cols = pl.ds(pl.multiple_of((index ^ step) * CHUNK, CHUNK), CHUNK)
        target[at, part * CHUNK : (part + 1) * CHUNK] = source[:, cols]


def ffn_grad_kernel(orders, scal, *refs):
    feeds, lows = refs[0:4], refs[4:8]
    (up_a, up_b, hid_a, hid_b), outs, (left, right) = refs[8:12], refs[12:16], refs[16:18]
    block = feeds[0].shape[0]
    index = scal[3]
    for k, (source, (rhs_a, rhs_b)) in enumerate(((feeds, (up_a, up_b)), (lows, (hid_a, hid_b)))):
        right[: 2 * block, :] = rhs_a[...]
        right[2 * block :, :] = rhs_b[...]
        for i in range(4):
            spread_columns(source[i], left, slice(i * block, (i + 1) * block), index, orders[k])
        for half in range(2):
            out = outs[2 * k + half]
            wide = PARTS // 2 * CHUNK
            got = dot_rows(left[:, half * wide : (half + 1) * wide], right[...]).astype(bf16)
            for part in range(PARTS // 2):
                out[part] = got[part * CHUNK : (part + 1) * CHUNK, :]


def ffn_whole_kernel(*refs):
    feeds, lows = refs[0:4], refs[4:8]
    (up_a, up_b, hid_a, hid_b), out, (left, right) = refs[8:12], refs[12], refs[13:15]
    block = feeds[0].shape[0]
    for k, (source, (rhs_a, rhs_b)) in enumerate(((feeds, (up_a, up_b)), (lows, (hid_a, hid_b)))):
        right[: 2 * block, :] = rhs_a[...]
        right[2 * block :, :] = rhs_b[...]
        for i in range(4):
            left[i * block : (i + 1) * block, :] = source[i][...]
        for half in range(2):
            rows = slice(half * D // 2, (half + 1) * D // 2)
            out[k, rows, :] = dot_rows(left[:, rows], right[...]).astype(bf16)


def ffn_whole(run, feeds, lows, ups, hids):
    block, width = feeds[0].shape[0], ups[0].shape[1]
    return run(
        ffn_whole_kernel,
        [(a, None) for a in (*feeds, *lows, *ups, *hids)],
        [struct((2, D, width), bf16)],
        scratch=[pltpu.VMEM((4 * block, D), bf16), pltpu.VMEM((4 * block, width), bf16)],
        name="ffn_whole",
    )[0]


def ffn_grad(run, orders, scal, feeds, lows, ups, hids):
    block, width = feeds[0].shape[0], ups[0].shape[1]
    out = struct((PARTS // 2, CHUNK, width), bf16)
    return run(
        functools.partial(ffn_grad_kernel, orders),
        [(scal, SMALL)] + [(a, None) for a in (*feeds, *lows, *ups, *hids)],
        [out] * 4,
        scratch=[pltpu.VMEM((4 * block, D), bf16), pltpu.VMEM((4 * block, width), bf16)],
        name="ffn_grad",
    )


def mix_whole_kernel(scal, *refs):
    normed, lows = refs[0:4], refs[4:8]
    in_low, mixed, out, left = refs[8:12]
    channels = mixed.shape[1]
    block = normed[0].shape[0]
    for source, rhs, base in ((normed, in_low, 0), (lows, mixed, STREAMS)):
        for rows, at in halves(*source, scal[1]):
            left[pl.ds(at, block), :] = rows[...]
        for half in range(2):
            rows = slice(half * D // 2, (half + 1) * D // 2)
            got = dot_rows(left[:, rows], rhs[...]).astype(bf16)
            for i in range(rhs.shape[1] // channels):
                out[base + i, rows, :] = got[:, i * channels : (i + 1) * channels]


def mix_whole(run, scal, normed, lows, in_low, mixed):
    block, channels = normed[0].shape[0], mixed.shape[1]
    return run(
        mix_whole_kernel,
        [(scal, SMALL)] + [(a, None) for a in (*normed, *lows, in_low, mixed)],
        [struct((STREAMS + 1, D, channels), bf16)],
        scratch=[pltpu.VMEM((4 * block, D), bf16)],
        name="mix_whole",
    )[0]


def mix_grad_kernel(orders, scal, *refs):
    normed, lows = refs[0:4], refs[4:8]
    in_low, mixed = refs[8:10]
    outs, left = refs[10:14], refs[14]
    channels = mixed.shape[1]
    core, index = scal[1], scal[3]
    groups = (
        (normed, in_low, slice(0, 2 * channels), 0, 0),
        (normed, in_low, slice(2 * channels, 3 * channels), 1, 0),
        (lows, mixed, slice(0, channels), 1, 1),
    )
    for source, rhs, cols, group, base in groups:
        own_a, own_b, got_a, got_b = source
        block = own_a.shape[0]
        for rows, at in halves(own_a, own_b, got_a, got_b, core):
            spread_columns(rows, left, pl.ds(at, block), index, orders[group])
        for half in range(2):
            out = outs[2 * group + half]
            wide = PARTS // 2 * CHUNK
            got = dot_rows(left[:, half * wide : (half + 1) * wide], rhs[:, cols]).astype(bf16)
            for part in range(PARTS // 2):
                for i in range(got.shape[1] // channels):
                    block_cols = slice(i * channels, (i + 1) * channels)
                    out[part, base + i] = got[part * CHUNK : (part + 1) * CHUNK, block_cols]


def mix_grad(run, orders, scal, normed, lows, in_low, mixed):
    block, channels = normed[0].shape[0], mixed.shape[1]
    out = struct((PARTS // 2, 2, CHUNK, channels), bf16)
    return run(
        functools.partial(mix_grad_kernel, orders),
        [(scal, SMALL)] + [(a, None) for a in (*normed, *lows, in_low, mixed)],
        [out] * 4,
        scratch=[pltpu.VMEM((4 * block, D), bf16)],
        name="mix_grad",
    )


def halve_kernel(keep, got, sent, kept):
    count = keep.shape[0] // 2
    for i in range(count):
        kept[i] = (keep[i].astype(f32) + got[i].astype(f32)).astype(bf16)
        sent[i] = (keep[count + i].astype(f32) + got[count + i].astype(f32)).astype(bf16)


def halve(run, keep, got):
    out = struct((keep.shape[0] // 2, *keep.shape[1:]), bf16)
    return run(halve_kernel, [(keep, None), (got, None)], [out, out], name="halve")


def total_of(refs, leads):
    return sum(ref[lead].astype(f32) for ref, lead in zip(refs, leads))


def finish_kernel(leads, turned, *refs):
    out, refs = refs[-1], list(refs[:-1])
    for layer, lead in enumerate(leads):
        total = total_of([refs.pop(0) for _ in lead], lead)
        out[layer] = total.T if turned else total


def ffn_finish(run, terms, turned):
    _, rows, cols = terms[0][0][0].shape
    shape = (cols, rows) if turned else (rows, cols)
    leads = [[lead for _, lead in pairs] for pairs in terms]
    return run(
        functools.partial(finish_kernel, leads, turned),
        [(a, None) for pairs in terms for a, _ in pairs],
        [struct((len(terms), *shape), f32)],
        name="ffn_finish",
    )[0]


def mix_finish_kernel(plan, *refs):
    into, out = refs[-2:]
    for layer, streams in enumerate(plan):
        for stream, parts in enumerate(streams):
            total = sum(refs[k][lead].astype(f32) for k, lead in parts)
            if stream < STREAMS:
                into[layer, stream] = total
            else:
                out[layer] = total.T


def mix_finish(run, arrays, plan):
    rows, channels = arrays[0].shape[-2:]
    return run(
        functools.partial(mix_finish_kernel, plan),
        [(a, None) for a in arrays],
        [struct((len(plan), STREAMS, rows, channels), f32), struct((len(plan), channels, rows), f32)],
        name="mix_finish",
    )


def pack_kernel(mix, filt, narrow, up_a, up_b, feed_a, feed_b, in_a, in_b, own, down, out):
    channels = mix.shape[1]
    out[:16, :] = mix[...]
    out[ROW_FILTER : ROW_FILTER + FILT, :] = filt[...]
    for q in range(D // channels):
        cols = slice(q * channels, (q + 1) * channels)
        out[ROW_UP_BIAS + q : ROW_UP_BIAS + q + 1, :] = up_a[:, cols] + up_b[:, cols]
        wide = [feed_a[i : i + 1, cols] + feed_b[i : i + 1, cols] for i in range(3)]
        wide.append(down[:, cols])
        wide += [in_a[i : i + 1, cols] + in_b[i : i + 1, cols] for i in range(2)]
        wide += [own[i : i + 1, cols] for i in range(2)]
        for i, value in enumerate(wide):
            at = ROW_WIDE + 4 * i + q
            out[at : at + 1, :] = value
    groups = [
        narrow[i * NARROW_GROUP : (i + 1) * NARROW_GROUP, :] for i in range(channels // FILT)
    ]
    out[ROW_NARROW:, :] = jnp.concatenate(groups, axis=1)


def pack(run, mix, filt, narrow, ups, feeds, ins, own, down):
    return run(
        pack_kernel,
        [(a, None) for a in (mix, filt, narrow, *ups, *feeds, *ins, own, down)],
        [struct((PACK_ROWS, mix.shape[1]), f32)],
        name="pack_small",
    )[0]


def gate(run, after=()):
    run(lambda: None, [], [], name="gate", after=after)


def sum_kernel(a, b, out):
    out[...] = a[...] + b[...]


def add_pair(run, a, b):
    return run(sum_kernel, [(a, None), (b, None)], [struct(a.shape, f32)], name="add_pair")[0]


def unpack_kernel(layers, *refs):
    chans, wides, outs = refs[:layers], refs[layers : 2 * layers], refs[2 * layers :]
    (gain, shift, out_bias, feed_gain, feed_shift, down_bias, in_bias, conv_w, conv_b, skip, filt, up_bias,
     w_in, b_in, f_in, w_mid, b_mid, f_mid) = outs
    channels = chans[0].shape[1]
    for layer in range(layers):
        chan, wide = chans[layer], wides[layer]
        row = slice(layer, layer + 1)

        def spread(target, ref, at, row=row):
            for q in range(D // channels):
                target[row, q * channels : (q + 1) * channels] = ref[at + q : at + q + 1, :]

        spread(feed_gain, wide, 0)
        spread(feed_shift, wide, 4)
        spread(out_bias, wide, 8)
        spread(down_bias, wide, 12)
        if layer + 1 < layers:
            spread(gain, wide, 16, slice(layer + 1, layer + 2))
            spread(shift, wide, 20, slice(layer + 1, layer + 2))
        if layer == 0:
            spread(gain, wide, 24)
            spread(shift, wide, 28)
        spread(up_bias, chan, ROW_UP_BIAS)
        for stream in range(STREAMS):
            in_bias[stream, row, :] = chan[ROW_IN_BIAS + stream : ROW_IN_BIAS + stream + 1, :]
            conv_b[stream, row, :] = chan[ROW_CONV_B + stream : ROW_CONV_B + stream + 1, :]
            for lag in range(SHORT):
                at = ROW_CONV_W + stream * SHORT + lag
                conv_w[stream, lag, row, :] = chan[at : at + 1, :]
        skip[row, :] = chan[ROW_SKIP : ROW_SKIP + 1, :]
        filt[layer] = chan[ROW_FILTER : ROW_FILTER + FILT, :]
        base = ROW_NARROW - ROW_WIDE
        rows = slice(base, base + NARROW_GROUP)
        narrow = jnp.concatenate(
            [wide[rows, i * FILT : (i + 1) * FILT] for i in range(channels // FILT)], axis=0
        )
        for target, at in ((b_in, NB_IN), (f_in, NF_IN), (b_mid, NB_MID), (f_mid, NF_MID)):
            target[row, :] = narrow[at : at + 1, :]
        w_in[layer] = narrow[:POS, :]
        w_mid[layer] = narrow[NW_MID : NW_MID + FILT, :]


def unpack(run, chans, wides, up_width):
    layers, channels = len(chans), chans[0].shape[1]
    return run(
        functools.partial(unpack_kernel, layers),
        [(a, None) for a in (*chans, *wides)],
        [struct((layers, D), f32)] * 6
        + [
            struct((STREAMS, layers, channels), f32),
            struct((STREAMS, SHORT, layers, channels), f32),
            struct((STREAMS, layers, channels), f32),
            struct((layers, channels), f32),
            struct((layers, FILT, channels), f32),
            struct((layers, up_width), f32),
            struct((layers, POS, FILT), f32),
            struct((layers, FILT), f32),
            struct((layers, FILT), f32),
            struct((layers, FILT, FILT), f32),
            struct((layers, FILT), f32),
            struct((layers, FILT), f32),
        ],
        name="unpack_small",
    )


def dp_swap(x, stride):
    size = lax.axis_size("dp")
    return lax.ppermute(x, "dp", [(i, i ^ stride) for i in range(size)])


class Scatter:
    def __init__(self, run, sent, keep, strides):
        self.run, self.keep = run, keep
        self.strides = list(strides)
        self.got = dp_swap(sent, self.strides.pop(0))

    def step(self):
        sent, self.keep = halve(self.run, self.keep, self.got)
        self.got = dp_swap(sent, self.strides.pop(0))

    def pair(self):
        while self.strides:
            self.step()
        return self.keep, self.got


class Sum:
    def __init__(self, run, value, wide):
        self.run, self.value, self.wide = run, value, wide
        size = lax.axis_size("dp")
        self.todo = [("dp", 1 << i) for i in range(size.bit_length() - 1)]
        self.todo += [("mp", 1 << i) for i in reversed(range(lax.axis_size("mp").bit_length() - 1))]
        self.chan = None
        self.send()

    def send(self):
        axis, stride = self.todo.pop(0)
        if axis == "mp" and self.chan is None:
            self.chan = self.value
            self.value = self.value[self.wide :] if self.wide else self.value
        size = lax.axis_size(axis)
        self.got = lax.ppermute(self.value, axis, [(i, i ^ stride) for i in range(size)])

    def step(self):
        self.value = add_pair(self.run, self.value, self.got)
        if self.todo:
            self.send()
        else:
            self.got = None

    def done(self):
        while self.got is not None:
            self.step()
        return self.chan, self.value


def share_out(pair):
    keep, got = pair
    total = (keep[0].astype(f32) + got[0].astype(f32)).reshape(-1, CHUNK, keep.shape[-1])
    left = lax.axis_size("dp") // PARTS
    index = lax.axis_index("dp")
    stride = 1
    total = total.reshape(total.shape[0], left, CHUNK // left, -1)
    while left > 1:
        total = total.reshape(total.shape[0], left // 2, 2, total.shape[2], -1)
        bit = (index // stride) % 2
        mine = lax.dynamic_index_in_dim(total, bit, 2, keepdims=False)
        other = lax.dynamic_index_in_dim(total, 1 - bit, 2, keepdims=False)
        total = mine + dp_swap(other.astype(bf16), stride).astype(f32)
        left, stride = left // 2, stride * 2
    return total[:, 0]


def shards(
    tokens,
    seg_lengths,
    cotangent,
    mixer_norm_gain,
    mixer_norm_bias,
    in_weight,
    in_bias,
    conv_weight,
    conv_bias,
    filter_in,
    filter_in_bias,
    filter_in_freq,
    filter_mid,
    filter_mid_bias,
    filter_mid_freq,
    filter_out,
    skip_bias,
    out_weight,
    out_bias,
    feed_norm_gain,
    feed_norm_bias,
    feed_up,
    feed_up_bias,
    feed_down,
    feed_down_bias,
):
    block = tokens.shape[1]
    length = block * lax.axis_size("mp")
    channels = in_weight.shape[3]
    layers = in_weight.shape[0]
    spot = lax.axis_index("mp").astype(jnp.int32)
    left = lax.axis_size("dp") // PARTS
    chunk = (lax.axis_index("dp") // left).astype(jnp.int32)
    scal = jnp.stack([seg_lengths[0, 0], spot % 2, spot // 2, chunk, spot])
    table = wave_table(length)
    waves = jnp.asarray(table)
    waves_t = jnp.asarray(np.ascontiguousarray(table.T))
    pos = jnp.asarray(position_table(length))
    run = Chain()

    in_w = in_weight.transpose(0, 2, 1, 3)
    in_b = in_bias.transpose(1, 0, 2)
    conv_w = conv_weight.transpose(1, 2, 0, 3)
    conv_b = conv_bias.transpose(1, 0, 2)
    filter_weights = (
        filter_in, filter_in_bias, filter_in_freq, filter_mid, filter_mid_bias, filter_mid_freq, filter_out
    )
    both = range(2)

    def start_sum(ends):
        got = [core_swap(ends[i]) for i in both]
        out = []
        for i in both:
            here = add_low(run, ends[2 + i], got[i])
            out.append((here, chip_swap(here)))
        return out

    def one_sum(sent, keep):
        here = add_low(run, keep, core_swap(sent))
        return here, chip_swap(here)

    def in_turn(first, pace=None):
        gate(run, [first[1]])
        if pace is None:
            gate(run)
        else:
            pace.step()

    mine = tokens[0]
    other = chip_swap(mine)
    filt = [None] * layers
    early = tuple(stay(a) for a in filter_weights)
    filt[0] = filter_fwd(run, 0, length, scal, stay(pos), early, stay(waves))
    low_a, low_b, res_a, res_b, cot = first_norm(
        run, scal, stay(mine), stay(other), stay(mixer_norm_gain), stay(mixer_norm_bias), stay(cotangent[0])
    )
    res, low = [res_a, res_b], [low_a, low_b]

    stored = []
    back = [None, None]
    for layer in range(layers):
        last = layer + 1 == layers
        entry = res
        got = [core_swap(x) for x in low]
        normed = (*low, *got)
        if layer == 0:
            cot_other = chip_swap(cot)
        proj, spec, longc, mixed, *ends = mix_fwd(
            run, layer, scal, normed, in_w, in_b, conv_w, conv_b, skip_bias, filt[layer][0], out_weight, waves, waves_t
        )
        if layer == 0:
            low_a, low_b, cot_sum = first_grad(run, scal, cot, cot_other)
            cot_low = [low_a, low_b]
        moves = start_sum(ends)
        if not last:
            filt[layer + 1] = filter_fwd(run, layer + 1, length, scal, pos, filter_weights, waves)
        if layer == 0:
            cot_got = [core_swap(x) for x in cot_low]
        middle, feed, feed_got, ffn, sums, back_sums = [], [], [], [], [], []

        def norm_half(i):
            b, a = add_norm(run, layer, layer, *moves[i], res[i], out_bias, feed_norm_gain, feed_norm_bias)
            middle.append(a)
            feed.append(b)
            feed_got.append(core_swap(b))

        def ffn_half(i):
            ffn.append(ffn_fwd(run, layer, feed[i], feed_got[i], feed_up, feed_up_bias, feed_down))
            if last:
                back[i] = ffn_bwd(run, layer, cot_low[i], cot_got[i], feed_up, feed_down, ffn[i][0])

        def sum_half(i):
            if last:
                back_sums.append(one_sum(back[i][2], back[i][3]))
            else:
                sums.append(one_sum(ffn[i][2], ffn[i][3]))

        norm_half(0)
        ffn_half(0)
        in_turn(moves[1])
        sum_half(0)
        norm_half(1)
        ffn_half(1)
        in_turn((back_sums if last else sums)[0])
        sum_half(1)
        stored.append((entry, normed, proj, spec, longc, mixed, middle, feed, feed_got, ffn))
        if not last:
            res, low = [], []
            for i in both:
                b, a = add_norm(
                    run, layer, layer + 1, *sums[i], middle[i], feed_down_bias, mixer_norm_gain, mixer_norm_bias, 1
                )
                res.append(a)
                low.append(b)

    rising, turned = (1, 2, 4), (2, 4, 1)
    feed_orders, mix_orders = (rising, turned), (rising, rising)

    def scatter_pair(sends, orders):
        return [
            Scatter(run, sends[2 * k + 1], sends[2 * k], [left * o for o in orders[k]]) for k in range(2)
        ]

    def scatter_rows(whole_grad):
        return lax.psum_scatter(whole_grad, "dp", scatter_dimension=1, tiled=True)

    def grad_args(layer, low, got, back):
        _, _, _, _, _, _, _, feed, feed_got, ffn = stored[layer]
        return (
            (feed[0], feed_got[0], feed[1], feed_got[1]),
            (low[0], got[0], low[1], got[1]),
            [back[i][0] for i in both],
            [ffn[i][1] for i in both],
        )

    grad, low, got = cot_low, cot_low, cot_got
    down_sum = cot_sum
    moves = back_sums
    feed_shares, mix_shares, packs = ([None] * layers for _ in range(3))
    no_sums = jnp.zeros((8, D), f32)
    in_sums = [no_sums, no_sums]
    for layer in reversed(range(layers)):
        above = layer + 1
        entry, normed, proj, spec, longc, mixed, middle, feed, feed_got, ffn = stored[layer]
        if layer:
            feed_shares[layer] = scatter_rows(ffn_whole(run, *grad_args(layer, low, got, back)))
        if above == layers:
            out_got = [core_swap(ffn[i][2]) for i in both]
            out_send, out_mine = pick_outputs(
                run, layer, scal, [ffn[i][3] for i in both], out_got, middle, feed_down_bias
            )
        new_grad, low, feed_sums = [], [], []
        for i in both:
            b, a, c = norm_back(run, layer, *moves[i], middle[i], grad[i], feed_norm_gain, 1)
            new_grad.append(a)
            low.append(b)
            feed_sums.append(c)
        grad = new_grad
        got = [core_swap(x) for x in low]
        rows = (*low, *got)
        in_low, taps_grad, mix_sums, *ends = mix_bwd(
            run, layer, scal, rows, out_weight, proj, spec, longc, in_w, conv_w, conv_b, skip_bias,
            filt[layer][0], waves, waves_t,
        )
        if layer:
            if above == layers:
                outputs = last_add(run, out_mine, chip_swap(out_send))
            moves = start_sum(ends)
            own_sums = no_sums
            mix_shares[layer] = scatter_rows(mix_whole(run, scal, normed, rows, in_low, mixed))
        else:
            swapped = [core_swap(ends[i]) for i in both]
        filt_out, narrow = filter_bwd(run, layer, length, scal, taps_grad, pos, filter_weights, filt[layer][1])
        if layer == 0:
            send, own, own_sums = last_pick(run, scal, ends[2:], swapped, entry)
            there = chip_swap(send)
        packed = pack(
            run, mix_sums, filt_out, narrow, [back[i][1] for i in both], feed_sums, in_sums, own_sums, down_sum
        )
        packs[layer] = Sum(run, packed, ROW_WIDE)
        if layer == 0:
            sends = mix_grad(
                run, [parts_order(o) for o in mix_orders], scal, normed, rows, in_low, mixed
            )
            mix_bigs = scatter_pair(sends, mix_orders)
            break
        packs[layer].step()
        new_grad, new_low, in_sums, new_got, new_back, back_sums = [], [], [], [], [], []

        def norm_half(i):
            b, a, c = norm_back(run, layer, *moves[i], entry[i], grad[i], mixer_norm_gain)
            new_grad.append(a)
            new_low.append(b)
            in_sums.append(c)
            new_got.append(core_swap(b))

        def ffn_half(i):
            below = stored[layer - 1][9]
            new_back.append(ffn_bwd(run, layer - 1, new_low[i], new_got[i], feed_up, feed_down, below[i][0]))

        def sum_half(i):
            back_sums.append(one_sum(new_back[i][2], new_back[i][3]))

        norm_half(0)
        ffn_half(0)
        in_turn(moves[1], packs[layer])
        sum_half(0)
        norm_half(1)
        ffn_half(1)
        if layer == 1:
            sends = ffn_grad(
                run, [parts_order(o) for o in feed_orders], scal, *grad_args(0, new_low, new_got, new_back)
            )
            up_big, down_big = scatter_pair(sends, feed_orders)
        in_turn(back_sums[0], packs[layer])
        sum_half(1)
        moves = back_sums
        back = new_back
        down_sum = (in_sums[0] + in_sums[1])[2:3]
        grad, low, got = new_grad, new_low, new_got
    packs[0].step()
    up_big.step()
    down_big.step()
    token_grad = last_back(run, 0, scal, own, there, entry, grad, mixer_norm_gain)
    packs[0].step()
    up_big.step()
    mix_bigs[0].step()
    for x in packs[1:]:
        x.step()
    packs[0].step()
    down_big.step()
    mix_bigs[1].step()
    packs[0].step()
    mix_bigs[0].step()
    packs[0].step()
    mix_bigs[1].step()
    up_pair, down_pair = up_big.pair(), down_big.pair()
    if left == 1:
        up_first, down_first = [[(a, 0) for a in pair] for pair in (up_pair, down_pair)]
    else:
        up_first, down_first = [[(share_out(pair), 0)] for pair in (up_pair, down_pair)]
    up_g = ffn_finish(run, [up_first] + [[(a, 0)] for a in feed_shares[1:]], False)
    down_g = ffn_finish(run, [down_first] + [[(a, 1)] for a in feed_shares[1:]], True)
    mix_pairs = [x.pair() for x in mix_bigs]
    if left == 1:
        arrays = [a for pair in mix_pairs for a in pair]
        first = [[(2 * k, (0, i)), (2 * k + 1, (0, i))] for k in both for i in both]
    else:
        arrays = [share_out(pair) for pair in mix_pairs]
        first = [[(k, i)] for k in both for i in both]
    plan = [first]
    for share in mix_shares[1:]:
        plan.append([[(len(arrays), i)] for i in range(STREAMS + 1)])
        arrays.append(share)
    in_g, out_g = mix_finish(run, arrays, plan)
    chans, wides = zip(*[x.done() for x in packs])
    (gain, shift, out_bias_g, feed_gain, feed_shift, down_bias_g, in_bias_g, conv_w_g, conv_b_g, skip_g, filt_g,
     up_bias_g, w_in_g, b_in_g, f_in_g, w_mid_g, b_mid_g, f_mid_g) = unpack(
        run, chans, wides, feed_up.shape[2]
    )
    return (
        outputs[None],
        token_grad[None],
        gain,
        shift,
        in_g.transpose(0, 2, 1, 3),
        in_bias_g.transpose(1, 0, 2),
        conv_w_g.transpose(2, 0, 1, 3),
        conv_b_g.transpose(1, 0, 2),
        w_in_g,
        b_in_g,
        f_in_g,
        w_mid_g,
        b_mid_g,
        f_mid_g,
        filt_g,
        skip_g,
        out_g,
        out_bias_g,
        feed_gain,
        feed_shift,
        up_g,
        up_bias_g,
        down_g,
        down_bias_g,
    )


def solution(mesh):
    in_specs = (
        P("dp", "mp", None),
        P("dp", None),
        P("dp", "mp", None),
        P(),
        P(),
        P(None, None, None, "mp"),
        P(None, None, "mp"),
        P(None, None, None, "mp"),
        P(None, None, "mp"),
        P(),
        P(),
        P(),
        P(),
        P(),
        P(),
        P(None, None, "mp"),
        P(None, "mp"),
        P(None, "mp", None),
        P(),
        P(),
        P(),
        P(None, None, "mp"),
        P(None, "mp"),
        P(None, "mp", None),
        P(),
    )
    out_specs = (
        P("dp", "mp", None),
        P("dp", "mp", None),
        P(),
        P(),
        P(None, "dp", None, "mp"),
        P(None, None, "mp"),
        P(None, None, None, "mp"),
        P(None, None, "mp"),
        P(),
        P(),
        P(),
        P(),
        P(),
        P(),
        P(None, None, "mp"),
        P(None, "mp"),
        P(None, "mp", "dp"),
        P(),
        P(),
        P(),
        P(None, "dp", "mp"),
        P(None, "mp"),
        P(None, "mp", "dp"),
        P(),
    )
    return jax.shard_map(shards, mesh=mesh, in_specs=in_specs, out_specs=out_specs, check_vma=False)
```

```python
import functools
import math

import jax
import jax.numpy as jnp
import ml_dtypes
import numpy as np
from jax import lax
from jax.experimental import pallas as pl
from jax.experimental.pallas import tpu as pltpu
from jax.sharding import PartitionSpec as P

D = 1024
POS = 33
FILT = 64
REACH = 896
WAVES = 2 * REACH
SHORT = 3
STREAMS = 3
TILE = 128
CHUNK = 128
PARTS = D // CHUNK

f32 = jnp.float32
bf16 = jnp.bfloat16
highest = lax.Precision.HIGHEST
norm_eps = 1e-05
slow_rate = math.log(100.0) / 1.5
fast_rate = math.log(100.0) / 0.3
GELU_A = math.sqrt(2.0 / math.pi)
GELU_B = 0.044715
SPARE_MB = 3

ROW_IN_BIAS = 0
ROW_CONV_W = 3
ROW_CONV_B = 12
ROW_SKIP = 15
ROW_FILTER = 16
ROW_UP_BIAS = 80
ROW_WIDE = 84
ROW_NARROW = 116
PACK_ROWS = 144
NARROW_ROWS = 112
NARROW_GROUP = 28
NB_IN, NF_IN, NW_MID, NB_MID, NF_MID = 33, 34, 35, 99, 100


def wave_table(length):
    freq = 2 * np.arange(REACH, dtype=np.int64) + 1
    phase = (freq[:, None] * np.arange(length, dtype=np.int64)[None, :]) % (2 * WAVES)
    angle = phase.astype(np.float64) * (math.pi / WAVES)
    return np.concatenate([np.cos(angle), -np.sin(angle)], axis=0).astype(ml_dtypes.bfloat16)


def position_table(length):
    places = np.arange(REACH, dtype=np.float64)
    count = (POS - 1) // 2
    bands = 0.0001 + np.arange(count, dtype=np.float64) * ((count - 1 - 0.0001) / (count - 1))
    phases = bands[:, None] * places[None, :] * (2.0 * math.pi / length)
    table = np.zeros((64, REACH), np.float32)
    table[0] = places / (length - 1)
    table[1 : 1 + count] = np.cos(phases)
    table[1 + count : POS] = -np.sin(phases)
    return table


def core_swap(x):
    size = lax.axis_size("mp")
    return lax.ppermute(x, "mp", [(i, i ^ 1) for i in range(size)])


def chip_swap(x):
    size = lax.axis_size("mp")
    return lax.ppermute(x, "mp", [(i, i ^ 2) for i in range(size)])


def dot(a, b):
    return jnp.dot(a, b, preferred_element_type=f32)


def dot_rows(a, b):
    return lax.dot_general(a, b, (((0,), (0,)), ((), ())), preferred_element_type=f32)


def dot_cols(a, b):
    return lax.dot_general(a, b, (((1,), (1,)), ((), ())), preferred_element_type=f32)


def fine(a, b, dims):
    return lax.dot_general(a, b, (dims, ((), ())), precision=highest, preferred_element_type=f32)


def whole(shape):
    return pl.BlockSpec(tuple(shape), lambda *_: (0,) * len(shape))


def layer_of(stacked, layer):
    shape = stacked.shape[1:]
    return pl.BlockSpec((None, *shape), lambda *_: (layer,) + (0,) * len(shape))


SMALL = pl.BlockSpec(memory_space=pltpu.SMEM)
FAR = pl.BlockSpec(memory_space=pl.ANY)
MAIN = pl.BlockSpec(memory_space=pltpu.HBM)


def struct(shape, dtype):
    return jax.ShapeDtypeStruct(tuple(shape), dtype)


class Chain:
    def __init__(self):
        self.token = None

    def release(self, arrays):
        *results, self.token = pl.pallas_call(
            lambda *refs: None,
            grid=(1,),
            out_shape=[pltpu.HBM(a.shape, a.dtype) for a in arrays] + [pltpu.HBM((8, 128), f32)],
            in_specs=[FAR] * (len(arrays) + 1),
            out_specs=[MAIN] * (len(arrays) + 1),
            input_output_aliases={i: i for i in range(len(arrays))},
            cost_estimate=pl.CostEstimate(flops=1, bytes_accessed=1, transcendentals=0),
            name="release",
        )(*[stay(a) for a in arrays], stay(self.token))
        return results

    def __call__(self, kernel, operands, outs, scratch=(), far=0, spill=0, name=None, after=()):
        arrays = [a for a, _ in operands]
        specs = [whole(a.shape) if s is None else s for a, s in operands]
        main = far + spill
        out_specs = [MAIN if i < main else whole(o.shape) for i, o in enumerate(outs)]
        spilled = [pltpu.VMEM(o.shape, o.dtype) for o in outs[far:main]]
        scratch = [*scratch, *spilled] + ([pltpu.SemaphoreType.DMA((spill,))] if spill else [])
        held = 0
        for a, s in list(zip(arrays, specs)) + list(zip(outs, out_specs)):
            if s is not SMALL and s is not FAR and s is not MAIN:
                held += math.prod(x for x in s.block_shape if x is not None) * a.dtype.itemsize
        for s in scratch:
            if getattr(s, "memory_space", None) == pltpu.VMEM:
                held += math.prod(s.shape) * jnp.dtype(s.dtype).itemsize
        count, given = len(arrays), len(outs)
        tokens = ([] if self.token is None else [stay(self.token)]) + list(after)

        def body(*refs):
            ins, refs = refs[:count], refs[count + len(tokens) :]
            results, rest = refs[:given], refs[given + 1 :]
            if spill:
                rest, buffers, sems = rest[: -spill - 1], rest[-spill - 1 : -1], rest[-1]
                kernel(*ins, *results[:far], *buffers, *results[main:], *rest)
                copies = [
                    pltpu.make_async_copy(buffers[i], results[far + i], sems.at[i]) for i in range(spill)
                ]
                for copy in copies:
                    copy.start()
                for copy in copies:
                    copy.wait()
            else:
                kernel(*ins, *results, *rest)

        *results, self.token = pl.pallas_call(
            body,
            grid=(1,),
            out_shape=[pltpu.HBM(o.shape, o.dtype) if i < main else o for i, o in enumerate(outs)]
            + [pltpu.HBM((8, 128), f32)],
            in_specs=specs + [FAR] * len(tokens),
            out_specs=out_specs + [MAIN],
            scratch_shapes=scratch,
            compiler_params=pltpu.CompilerParams(vmem_limit_bytes=held + SPARE_MB * 1024 * 1024),
            cost_estimate=pl.CostEstimate(flops=1, bytes_accessed=1, transcendentals=0),
            name=name,
        )(*arrays, *tokens)
        return results


def unit_of(values):
    center = values - jnp.mean(values, axis=-1, keepdims=True)
    spread = jnp.mean(center * center, axis=-1, keepdims=True)
    rstd = lax.rsqrt(spread + norm_eps)
    return center * rstd, rstd


def row_tiles(count, size=32):
    return [slice(i * size, (i + 1) * size) for i in range(count // size)]


def stay(x):
    return pltpu.with_memory_space_constraint(x, pltpu.HBM)


def first_norm_kernel(scal, mine, other, gain, shift, cot, low_a, low_b, res_a, res_b, cot_out):
    chip = scal[2]
    cot_out[...] = cot[...]
    for rows in row_tiles(mine.shape[0]):
        a, b = mine[rows, :].astype(f32), other[rows, :].astype(f32)
        for values, res, low in (
            (jnp.where(chip == 0, a, b), res_a, low_a),
            (jnp.where(chip == 0, b, a), res_b, low_b),
        ):
            res[rows, :] = values
            unit, _ = unit_of(values)
            low[rows, :] = (unit * gain[0:1, :] + shift[0:1, :]).astype(bf16)


def first_norm(run, scal, mine, other, gain, shift, cot):
    block = mine.shape[0]
    return run(
        first_norm_kernel,
        [(scal, SMALL)] + [(a, None) for a in (mine, other, gain, shift, cot)],
        [struct((block, D), bf16)] * 2 + [struct((block, D), f32)] * 2 + [struct((block, D), bf16)],
        spill=2,
        name="first_norm",
    )


def first_grad_kernel(scal, mine, other, sums, low_a, low_b):
    chip = scal[2]
    total = jnp.zeros((8, D), f32)
    for rows in row_tiles(mine.shape[0]):
        a, b = mine[rows, :], other[rows, :]
        low_a[rows, :] = jnp.where(chip == 0, a, b)
        low_b[rows, :] = jnp.where(chip == 0, b, a)
        total = total + fold(a.astype(f32)) + fold(b.astype(f32))
    sums[...] = 0.5 * jnp.sum(total, axis=0, keepdims=True)


def first_grad(run, scal, mine, other):
    block = mine.shape[0]
    return run(
        first_grad_kernel,
        [(scal, SMALL), (mine, None), (other, None)],
        [struct((1, D), f32)] + [struct((block, D), bf16)] * 2,
        spill=1,
        name="first_grad",
    )


def add_kernel(keep, got, out):
    for rows in row_tiles(keep.shape[0], 64):
        out[rows, :] = (keep[rows, :] + got[rows, :].astype(f32)).astype(out.dtype)


def add_low(run, keep, got, after=()):
    out = [struct(keep.shape, bf16)]
    return run(add_kernel, [(keep, None), (got, None)], out, name="add_low", after=after)[0]


def last_pick_kernel(scal, keep_a, got_a, val_a, keep_b, got_b, val_b, send, mine, sums):
    totals = [jnp.zeros((8, D), f32) for _ in range(2)]
    near_a = scal[2] == 0
    for rows in row_tiles(mine.shape[0]):
        parts = []
        for keep, got, values in ((keep_a, got_a, val_a), (keep_b, got_b, val_b)):
            total = keep[rows, :] + got[rows, :].astype(f32)
            unit, _ = unit_of(values[rows, :])
            totals[0] = totals[0] + fold(total * unit)
            totals[1] = totals[1] + fold(total)
            parts.append(total)
        mine[rows, :] = jnp.where(near_a, parts[0], parts[1])
        send[rows, :] = jnp.where(near_a, parts[1], parts[0]).astype(bf16)
    for i, total in enumerate(totals):
        sums[i : i + 1, :] = jnp.sum(total, axis=0, keepdims=True)
    sums[2:8, :] = jnp.zeros((6, D), f32)


def last_pick(run, scal, keeps, gots, entry):
    shape = keeps[0].shape
    operands = [a for i in range(2) for a in (keeps[i], gots[i], entry[i])]
    return run(
        last_pick_kernel,
        [(scal, SMALL)] + [(a, None) for a in operands],
        [struct(shape, bf16), struct(shape, f32), struct((8, D), f32)],
        name="last_pick",
    )


def add_norm_kernel(layer, norm_layer, here, there, residual, bias, gain, shift, low, out):
    for rows in row_tiles(here.shape[0]):
        values = residual[rows, :] + here[rows, :].astype(f32) + there[rows, :].astype(f32)
        values = values + bias[layer : layer + 1, :]
        out[rows, :] = values
        unit, _ = unit_of(values)
        low[rows, :] = (
            unit * gain[norm_layer : norm_layer + 1, :] + shift[norm_layer : norm_layer + 1, :]
        ).astype(bf16)


def add_norm(run, layer, norm_layer, here, there, residual, bias, gain, shift, spill=0):
    shape = here.shape
    return run(
        functools.partial(add_norm_kernel, layer, norm_layer),
        [(a, None) for a in (here, there, residual, bias, gain, shift)],
        [struct(shape, bf16), struct(shape, f32)],
        spill=spill,
        name="add_norm",
    )


def pick_kernel(layer, scal, keep_a, got_a, keep_b, got_b, mid_a, mid_b, bias, send, mine):
    def pick(near, far_away):
        keep, got, middle = near
        for rows in row_tiles(mine.shape[0]):
            values = keep[rows, :] + got[rows, :].astype(f32) + middle[rows, :]
            mine[rows, :] = values + bias[layer : layer + 1, :]
            send[rows, :] = (far_away[0][rows, :] + far_away[1][rows, :].astype(f32)).astype(bf16)

    @pl.when(scal[2] == 0)
    def _():
        pick((keep_a, got_a, mid_a), (keep_b, got_b))

    @pl.when(scal[2] != 0)
    def _():
        pick((keep_b, got_b, mid_b), (keep_a, got_a))


def pick_outputs(run, layer, scal, keeps, gots, middles, bias):
    shape = keeps[0].shape
    operands = (keeps[0], gots[0], keeps[1], gots[1], *middles, bias)
    return run(
        functools.partial(pick_kernel, layer),
        [(scal, SMALL)] + [(a, None) for a in operands],
        [struct(shape, bf16), struct(shape, f32)],
        name="pick_outputs",
    )


def last_add_kernel(mine, there, out):
    for rows in row_tiles(out.shape[0], 64):
        out[rows, :] = mine[rows, :] + there[rows, :].astype(f32)


def last_add(run, mine, there):
    return run(last_add_kernel, [(mine, None), (there, None)], [struct(mine.shape, f32)], name="last_add")[0]


def fold(x):
    return sum(x[8 * i : 8 * i + 8, :] for i in range(x.shape[0] // 8))


def norm_back_kernel(layer, here, there, values, grad, gain, out, sums, low):
    totals = [jnp.zeros((8, D), f32) for _ in range(3)]
    for rows in row_tiles(here.shape[0], 16):
        dy = here[rows, :].astype(f32) + there[rows, :].astype(f32)
        unit, rstd = unit_of(values[rows, :])
        scaled = dy * gain[layer : layer + 1, :]
        into = rstd * (
            scaled
            - jnp.mean(scaled, axis=-1, keepdims=True)
            - unit * jnp.mean(scaled * unit, axis=-1, keepdims=True)
        )
        new = grad[rows, :].astype(f32) + into
        out[rows, :] = new
        low[rows, :] = new.astype(bf16)
        for k, part in enumerate((dy * unit, dy, new)):
            totals[k] = totals[k] + fold(part)
    for k, total in enumerate(totals):
        sums[k : k + 1, :] = 0.5 * jnp.sum(total, axis=0, keepdims=True)
    sums[3:8, :] = jnp.zeros((5, D), f32)


def norm_back(run, layer, here, there, values, grad, gain, spill=0):
    shape = here.shape
    return run(
        functools.partial(norm_back_kernel, layer),
        [(a, None) for a in (here, there, values, grad, gain)],
        [struct(shape, f32), struct((8, D), f32), struct(shape, bf16)],
        spill=2 + spill,
        name="norm_back",
    )


def last_back_kernel(layer, scal, mine, there, val_a, val_b, grad_a, grad_b, gain, out):
    near_a = scal[2] == 0
    for rows in row_tiles(out.shape[0], 16):
        dy = mine[rows, :] + there[rows, :].astype(f32)
        unit, rstd = unit_of(jnp.where(near_a, val_a[rows, :], val_b[rows, :]))
        scaled = dy * gain[layer : layer + 1, :]
        into = rstd * (
            scaled
            - jnp.mean(scaled, axis=-1, keepdims=True)
            - unit * jnp.mean(scaled * unit, axis=-1, keepdims=True)
        )
        out[rows, :] = jnp.where(near_a, grad_a[rows, :], grad_b[rows, :]) + into


def last_back(run, layer, scal, mine, there, entry, grad, gain):
    return run(
        functools.partial(last_back_kernel, layer),
        [(scal, SMALL), (mine, None), (there, None)]
        + [(a, None) for a in (*entry, *grad, gain)],
        [struct(mine.shape, f32)],
        name="last_back",
    )[0]


def ffn_fwd_kernel(
    layer, own, got, up_far, up_bias, down_far, pre_far, hid_far, sent, keep, both, pre, hid, up, down, sems
):
    copy_up = pltpu.make_async_copy(up_far.at[layer], up, sems.at[2])
    copy_down = pltpu.make_async_copy(down_far.at[layer], down, sems.at[3])
    copy_up.start()
    copy_down.start()
    half = own.shape[0]
    both[:half, :] = own[...]
    both[half:, :] = got[...]
    copy_up.wait()
    v = dot(both[...], up[...]) + up_bias[layer : layer + 1, :]
    pre[...] = v.astype(bf16)
    hid[...] = (0.5 * v * (1.0 + jnp.tanh(GELU_A * (v + GELU_B * v * v * v)))).astype(bf16)
    copies = [
        pltpu.make_async_copy(a, b, sems.at[i]) for i, (a, b) in enumerate(((pre, pre_far), (hid, hid_far)))
    ]
    for copy in copies:
        copy.start()
    copy_down.wait()
    total = dot(hid[...], down[...])
    keep[...] = total[:half, :]
    sent[...] = total[half:, :].astype(bf16)
    for copy in copies:
        copy.wait()


def ffn_fwd(run, layer, own, got, up, up_bias, down):
    half, width = own.shape[0], up.shape[2]
    return run(
        functools.partial(ffn_fwd_kernel, layer),
        [(own, None), (got, None), (up, FAR), (up_bias, None), (down, FAR)],
        [
            struct((2 * half, width), bf16),
            struct((2 * half, width), bf16),
            struct((half, D), bf16),
            struct((half, D), f32),
        ],
        scratch=[
            pltpu.VMEM((2 * half, D), bf16),
            pltpu.VMEM((2 * half, width), bf16),
            pltpu.VMEM((2 * half, width), bf16),
            pltpu.VMEM((D, width), bf16),
            pltpu.VMEM((width, D), bf16),
            pltpu.SemaphoreType.DMA((4,)),
        ],
        far=2,
        name="ffn_fwd",
    )


def ffn_bwd_kernel(
    layer, own, got, up_far, down_far, pre_far, up_low_far, bias_sum, sent, keep,
    both, up, down, pre, up_low, sems,
):
    ins = ((down_far.at[layer], down), (pre_far, pre), (up_far.at[layer], up))
    copies = [pltpu.make_async_copy(a, b, sems.at[i]) for i, (a, b) in enumerate(ins)]
    for copy in copies:
        copy.start()
    half = own.shape[0]
    both[:half, :] = own[...]
    both[half:, :] = got[...]
    copies[0].wait()
    copies[1].wait()
    v = pre[...].astype(f32)
    t = jnp.tanh(GELU_A * (v + GELU_B * v * v * v))
    slope = 0.5 * (1.0 + t) + 0.5 * v * (1.0 - t * t) * (GELU_A * (1.0 + 3.0 * GELU_B * v * v))
    g = dot_cols(both[...], down[...]) * slope
    bias_sum[...] = jnp.sum(g, axis=0, keepdims=True)
    up_low[...] = g.astype(bf16)
    copy_low = pltpu.make_async_copy(up_low, up_low_far, sems.at[3])
    copy_low.start()
    copies[2].wait()
    total = dot_cols(up_low[...], up[...])
    keep[...] = total[:half, :]
    sent[...] = total[half:, :].astype(bf16)
    copy_low.wait()


def ffn_bwd(run, layer, own, got, up, down, pre, near):
    half, width = own.shape[0], up.shape[2]
    if not near:
        up, down = stay(up), stay(down)
    up_low, bias_sum, sent, keep = run(
        functools.partial(ffn_bwd_kernel, layer),
        [(own, None), (got, None), (up, FAR), (down, FAR), (stay(pre), FAR)],
        [
            struct((2 * half, width), bf16),
            struct((1, width), f32),
            struct((half, D), bf16),
            struct((half, D), f32),
        ],
        scratch=[
            pltpu.VMEM((2 * half, D), bf16),
            pltpu.VMEM((D, width), bf16),
            pltpu.VMEM((width, D), bf16),
            pltpu.VMEM((2 * half, width), bf16),
            pltpu.VMEM((2 * half, width), bf16),
            pltpu.SemaphoreType.DMA((4,)),
        ],
        far=1,
        spill=1,
        name="ffn_bwd",
    )
    return bias_sum, up_low, sent, keep


def sine(x, both=False):
    turns = jnp.floor(x * (1.0 / math.pi) + 0.5)
    rest = (x - turns * 3.140625) - turns * 9.67653589793e-4
    sign = 1.0 - 2.0 * (turns - 2.0 * jnp.floor(turns * 0.5))
    sq = rest * rest
    odd = -1.0 / 39916800.0
    for c in (1.0 / 362880.0, -1.0 / 5040.0, 1.0 / 120.0, -1.0 / 6.0, 1.0):
        odd = odd * sq + c
    value = sign * rest * odd
    if not both:
        return value
    even = 1.0 / 479001600.0
    for c in (-1.0 / 3628800.0, 1.0 / 40320.0, -1.0 / 720.0, 1.0 / 24.0, -0.5, 1.0):
        even = even * sq + c
    return value, sign * even


def decay(spot, channels, length):
    lane = lax.broadcasted_iota(jnp.int32, (1, channels), 1) + spot * channels
    row = lax.broadcasted_iota(jnp.int32, (REACH, channels), 0).astype(f32)
    rate = slow_rate + (fast_rate - slow_rate) * lane.astype(f32) / (D - 1)
    return jnp.exp(-(row * (1.0 / (length - 1))) * rate)


def columns(layer, *refs):
    rows = [r[layer : layer + 1, :] for r in refs] + [jnp.zeros((8 - len(refs), FILT), f32)]
    wide = jnp.concatenate([jnp.concatenate(rows, axis=0), jnp.zeros((8, 128 - FILT), f32)], axis=1).T
    return [wide[:FILT, i : i + 1] for i in range(len(refs))]


def filter_fwd_kernel(
    layer, length, scal, pos, w_in, b_in, f_in, w_mid, b_mid, f_mid, w_out, waves, spec, kept
):
    channels = w_out.shape[1]
    b_in, f_in, b_mid, f_mid = columns(layer, b_in, f_in, b_mid, f_mid)
    z = fine(w_in[...], pos[:POS, :], ((0,), (0,))) + b_in
    h, c = sine(f_in * z, both=True)
    kept[0] = z
    kept[1] = h
    kept[2] = c
    z = fine(w_mid[...], h, ((0,), (0,))) + b_mid
    h, c = sine(f_mid * z, both=True)
    kept[3] = z
    kept[4] = h
    kept[5] = c
    taps = fine(h, w_out[...], ((0,), (0,))) * decay(scal[4], channels, length)
    spec[...] = dot(waves[:, :REACH], taps.astype(bf16)) * (2.0 / WAVES)


def filter_fwd(run, layer, length, scal, pos, weights, waves):
    channels = weights[-1].shape[2]
    return run(
        functools.partial(filter_fwd_kernel, layer, length),
        [(scal, SMALL), (pos, None)]
        + [(a, layer_of(a, layer) if a.ndim == 3 else None) for a in weights]
        + [(waves, None)],
        [struct((WAVES, channels), f32), struct((6, FILT, REACH), f32)],
        spill=2,
        name="filter_fwd",
    )


def filter_bwd_kernel(layer, length, scal, taps_grad, pos, f_in, w_mid, f_mid, w_out, kept, by_chan, narrow):
    channels = w_out.shape[1]
    dt = taps_grad[...] * decay(scal[4], channels, length)
    by_chan[...] = fine(kept[4], dt, ((1,), (0,)))
    f_in, f_mid = columns(layer, f_in, f_mid)
    dh = fine(w_out[...], dt, ((1,), (1,)))
    c = kept[5] * dh
    dz = c * f_mid
    narrow[NW_MID : NW_MID + FILT, :] = fine(kept[1], dz, ((1,), (1,)))
    mid_sums = jnp.concatenate(
        [jnp.sum(dz, axis=1, keepdims=True), jnp.sum(c * kept[3], axis=1, keepdims=True)], axis=1
    )
    dh = fine(w_mid[...], dz, ((1,), (0,)))
    c = kept[2] * dh
    dz = c * f_in
    narrow[:POS, :] = fine(pos[...], dz, ((1,), (1,)))[:POS, :]
    in_sums = jnp.concatenate(
        [jnp.sum(dz, axis=1, keepdims=True), jnp.sum(c * kept[0], axis=1, keepdims=True)], axis=1
    )
    sums = jnp.concatenate([in_sums, mid_sums, jnp.zeros((FILT, 124), f32)], axis=1).T
    narrow[NB_IN : NB_IN + 2, :] = sums[0:2, :]
    narrow[NB_MID : NB_MID + 2, :] = sums[2:4, :]
    narrow[NF_MID + 1 :, :] = jnp.zeros((NARROW_ROWS - NF_MID - 1, FILT), f32)


def filter_bwd(run, layer, length, scal, taps_grad, pos, weights, kept):
    _, _, f_in, w_mid, _, f_mid, w_out = weights
    return run(
        functools.partial(filter_bwd_kernel, layer, length),
        [(scal, SMALL), (taps_grad, None), (pos, None)]
        + [(a, layer_of(a, layer) if a.ndim == 3 else None) for a in (f_in, w_mid, f_mid, w_out)]
        + [(kept, None)],
        [struct((FILT, w_out.shape[2]), f32), struct((NARROW_ROWS, FILT), f32)],
        name="filter_bwd",
    )


def lagged(ref, tile, cols, lag, before=None):
    if tile:
        return ref[tile * TILE - lag : (tile + 1) * TILE - lag, cols]
    if before is None:
        head = jnp.zeros((lag, cols.stop - cols.start), f32)
    else:
        head = before[before.shape[0] - lag :, cols]
    return jnp.concatenate([head, ref[: TILE - lag, cols]], axis=0)


def ahead(ref, tile, cols, lag, last):
    if tile < last:
        return ref[tile * TILE + lag : (tile + 1) * TILE + lag, cols]
    empty = jnp.zeros((lag, cols.stop - cols.start), f32)
    return jnp.concatenate([ref[tile * TILE + lag : (tile + 1) * TILE, cols], empty], axis=0)


def place(tile, first, shift=0):
    row = lax.broadcasted_iota(jnp.int32, (TILE, 1), 0) + (tile * TILE + shift)
    in_first = row < first
    return in_first, jnp.where(in_first, row, row - first)


def short_tile(proj, conv_w, conv_b, layer, tile, stream, offset, channels, before=None):
    cols = slice(stream * channels, (stream + 1) * channels)
    row = slice(layer, layer + 1)
    total = proj[tile * TILE : (tile + 1) * TILE, cols] * conv_w[stream, 0, row, :]
    total = total + conv_b[stream, row, :]
    for lag in range(1, SHORT):
        weight = conv_w[stream, lag, row, :]
        total = total + jnp.where(offset >= lag, lagged(proj, tile, cols, lag, before) * weight, 0.0)
    return total


def tile_rows(tile):
    return slice(tile * TILE, (tile + 1) * TILE)


def halves(own_a, own_b, got_a, got_b, core):
    block = own_a.shape[0]
    out = []
    for half, (own, got) in enumerate(((own_a, got_a), (own_b, got_b))):
        for rows, side in ((own, core), (got, 1 - core)):
            out.append((rows, pl.multiple_of(2 * block * half + side * block, block)))
    return out


def mix_fwd_kernel(layer, half, *refs):
    (scal, in_b, conv_w, conv_b, skip, own_far, got_far, in_w_far, taps_far, out_w_far, waves_far, waves_t_far), refs = (
        refs[:12],
        refs[12:],
    )
    before, prev = None, None
    if half:
        (before, prev), refs = refs[:2], refs[2:]
    (proj_far, longc_far, mixed_far, spec, tail, sent, keep), refs = refs[:7], refs[7:]
    own, got, in_w, waves, waves_t, taps, out_w, proj, gated, mixed, s0, pieces, prod, sems = refs
    block = own.shape[0]
    length = 2 * block
    first_ins = ((own_far, own), (got_far, got), (in_w_far.at[layer], in_w))
    first_copies = [pltpu.make_async_copy(a, b, sems.at[8 + i]) for i, (a, b) in enumerate(first_ins)]
    for copy in first_copies:
        copy.start()
    places = slice(half * length, (half + 1) * length)
    ins = [
        (waves_far.at[:, places], waves),
        (taps_far, taps),
        (waves_t_far.at[places, :], waves_t),
        (out_w_far.at[layer], out_w),
    ]
    copies = [pltpu.make_async_copy(a, b, sems.at[i]) for i, (a, b) in enumerate(ins)]
    outs = ((proj, proj_far), (gated, longc_far), (mixed, mixed_far))
    copy_proj, copy_long, copy_mixed = [
        pltpu.make_async_copy(a, b, sems.at[4 + i]) for i, (a, b) in enumerate(outs)
    ]
    for copy in copies:
        copy.start()
    for copy in first_copies:
        copy.wait()
    first, core = scal[0], scal[1]
    channels = skip.shape[1]
    row = slice(layer, layer + 1)
    sides = [pl.multiple_of(side * block, block) for side in (core, 1 - core)]
    for rows, at in zip((own, got), sides):
        for stream in range(STREAMS):
            cols = slice(stream * channels, (stream + 1) * channels)
            proj[pl.ds(at, block), cols] = dot(rows[...], in_w[stream]) + in_b[stream, row, :]
    copy_proj.start()
    tail[...] = proj[length - 8 :, :]
    for tile in range(length // TILE):
        rows = tile_rows(tile)
        in_first, offset = place(tile, first, half * length)
        one, two, zero = [
            short_tile(proj, conv_w, conv_b, layer, tile, stream, offset, channels, before)
            for stream in (1, 2, 0)
        ]
        g = one * two
        gated[rows, :] = g
        s0[rows, :] = zero
        pieces[rows, :channels] = jnp.where(in_first, g, 0.0).astype(bf16)
        pieces[rows, channels:] = jnp.where(in_first, 0.0, g).astype(bf16)
    copies[0].wait()
    copies[1].wait()
    steps = 2
    part = REACH // steps
    for step in range(steps):
        lo = slice(step * part, (step + 1) * part)
        hi = slice(REACH + step * part, REACH + (step + 1) * part)
        for seg in range(2):
            cols = slice(seg * channels, (seg + 1) * channels)
            re = dot(waves[lo, :], pieces[:, cols])
            im = dot(waves[hi, :], pieces[:, cols])
            if half:
                re = re + prev[lo, cols].astype(f32)
                im = im + prev[hi, cols].astype(f32)
            t_re, t_im = taps[lo, :], taps[hi, :]
            spec[lo, cols] = re.astype(bf16)
            spec[hi, cols] = im.astype(bf16)
            prod[lo, cols] = (re * t_re - im * t_im).astype(bf16)
            prod[hi, cols] = (re * t_im + im * t_re).astype(bf16)
    copies[2].wait()
    in_first = lax.broadcasted_iota(jnp.int32, (length, 1), 0) + half * length < first
    a = dot(waves_t[...], prod[:, :channels])
    b = dot(waves_t[...], prod[:, channels:])
    total = jnp.where(in_first, a, b) + skip[row, :] * gated[...]
    gated[...] = total
    mixed[...] = (total * s0[...]).astype(bf16)
    copy_long.start()
    copy_mixed.start()
    copies[3].wait()
    keep[...] = dot(mixed[pl.ds(sides[0], block), :], out_w[...])
    sent[...] = dot(mixed[pl.ds(sides[1], block), :], out_w[...]).astype(bf16)
    for copy in (copy_proj, copy_long, copy_mixed):
        copy.wait()


def mix_fwd(run, layer, half, scal, own, got, in_w, in_b, conv_w, conv_b, skip, taps, out_w, waves, waves_t, prev):
    block, channels = own.shape[0], skip.shape[1]
    length = 2 * block
    extra = [] if prev is None else [(a, None) for a in prev]
    proj, longc, mixed, spec, tail, sent, keep = run(
        functools.partial(mix_fwd_kernel, layer, half),
        [(scal, SMALL)]
        + [(a, None) for a in (in_b, conv_w, conv_b, skip)]
        + [(a, FAR) for a in (own, got)]
        + [(stay(a), FAR) for a in (in_w, taps, out_w, waves, waves_t)]
        + extra,
        [
            struct((length, STREAMS * channels), f32),
            struct((length, channels), f32),
            struct((length, channels), bf16),
            struct((WAVES, 2 * channels), bf16),
            struct((8, STREAMS * channels), f32),
            struct((block, D), bf16),
            struct((block, D), f32),
        ],
        scratch=[
            pltpu.VMEM((block, D), bf16),
            pltpu.VMEM((block, D), bf16),
            pltpu.VMEM((STREAMS, D, channels), bf16),
            pltpu.VMEM((WAVES, length), bf16),
            pltpu.VMEM((length, WAVES), bf16),
            pltpu.VMEM((WAVES, channels), f32),
            pltpu.VMEM((channels, D), bf16),
            pltpu.VMEM((length, STREAMS * channels), f32),
            pltpu.VMEM((length, channels), f32),
            pltpu.VMEM((length, channels), bf16),
            pltpu.VMEM((length, channels), f32),
            pltpu.VMEM((length, 2 * channels), bf16),
            pltpu.VMEM((WAVES, 2 * channels), bf16),
            pltpu.SemaphoreType.DMA((11,)),
        ],
        far=3,
        spill=half,
        name="mix_fwd",
    )
    return (proj, longc, mixed), (tail, spec), sent, keep


def mix_bwd_kernel(
    layer, scal, conv_w, conv_b, skip, own_a_far, own_b_far, got_a_far, got_b_far, out_w_far,
    proj_a_far, proj_b_far, longc_a_far, longc_b_far, waves_far, spec_far, taps_far, waves_t_far, in_w_far,
    in_low, taps_grad, sums, sent_a, sent_b, keep_a, keep_b,
    own_a, own_b, got_a, got_b, out_w, proj, longc, waves, spec, taps, waves_t, in_w, mgrad, ds, pieces, prod,
    corr, sems,
):
    first_ins = (
        (own_a_far, own_a),
        (own_b_far, own_b),
        (got_a_far, got_a),
        (got_b_far, got_b),
        (out_w_far.at[layer], out_w),
    )
    first_copies = [pltpu.make_async_copy(a, b, sems.at[9 + i]) for i, (a, b) in enumerate(first_ins)]
    for copy in first_copies:
        copy.start()
    half_rows = proj_a_far.shape[0]
    near, later = pl.ds(0, half_rows), pl.ds(half_rows, half_rows)
    ins = (
        (proj_a_far, proj.at[near, :]),
        (longc_a_far, longc.at[near, :]),
        (proj_b_far, proj.at[later, :]),
        (longc_b_far, longc.at[later, :]),
        (waves_far, waves),
        (spec_far, spec),
        (taps_far, taps),
        (waves_t_far, waves_t),
        (in_w_far.at[layer], in_w),
    )
    copies = [pltpu.make_async_copy(a, b, sems.at[i]) for i, (a, b) in enumerate(ins)]
    for copy in copies[:4]:
        copy.start()
    first, core = scal[0], scal[1]
    block = own_a.shape[0]
    channels = skip.shape[1]
    row = slice(layer, layer + 1)
    length = 4 * block
    tiles = length // TILE
    for copy in first_copies:
        copy.wait()
    for copy in copies[4:]:
        copy.start()
    for rows, at in halves(own_a, own_b, got_a, got_b, core):
        mgrad[pl.ds(at, block), :] = dot_cols(rows[...], out_w[...])
    skip_sum = jnp.zeros((1, channels), f32)
    for copy in copies[:4]:
        copy.wait()
    mid, end = slice(channels, 2 * channels), slice(2 * channels, 3 * channels)
    for tile in range(tiles):
        rows = tile_rows(tile)
        in_first, offset = place(tile, first)
        one = short_tile(proj, conv_w, conv_b, layer, tile, 1, offset, channels)
        two = short_tile(proj, conv_w, conv_b, layer, tile, 2, offset, channels)
        ds[rows, mid] = one
        ds[rows, end] = two
        m = mgrad[rows, :]
        r = m * short_tile(proj, conv_w, conv_b, layer, tile, 0, offset, channels)
        mgrad[rows, :] = r
        ds[rows, :channels] = m * longc[rows, :]
        skip_sum = skip_sum + jnp.sum(r * one * two, axis=0, keepdims=True)
        pieces[rows, :channels] = jnp.where(in_first, r, 0.0).astype(bf16)
        pieces[rows, channels:] = jnp.where(in_first, 0.0, r).astype(bf16)
    sums[ROW_SKIP : ROW_SKIP + 1, :] = skip_sum
    for copy in copies[4:7]:
        copy.wait()
    steps = 2
    part = REACH // steps
    for step in range(steps):
        lo = slice(step * part, (step + 1) * part)
        hi = slice(REACH + step * part, REACH + (step + 1) * part)
        corr_re, corr_im = None, None
        for seg in range(2):
            cols = slice(seg * channels, (seg + 1) * channels)
            re = dot(waves[lo, :], pieces[:, cols])
            im = dot(waves[hi, :], pieces[:, cols])
            t_re, t_im = taps[lo, :], taps[hi, :]
            prod[lo, cols] = (re * t_re + im * t_im).astype(bf16)
            prod[hi, cols] = (im * t_re - re * t_im).astype(bf16)
            g_re, g_im = spec[lo, cols].astype(f32), spec[hi, cols].astype(f32)
            c_re = g_re * re + g_im * im
            c_im = g_re * im - g_im * re
            corr_re = c_re if corr_re is None else corr_re + c_re
            corr_im = c_im if corr_im is None else corr_im + c_im
        corr[lo, :] = corr_re.astype(bf16)
        corr[hi, :] = corr_im.astype(bf16)
    copies[7].wait()
    big = 512
    for r in range(length // big):
        rows = slice(r * big, (r + 1) * big)
        in_first = lax.broadcasted_iota(jnp.int32, (big, 1), 0) + r * big < first
        a = dot(waves_t[rows, :], prod[:, :channels])
        b = dot(waves_t[rows, :], prod[:, channels:])
        total = jnp.where(in_first, a, b) + skip[row, :] * mgrad[rows, :]
        one, two = ds[rows, mid], ds[rows, end]
        ds[rows, mid] = total * two
        ds[rows, end] = total * one
    for stream in range(STREAMS):
        cols = slice(stream * channels, (stream + 1) * channels)
        at = stream * SHORT
        bias_sum = jnp.zeros((1, channels), f32)
        in_sum = jnp.zeros((1, channels), f32)
        lag_sums = [jnp.zeros((1, channels), f32) for _ in range(SHORT)]
        for tile in range(tiles):
            rows = tile_rows(tile)
            _, offset = place(tile, first)
            d = ds[rows, cols]
            p = proj[rows, cols]
            total = d * conv_w[stream, 0, row, :]
            bias_sum = bias_sum + jnp.sum(d, axis=0, keepdims=True)
            lag_sums[0] = lag_sums[0] + jnp.sum(d * p, axis=0, keepdims=True)
            for lag in range(1, SHORT):
                _, later = place(tile, first, lag)
                moved = jnp.where(later >= lag, ahead(ds, tile, cols, lag, tiles - 1), 0.0)
                total = total + moved * conv_w[stream, lag, row, :]
                lag_sums[lag] = lag_sums[lag] + jnp.sum(moved * p, axis=0, keepdims=True)
            in_sum = in_sum + jnp.sum(total, axis=0, keepdims=True)
            in_low[rows, cols] = total.astype(bf16)
        sums[ROW_IN_BIAS + stream : ROW_IN_BIAS + stream + 1, :] = in_sum
        sums[ROW_CONV_B + stream : ROW_CONV_B + stream + 1, :] = bias_sum
        for lag in range(SHORT):
            sums[ROW_CONV_W + at + lag : ROW_CONV_W + at + lag + 1, :] = lag_sums[lag]

    def into(at):
        rows = pl.ds(at, block)
        total = dot_cols(in_low[rows, :channels], in_w[0])
        for stream in range(1, STREAMS):
            cols = slice(stream * channels, (stream + 1) * channels)
            total = total + dot_cols(in_low[rows, cols], in_w[stream])
        return total

    copies[8].wait()
    for half, (sent, keep) in enumerate(((sent_a, keep_a), (sent_b, keep_b))):
        at = pl.multiple_of(2 * block * half + (1 - core) * block, block)
        sent[...] = into(at).astype(bf16)
        at = pl.multiple_of(2 * block * half + core * block, block)
        keep[...] = into(at)
    taps_grad[...] = dot(waves_t[:REACH, :], corr[...]) * (2.0 / WAVES)


def mix_bwd(run, layer, scal, rows, out_w, saved, spec, in_w, conv_w, conv_b, skip, taps, waves, waves_t):
    block, channels = rows[0].shape[0], skip.shape[1]
    length = 4 * block
    return run(
        functools.partial(mix_bwd_kernel, layer),
        [(scal, SMALL)]
        + [(a, None) for a in (conv_w, conv_b, skip)]
        + [(a, FAR) for a in rows]
        + [(stay(out_w), FAR)]
        + [(stay(a), FAR) for a in (saved[0][0], saved[1][0], saved[0][1], saved[1][1], waves, spec, taps, waves_t, in_w)],
        [
            struct((length, STREAMS * channels), bf16),
            struct((REACH, channels), f32),
            struct((16, channels), f32),
            struct((block, D), bf16),
            struct((block, D), bf16),
            struct((block, D), f32),
            struct((block, D), f32),
        ],
        scratch=[
            pltpu.VMEM((block, D), bf16),
            pltpu.VMEM((block, D), bf16),
            pltpu.VMEM((block, D), bf16),
            pltpu.VMEM((block, D), bf16),
            pltpu.VMEM((channels, D), bf16),
            pltpu.VMEM((length, STREAMS * channels), f32),
            pltpu.VMEM((length, channels), f32),
            pltpu.VMEM((WAVES, length), bf16),
            pltpu.VMEM((WAVES, 2 * channels), bf16),
            pltpu.VMEM((WAVES, channels), f32),
            pltpu.VMEM((length, WAVES), bf16),
            pltpu.VMEM((STREAMS, D, channels), bf16),
            pltpu.VMEM((length, channels), f32),
            pltpu.VMEM((length, STREAMS * channels), f32),
            pltpu.VMEM((length, 2 * channels), bf16),
            pltpu.VMEM((WAVES, 2 * channels), bf16),
            pltpu.VMEM((WAVES, channels), bf16),
            pltpu.SemaphoreType.DMA((14,)),
        ],
        name="mix_bwd",
    )


def parts_order(strides):
    bits = len(strides)
    return [sum(((part >> (bits - 1 - i)) & 1) * s for i, s in enumerate(strides)) for part in range(1 << bits)]


def spread_columns(source, target, at, index, order):
    for part, step in enumerate(order):
        cols = pl.ds(pl.multiple_of((index ^ step) * CHUNK, CHUNK), CHUNK)
        target[at, part * CHUNK : (part + 1) * CHUNK] = source[:, cols]


def ffn_grad_kernel(orders, scal, *refs):
    feeds, lows = refs[0:4], refs[4:8]
    (up_a, up_b, hid_a, hid_b), outs, (left, right) = refs[8:12], refs[12:16], refs[16:18]
    block = feeds[0].shape[0]
    index = scal[3]
    for k, (source, (rhs_a, rhs_b)) in enumerate(((feeds, (up_a, up_b)), (lows, (hid_a, hid_b)))):
        right[: 2 * block, :] = rhs_a[...]
        right[2 * block :, :] = rhs_b[...]
        for i in range(4):
            spread_columns(source[i], left, slice(i * block, (i + 1) * block), index, orders[k])
        for half in range(2):
            out = outs[2 * k + half]
            wide = PARTS // 2 * CHUNK
            got = dot_rows(left[:, half * wide : (half + 1) * wide], right[...]).astype(bf16)
            for part in range(PARTS // 2):
                out[part] = got[part * CHUNK : (part + 1) * CHUNK, :]


def ffn_whole_kernel(*refs):
    feeds, lows = refs[0:4], refs[4:8]
    (up_a, up_b, hid_a, hid_b), out, (left, right) = refs[8:12], refs[12], refs[13:15]
    block = feeds[0].shape[0]
    for k, (source, (rhs_a, rhs_b)) in enumerate(((feeds, (up_a, up_b)), (lows, (hid_a, hid_b)))):
        right[: 2 * block, :] = rhs_a[...]
        right[2 * block :, :] = rhs_b[...]
        for i in range(4):
            left[i * block : (i + 1) * block, :] = source[i][...]
        for half in range(2):
            rows = slice(half * D // 2, (half + 1) * D // 2)
            out[k, rows, :] = dot_rows(left[:, rows], right[...]).astype(bf16)


def ffn_whole(run, feeds, lows, ups, hids):
    block, width = feeds[0].shape[0], ups[0].shape[1]
    return run(
        ffn_whole_kernel,
        [(a, None) for a in (*feeds, *lows, *ups, *hids)],
        [struct((2, D, width), bf16)],
        scratch=[pltpu.VMEM((4 * block, D), bf16), pltpu.VMEM((4 * block, width), bf16)],
        spill=1,
        name="ffn_whole",
    )[0]


def ffn_grad(run, orders, scal, feeds, lows, ups, hids):
    block, width = feeds[0].shape[0], ups[0].shape[1]
    out = struct((PARTS // 2, CHUNK, width), bf16)
    return run(
        functools.partial(ffn_grad_kernel, orders),
        [(scal, SMALL)] + [(a, None) for a in (*feeds, *lows, *ups, *hids)],
        [out] * 4,
        scratch=[pltpu.VMEM((4 * block, D), bf16), pltpu.VMEM((4 * block, width), bf16)],
        spill=4,
        name="ffn_grad",
    )


def join(target, a, b):
    rows = a.shape[0]
    target[:rows, :] = a[...]
    target[rows:, :] = b[...]


def mix_grad_kernel(orders, scal, *refs):
    normed, lows = refs[0:4], refs[4:8]
    in_low, mixed_a, mixed_b = refs[8:11]
    outs, (left, mixed) = refs[11:-2], refs[-2:]
    joined = len(outs) == 2
    channels = mixed.shape[1]
    join(mixed, mixed_a, mixed_b)
    core, index = scal[1], scal[3]
    groups = (
        (normed, in_low, slice(0, 2 * channels), 0, 0),
        (normed, in_low, slice(2 * channels, 3 * channels), 1, 0),
        (lows, mixed, slice(0, channels), 1, 1),
    )
    for source, rhs, cols, group, base in groups:
        own_a, own_b, got_a, got_b = source
        block = own_a.shape[0]
        for rows, at in halves(own_a, own_b, got_a, got_b, core):
            spread_columns(rows, left, pl.ds(at, block), index, orders[group])
        for half in range(2):
            out = outs[half if joined else 2 * group + half]
            first = base + 2 * group if joined else base
            wide = PARTS // 2 * CHUNK
            got = dot_rows(left[:, half * wide : (half + 1) * wide], rhs[:, cols]).astype(bf16)
            for part in range(PARTS // 2):
                for i in range(got.shape[1] // channels):
                    block_cols = slice(i * channels, (i + 1) * channels)
                    out[part, first + i] = got[part * CHUNK : (part + 1) * CHUNK, block_cols]


def mix_grad(run, orders, scal, normed, lows, in_low, mixed, joined):
    block, channels = normed[0].shape[0], mixed[0].shape[1]
    if joined:
        outs = [struct((PARTS // 2, 4, CHUNK, channels), bf16)] * 2
    else:
        outs = [struct((PARTS // 2, 2, CHUNK, channels), bf16)] * 4
    return run(
        functools.partial(mix_grad_kernel, orders),
        [(scal, SMALL)] + [(a, None) for a in (*normed, *lows, in_low, *mixed)],
        outs,
        scratch=[pltpu.VMEM((4 * block, D), bf16), pltpu.VMEM((4 * block, channels), bf16)],
        spill=len(outs),
        name="mix_grad",
    )


def halve_kernel(keep, got, sent, kept):
    count = keep.shape[0] // 2
    for i in range(count):
        kept[i] = (keep[i].astype(f32) + got[i].astype(f32)).astype(bf16)
        sent[i] = (keep[count + i].astype(f32) + got[count + i].astype(f32)).astype(bf16)


def halve(run, keep, got):
    out = struct((keep.shape[0] // 2, *keep.shape[1:]), bf16)
    return run(halve_kernel, [(keep, None), (got, None)], [out, out], spill=2, name="halve")


def total_of(refs, leads):
    return sum(ref[lead].astype(f32) for ref, lead in zip(refs, leads))


def finish_kernel(leads, turned, *refs):
    out, refs = refs[-1], list(refs[:-1])
    for layer, lead in enumerate(leads):
        total = total_of([refs.pop(0) for _ in lead], lead)
        out[layer] = total.T if turned else total


def ffn_finish(run, terms, turned):
    _, rows, cols = terms[0][0][0].shape
    shape = (cols, rows) if turned else (rows, cols)
    leads = [[lead for _, lead in pairs] for pairs in terms]
    return run(
        functools.partial(finish_kernel, leads, turned),
        [(a, None) for pairs in terms for a, _ in pairs],
        [struct((len(terms), *shape), f32)],
        name="ffn_finish",
    )[0]


def mix_finish_kernel(plan, *refs):
    into, out = refs[-2:]
    for layer, streams in enumerate(plan):
        for stream, parts in enumerate(streams):
            total = sum(refs[k][lead].astype(f32) for k, lead in parts)
            if stream < STREAMS:
                into[layer, stream] = total
            else:
                out[layer] = total.T


def mix_finish(run, arrays, plan):
    rows, channels = arrays[0].shape[-2:]
    return run(
        functools.partial(mix_finish_kernel, plan),
        [(a, None) for a in arrays],
        [struct((len(plan), STREAMS, rows, channels), f32), struct((len(plan), channels, rows), f32)],
        name="mix_finish",
    )


def pack_kernel(mix, filt, narrow, up_a, up_b, feed_a, feed_b, in_a, in_b, own, down, out):
    channels = mix.shape[1]
    out[:16, :] = mix[...]
    out[ROW_FILTER : ROW_FILTER + FILT, :] = filt[...]
    for q in range(D // channels):
        cols = slice(q * channels, (q + 1) * channels)
        out[ROW_UP_BIAS + q : ROW_UP_BIAS + q + 1, :] = up_a[:, cols] + up_b[:, cols]
        wide = [feed_a[i : i + 1, cols] + feed_b[i : i + 1, cols] for i in range(3)]
        wide.append(down[:, cols])
        wide += [in_a[i : i + 1, cols] + in_b[i : i + 1, cols] for i in range(2)]
        wide += [own[i : i + 1, cols] for i in range(2)]
        for i, value in enumerate(wide):
            at = ROW_WIDE + 4 * i + q
            out[at : at + 1, :] = value
    groups = [
        narrow[i * NARROW_GROUP : (i + 1) * NARROW_GROUP, :] for i in range(channels // FILT)
    ]
    out[ROW_NARROW:, :] = jnp.concatenate(groups, axis=1)


def pack(run, mix, filt, narrow, ups, feeds, ins, own, down):
    return run(
        pack_kernel,
        [(a, None) for a in (mix, filt, narrow, *ups, *feeds, *ins, own, down)],
        [struct((PACK_ROWS, mix.shape[1]), f32)],
        name="pack_small",
    )[0]


def gate(run, after=()):
    run(lambda: None, [], [], name="gate", after=after)


def stack_kernel(*refs):
    size = refs[0].shape[0]
    total, low = refs[-2:]
    for i, ref in enumerate(refs[:-2]):
        total[i * size : (i + 1) * size, :] = ref[...]
        low[i * size : (i + 1) * size, :] = ref[...].astype(bf16)


def stack_packs(run, packs):
    rows, cols = packs[0].shape
    shape = (len(packs) * rows, cols)
    return run(
        stack_kernel, [(a, None) for a in packs], [struct(shape, f32), struct(shape, bf16)], name="stack_packs"
    )


def add_small_kernel(value, got, total, low):
    added = value[...] + got[...].astype(f32)
    total[...] = added
    low[...] = added.astype(bf16)


def add_small(run, value, got):
    outs = [struct(value.shape, f32), struct(value.shape, bf16)]
    return run(add_small_kernel, [(value, None), (got, None)], outs, name="add_small")


def last_small_kernel(value, got, total, wide):
    added = value[...] + got[...].astype(f32)
    total[...] = added
    size = PACK_ROWS - ROW_WIDE
    for i in range(value.shape[0] // PACK_ROWS):
        wide[i * size : (i + 1) * size, :] = added[i * PACK_ROWS + ROW_WIDE : (i + 1) * PACK_ROWS, :]


def last_small(run, value, got):
    rows, cols = value.shape
    wide = struct((rows // PACK_ROWS * (PACK_ROWS - ROW_WIDE), cols), f32)
    return run(
        last_small_kernel, [(value, None), (got, None)], [struct(value.shape, f32), wide], name="last_small"
    )


def sum_kernel(a, b, out):
    out[...] = a[...] + b[...]


def add_pair(run, a, b):
    return run(sum_kernel, [(a, None), (b, None)], [struct(a.shape, f32)], name="add_pair")[0]


def unpack_kernel(layers, *refs):
    (chans, wides), outs = refs[:2], refs[2:]
    (gain, shift, out_bias, feed_gain, feed_shift, down_bias, in_bias, conv_w, conv_b, skip, filt, up_bias,
     w_in, b_in, f_in, w_mid, b_mid, f_mid) = outs
    channels = chans.shape[1]
    size = PACK_ROWS - ROW_WIDE
    for layer in range(layers):
        chan = chans[layer * PACK_ROWS : (layer + 1) * PACK_ROWS, :]
        wide = wides[layer * size : (layer + 1) * size, :]
        row = slice(layer, layer + 1)

        def spread(target, ref, at, row=row):
            for q in range(D // channels):
                target[row, q * channels : (q + 1) * channels] = ref[at + q : at + q + 1, :]

        spread(feed_gain, wide, 0)
        spread(feed_shift, wide, 4)
        spread(out_bias, wide, 8)
        spread(down_bias, wide, 12)
        if layer + 1 < layers:
            spread(gain, wide, 16, slice(layer + 1, layer + 2))
            spread(shift, wide, 20, slice(layer + 1, layer + 2))
        if layer == 0:
            spread(gain, wide, 24)
            spread(shift, wide, 28)
        spread(up_bias, chan, ROW_UP_BIAS)
        for stream in range(STREAMS):
            in_bias[stream, row, :] = chan[ROW_IN_BIAS + stream : ROW_IN_BIAS + stream + 1, :]
            conv_b[stream, row, :] = chan[ROW_CONV_B + stream : ROW_CONV_B + stream + 1, :]
            for lag in range(SHORT):
                at = ROW_CONV_W + stream * SHORT + lag
                conv_w[stream, lag, row, :] = chan[at : at + 1, :]
        skip[row, :] = chan[ROW_SKIP : ROW_SKIP + 1, :]
        filt[layer] = chan[ROW_FILTER : ROW_FILTER + FILT, :]
        base = ROW_NARROW - ROW_WIDE
        rows = slice(base, base + NARROW_GROUP)
        narrow = jnp.concatenate(
            [wide[rows, i * FILT : (i + 1) * FILT] for i in range(channels // FILT)], axis=0
        )
        for target, at in ((b_in, NB_IN), (f_in, NF_IN), (b_mid, NB_MID), (f_mid, NF_MID)):
            target[row, :] = narrow[at : at + 1, :]
        w_in[layer] = narrow[:POS, :]
        w_mid[layer] = narrow[NW_MID : NW_MID + FILT, :]


def unpack(run, chans, wides, up_width):
    layers, channels = chans.shape[0] // PACK_ROWS, chans.shape[1]
    return run(
        functools.partial(unpack_kernel, layers),
        [(chans, None), (wides, None)],
        [struct((layers, D), f32)] * 6
        + [
            struct((STREAMS, layers, channels), f32),
            struct((STREAMS, SHORT, layers, channels), f32),
            struct((STREAMS, layers, channels), f32),
            struct((layers, channels), f32),
            struct((layers, FILT, channels), f32),
            struct((layers, up_width), f32),
            struct((layers, POS, FILT), f32),
            struct((layers, FILT), f32),
            struct((layers, FILT), f32),
            struct((layers, FILT, FILT), f32),
            struct((layers, FILT), f32),
            struct((layers, FILT), f32),
        ],
        name="unpack_small",
    )


def dp_swap(x, stride):
    size = lax.axis_size("dp")
    return lax.ppermute(x, "dp", [(i, i ^ stride) for i in range(size)])


class Scatter:
    def __init__(self, run, sent, keep, strides):
        self.run, self.keep = run, keep
        self.strides = list(strides)
        self.got = dp_swap(sent, self.strides.pop(0))

    def step(self):
        sent, self.keep = halve(self.run, self.keep, self.got)
        self.got = dp_swap(sent, self.strides.pop(0))

    def pair(self):
        while self.strides:
            self.step()
        return self.keep, self.got


class SmallSum:
    def __init__(self, run, packs, strides):
        self.run, self.strides = run, list(strides)
        self.value, low = stack_packs(run, packs)
        self.got = dp_swap(low, self.strides.pop(0))

    def step(self):
        self.value, low = add_small(self.run, self.value, self.got)
        self.got = dp_swap(low, self.strides.pop(0))

    def sums(self):
        return last_small(self.run, self.value, self.got)


def share_out(pair):
    keep, got = pair
    total = (keep[0].astype(f32) + got[0].astype(f32)).reshape(-1, CHUNK, keep.shape[-1])
    left = lax.axis_size("dp") // PARTS
    index = lax.axis_index("dp")
    stride = 1
    total = total.reshape(total.shape[0], left, CHUNK // left, -1)
    while left > 1:
        total = total.reshape(total.shape[0], left // 2, 2, total.shape[2], -1)
        bit = (index // stride) % 2
        mine = lax.dynamic_index_in_dim(total, bit, 2, keepdims=False)
        other = lax.dynamic_index_in_dim(total, 1 - bit, 2, keepdims=False)
        total = mine + dp_swap(other.astype(bf16), stride).astype(f32)
        left, stride = left // 2, stride * 2
    return total[:, 0]


def shards(
    tokens,
    seg_lengths,
    cotangent,
    mixer_norm_gain,
    mixer_norm_bias,
    in_weight,
    in_bias,
    conv_weight,
    conv_bias,
    filter_in,
    filter_in_bias,
    filter_in_freq,
    filter_mid,
    filter_mid_bias,
    filter_mid_freq,
    filter_out,
    skip_bias,
    out_weight,
    out_bias,
    feed_norm_gain,
    feed_norm_bias,
    feed_up,
    feed_up_bias,
    feed_down,
    feed_down_bias,
):
    block = tokens.shape[1]
    length = block * lax.axis_size("mp")
    channels = in_weight.shape[3]
    layers = in_weight.shape[0]
    spot = lax.axis_index("mp").astype(jnp.int32)
    left = lax.axis_size("dp") // PARTS
    chunk = (lax.axis_index("dp") // left).astype(jnp.int32)
    scal = jnp.stack([seg_lengths[0, 0], spot % 2, spot // 2, chunk, spot])
    table = wave_table(length)
    waves = jnp.asarray(table)
    waves_t = jnp.asarray(np.ascontiguousarray(table.T))
    pos = jnp.asarray(position_table(length))
    run = Chain()

    in_w = in_weight.transpose(0, 2, 1, 3)
    in_b = in_bias.transpose(1, 0, 2)
    conv_w = conv_weight.transpose(1, 2, 0, 3)
    conv_b = conv_bias.transpose(1, 0, 2)
    filter_weights = (
        filter_in, filter_in_bias, filter_in_freq, filter_mid, filter_mid_bias, filter_mid_freq, filter_out
    )
    both = range(2)

    def start_sum(ends):
        got = [core_swap(ends[i]) for i in both]
        out = []
        for i in both:
            here = add_low(run, ends[2 + i], got[i])
            out.append((here, chip_swap(here)))
        return out

    def one_sum(sent, keep):
        here = add_low(run, keep, core_swap(sent))
        return here, chip_swap(here)

    def in_turn(first, pace=None):
        gate(run, [first[1]])
        if pace is None:
            gate(run)
        else:
            pace.step()

    mine = tokens[0]
    other = chip_swap(mine)
    filt = [None] * layers
    early = tuple(stay(a) for a in filter_weights)
    filt[0] = filter_fwd(run, 0, length, scal, stay(pos), early, stay(waves))
    low_a, low_b, res_a, res_b, cot = first_norm(
        run, scal, stay(mine), other, stay(mixer_norm_gain), stay(mixer_norm_bias), stay(cotangent[0])
    )
    res, low = [res_a, res_b], [low_a, low_b]

    def in_halves(prepare, work, sums):
        out = []
        for i in both:
            prepare(i)
            sent, keep = work(i)
            if i == 0 and sums is not None:
                in_turn(sums[1])
            if i == 1:
                in_turn(out[0])
            out.append(one_sum(sent, keep))
        return out

    stored, cot_parts = [], []
    back = [None, None]
    got = [core_swap(x) for x in low]
    cot_other = chip_swap(cot)
    sums = None
    for layer in range(layers):
        last = layer + 1 == layers
        saved, passed, middle, feed, feed_got, ffn = [], [None], [], [], [], []
        if layer:
            res, low, got = [], [], []

        def mix_prepare(i):
            if layer:
                b, a = add_norm(
                    run, layer - 1, layer, *sums[i], stored[layer - 1][5][i],
                    feed_down_bias, mixer_norm_gain, mixer_norm_bias, 1,
                )
                res.append(a)
                low.append(b)
                got.append(core_swap(b))

        def mix_work(i):
            kept, on, sent, keep = mix_fwd(
                run, layer, i, scal, low[i], got[i], in_w, in_b, conv_w, conv_b, skip_bias, filt[layer][0],
                out_weight, waves, waves_t, passed[-1],
            )
            saved.append(kept)
            passed.append(on)
            if layer == 0 and i == 0:
                cot_parts.extend(first_grad(run, scal, cot, cot_other))
            if layer == 0 and i == 1:
                for other_layer in range(1, layers):
                    filt[other_layer] = filter_fwd(
                        run, other_layer, length, scal, pos, filter_weights, waves
                    )
            return sent, keep

        def feed_prepare(i):
            b, a = add_norm(run, layer, layer, *sums[i], res[i], out_bias, feed_norm_gain, feed_norm_bias)
            middle.append(a)
            feed.append(b)
            feed_got.append(core_swap(b))

        def feed_work(i):
            ffn.append(ffn_fwd(run, layer, feed[i], feed_got[i], feed_up, feed_up_bias, feed_down))
            if not last:
                return ffn[i][2], ffn[i][3]
            back[i] = ffn_bwd(run, layer, cot_low[i], cot_got[i], feed_up, feed_down, ffn[i][0], True)
            return back[i][2], back[i][3]

        sums = in_halves(mix_prepare, mix_work, sums)
        if layer == 0:
            cot_sum, *cot_low = cot_parts
            cot_got = [core_swap(x) for x in cot_low]
        stored.append(
            (res, (*low, *got), saved, passed[2][1], [kept[2] for kept in saved], middle, feed, feed_got, ffn)
        )
        sums = in_halves(feed_prepare, feed_work, sums)
    back_sums = sums

    rising, turned = (1, 2, 4), (2, 4, 1)
    feed_orders, mix_orders = (rising, turned), (rising, rising)

    def scatter_pair(sends, orders):
        return [
            Scatter(run, sends[2 * k + 1], sends[2 * k], [left * o for o in orders[k]]) for k in range(2)
        ]

    def scatter_rows(whole_grad):
        return lax.psum_scatter(whole_grad, "dp", scatter_dimension=1, tiled=True)

    def grad_args(layer, low, got, back):
        feed, feed_got, ffn = stored[layer][6:]
        return (
            (feed[0], feed_got[0], feed[1], feed_got[1]),
            (low[0], got[0], low[1], got[1]),
            [back[i][1] for i in both],
            [ffn[i][1] for i in both],
        )

    grad, low, got = cot_low, cot_low, cot_got
    down_sum = cot_sum
    moves = back_sums
    feed_shares, mix_rest, packs = ([None] * layers for _ in range(3))
    no_sums = jnp.zeros((8, D), f32)
    in_sums = [no_sums, no_sums]
    for layer in reversed(range(layers)):
        above = layer + 1
        entry, normed, saved, spec, mixed, middle, feed, feed_got, ffn = stored[layer]
        if layer:
            feed_whole = ffn_whole(run, *grad_args(layer, low, got, back))
        else:
            feed_sends = ffn_grad(
                run, [parts_order(o) for o in feed_orders], scal, *grad_args(layer, low, got, back)
            )
        if above == layers:
            out_got = [core_swap(ffn[i][2]) for i in both]
            out_send, out_mine = pick_outputs(
                run, layer, scal, [ffn[i][3] for i in both], out_got, middle, feed_down_bias
            )
        new_grad, low, feed_sums = [], [], []
        for i in both:
            a, c, b = norm_back(run, layer, *moves[i], middle[i], grad[i], feed_norm_gain, 1)
            new_grad.append(a)
            low.append(b)
            feed_sums.append(c)
        grad = new_grad
        got = [core_swap(x) for x in low]
        rows = (*low, *got)
        if layer:
            feed_shares[layer] = scatter_rows(run.release([feed_whole])[0])
        else:
            feed_sends[1], feed_sends[3] = run.release([feed_sends[1], feed_sends[3]])
            up_big, down_big = scatter_pair(feed_sends, feed_orders)
        in_low, taps_grad, mix_sums, *ends = mix_bwd(
            run, layer, scal, rows, out_weight, saved, spec, in_w, conv_w, conv_b, skip_bias,
            filt[layer][0], waves, waves_t,
        )
        if layer:
            if above == layers:
                outputs = last_add(run, out_mine, chip_swap(out_send))
            moves = start_sum(ends)
            own_sums = no_sums
            mix_keep, mix_sent = mix_grad(
                run, [parts_order(rising)] * 2, scal, normed, rows, in_low, mixed, True
            )
        else:
            for x in mix_rest[1:]:
                x.step()
            up_big.step()
            swapped = [core_swap(ends[i]) for i in both]
        filt_out, narrow = filter_bwd(run, layer, length, scal, taps_grad, pos, filter_weights, filt[layer][1])
        if layer == 0:
            send, own, own_sums = last_pick(run, scal, ends[2:], swapped, entry)
            there = chip_swap(send)
            down_big.step()
        packs[layer] = pack(
            run, mix_sums, filt_out, narrow, [back[i][0] for i in both], feed_sums, in_sums, own_sums, down_sum
        )
        if layer == 0:
            small = SmallSum(
                run, packs, [1 << i for i in range(left.bit_length() - 1)] + [left * o for o in rising]
            )
            sends = mix_grad(
                run, [parts_order(o) for o in mix_orders], scal, normed, rows, in_low, mixed, False
            )
            small.step()
            sends[1], sends[3] = run.release([sends[1], sends[3]])
            mix_bigs = scatter_pair(sends, mix_orders)
            up_big.step()
            for x in mix_rest[1:]:
                x.step()
            break
        new_grad, new_low, in_sums, new_got, new_back, back_sums = [], [], [], [], [], []

        def norm_half(i):
            a, c, b = norm_back(run, layer, *moves[i], entry[i], grad[i], mixer_norm_gain)
            new_grad.append(a)
            new_low.append(b)
            in_sums.append(c)
            new_got.append(core_swap(b))

        def ffn_half(i):
            below = stored[layer - 1][8]
            new_back.append(
                ffn_bwd(run, layer - 1, new_low[i], new_got[i], feed_up, feed_down, below[i][0], False)
            )

        def sum_half(i):
            back_sums.append(one_sum(new_back[i][2], new_back[i][3]))

        norm_half(0)
        mix_rest[layer] = Scatter(run, run.release([mix_sent])[0], mix_keep, [left * o for o in rising])
        ffn_half(0)
        in_turn(moves[1])
        sum_half(0)
        norm_half(1)
        ffn_half(1)
        in_turn(back_sums[0])
        sum_half(1)
        moves = back_sums
        back = new_back
        down_sum = (in_sums[0] + in_sums[1])[2:3]
        grad, low, got = new_grad, new_low, new_got
    token_grad = last_back(run, 0, scal, own, there, entry, grad, mixer_norm_gain)
    while small.strides:
        small.step()
    down_big.step()
    mix_bigs[0].step()
    small_sums, wide = small.sums()
    wide_got = chip_swap(wide)
    mix_bigs[1].step()
    wide = add_pair(run, wide, wide_got)
    wide_got = core_swap(wide)
    mix_bigs[0].step()
    mix_bigs[1].step()
    (gain, shift, out_bias_g, feed_gain, feed_shift, down_bias_g, in_bias_g, conv_w_g, conv_b_g, skip_g, filt_g,
     up_bias_g, w_in_g, b_in_g, f_in_g, w_mid_g, b_mid_g, f_mid_g) = unpack(
        run, small_sums, add_pair(run, wide, wide_got), feed_up.shape[2]
    )
    up_pair, down_pair = up_big.pair(), down_big.pair()
    if left == 1:
        up_first, down_first = [[(a, 0) for a in pair] for pair in (up_pair, down_pair)]
    else:
        up_first, down_first = [[(share_out(pair), 0)] for pair in (up_pair, down_pair)]
    up_g = ffn_finish(run, [up_first] + [[(a, 0)] for a in feed_shares[1:]], False)
    down_g = ffn_finish(run, [down_first] + [[(a, 1)] for a in feed_shares[1:]], True)
    mix_pairs = [x.pair() for x in mix_bigs]
    if left == 1:
        arrays = [a for pair in mix_pairs for a in pair]
        first = [[(2 * k, (0, i)), (2 * k + 1, (0, i))] for k in both for i in both]
    else:
        arrays = [share_out(pair) for pair in mix_pairs]
        first = [[(k, i)] for k in both for i in both]
    plan = [first]
    for x in mix_rest[1:]:
        pair = x.pair()
        if left == 1:
            plan.append([[(len(arrays), (0, i)), (len(arrays) + 1, (0, i))] for i in range(STREAMS + 1)])
            arrays += pair
        else:
            plan.append([[(len(arrays), i)] for i in range(STREAMS + 1)])
            arrays.append(share_out(pair))
    in_g, out_g = mix_finish(run, arrays, plan)
    return (
        outputs[None],
        token_grad[None],
        gain,
        shift,
        in_g.transpose(0, 2, 1, 3),
        in_bias_g.transpose(1, 0, 2),
        conv_w_g.transpose(2, 0, 1, 3),
        conv_b_g.transpose(1, 0, 2),
        w_in_g,
        b_in_g,
        f_in_g,
        w_mid_g,
        b_mid_g,
        f_mid_g,
        filt_g,
        skip_g,
        out_g,
        out_bias_g,
        feed_gain,
        feed_shift,
        up_g,
        up_bias_g,
        down_g,
        down_bias_g,
    )


def solution(mesh):
    in_specs = (
        P("dp", "mp", None),
        P("dp", None),
        P("dp", "mp", None),
        P(),
        P(),
        P(None, None, None, "mp"),
        P(None, None, "mp"),
        P(None, None, None, "mp"),
        P(None, None, "mp"),
        P(),
        P(),
        P(),
        P(),
        P(),
        P(),
        P(None, None, "mp"),
        P(None, "mp"),
        P(None, "mp", None),
        P(),
        P(),
        P(),
        P(None, None, "mp"),
        P(None, "mp"),
        P(None, "mp", None),
        P(),
    )
    out_specs = (
        P("dp", "mp", None),
        P("dp", "mp", None),
        P(),
        P(),
        P(None, "dp", None, "mp"),
        P(None, None, "mp"),
        P(None, None, None, "mp"),
        P(None, None, "mp"),
        P(),
        P(),
        P(),
        P(),
        P(),
        P(),
        P(None, None, "mp"),
        P(None, "mp"),
        P(None, "mp", "dp"),
        P(),
        P(),
        P(),
        P(None, "dp", "mp"),
        P(None, "mp"),
        P(None, "mp", "dp"),
        P(),
    )
    return jax.shard_map(shards, mesh=mesh, in_specs=in_specs, out_specs=out_specs, check_vma=False)
```

```python
import functools
import math

import jax
import jax.numpy as jnp
import ml_dtypes
import numpy as np
from jax import lax
from jax.experimental import pallas as pl
from jax.experimental.pallas import tpu as pltpu
from jax.sharding import PartitionSpec as P

D = 1024
POS = 33
FILT = 64
REACH = 896
WAVES = 2 * REACH
SHORT = 3
STREAMS = 3
TILE = 128
CHUNK = 128
PARTS = D // CHUNK

f32 = jnp.float32
bf16 = jnp.bfloat16
highest = lax.Precision.HIGHEST
norm_eps = 1e-05
slow_rate = math.log(100.0) / 1.5
fast_rate = math.log(100.0) / 0.3
GELU_A = math.sqrt(2.0 / math.pi)
GELU_B = 0.044715
SPARE_MB = 3

ROW_IN_BIAS = 0
ROW_CONV_W = 3
ROW_CONV_B = 12
ROW_SKIP = 15
ROW_FILTER = 16
ROW_UP_BIAS = 80
ROW_WIDE = 84
ROW_NARROW = 116
PACK_ROWS = 144
NARROW_ROWS = 112
NARROW_GROUP = 28
NB_IN, NF_IN, NW_MID, NB_MID, NF_MID = 33, 34, 35, 99, 100


def wave_table(length):
    freq = 2 * np.arange(REACH, dtype=np.int64) + 1
    phase = (freq[:, None] * np.arange(length, dtype=np.int64)[None, :]) % (2 * WAVES)
    angle = phase.astype(np.float64) * (math.pi / WAVES)
    return np.concatenate([np.cos(angle), -np.sin(angle)], axis=0).astype(ml_dtypes.bfloat16)


def position_table(length):
    places = np.arange(REACH, dtype=np.float64)
    count = (POS - 1) // 2
    bands = 0.0001 + np.arange(count, dtype=np.float64) * ((count - 1 - 0.0001) / (count - 1))
    phases = bands[:, None] * places[None, :] * (2.0 * math.pi / length)
    table = np.zeros((64, REACH), np.float32)
    table[0] = places / (length - 1)
    table[1 : 1 + count] = np.cos(phases)
    table[1 + count : POS] = -np.sin(phases)
    return table


def core_swap(x):
    size = lax.axis_size("mp")
    return lax.ppermute(x, "mp", [(i, i ^ 1) for i in range(size)])


def chip_swap(x):
    size = lax.axis_size("mp")
    return lax.ppermute(x, "mp", [(i, i ^ 2) for i in range(size)])


def dot(a, b):
    return jnp.dot(a, b, preferred_element_type=f32)


def dot_rows(a, b):
    return lax.dot_general(a, b, (((0,), (0,)), ((), ())), preferred_element_type=f32)


def dot_cols(a, b):
    return lax.dot_general(a, b, (((1,), (1,)), ((), ())), preferred_element_type=f32)


def fine(a, b, dims):
    return lax.dot_general(a, b, (dims, ((), ())), precision=highest, preferred_element_type=f32)


def whole(shape):
    return pl.BlockSpec(tuple(shape), lambda *_: (0,) * len(shape))


def layer_of(stacked, layer):
    shape = stacked.shape[1:]
    return pl.BlockSpec((None, *shape), lambda *_: (layer,) + (0,) * len(shape))


SMALL = pl.BlockSpec(memory_space=pltpu.SMEM)
FAR = pl.BlockSpec(memory_space=pl.ANY)
MAIN = pl.BlockSpec(memory_space=pltpu.HBM)


def struct(shape, dtype):
    return jax.ShapeDtypeStruct(tuple(shape), dtype)


class Chain:
    def __init__(self):
        self.token = None

    def release(self, arrays):
        *results, self.token = pl.pallas_call(
            lambda *refs: None,
            grid=(1,),
            out_shape=[pltpu.HBM(a.shape, a.dtype) for a in arrays] + [pltpu.HBM((8, 128), f32)],
            in_specs=[FAR] * (len(arrays) + 1),
            out_specs=[MAIN] * (len(arrays) + 1),
            input_output_aliases={i: i for i in range(len(arrays))},
            cost_estimate=pl.CostEstimate(flops=1, bytes_accessed=1, transcendentals=0),
            name="release",
        )(*[stay(a) for a in arrays], stay(self.token))
        return results

    def __call__(self, kernel, operands, outs, scratch=(), far=0, spill=0, name=None, after=()):
        arrays = [a for a, _ in operands]
        specs = [whole(a.shape) if s is None else s for a, s in operands]
        main = far + spill
        out_specs = [MAIN if i < main else whole(o.shape) for i, o in enumerate(outs)]
        spilled = [pltpu.VMEM(o.shape, o.dtype) for o in outs[far:main]]
        scratch = [*scratch, *spilled] + ([pltpu.SemaphoreType.DMA((spill,))] if spill else [])
        held = 0
        for a, s in list(zip(arrays, specs)) + list(zip(outs, out_specs)):
            if s is not SMALL and s is not FAR and s is not MAIN:
                held += math.prod(x for x in s.block_shape if x is not None) * a.dtype.itemsize
        for s in scratch:
            if getattr(s, "memory_space", None) == pltpu.VMEM:
                held += math.prod(s.shape) * jnp.dtype(s.dtype).itemsize
        count, given = len(arrays), len(outs)
        tokens = ([] if self.token is None else [stay(self.token)]) + list(after)

        def body(*refs):
            ins, refs = refs[:count], refs[count + len(tokens) :]
            results, rest = refs[:given], refs[given + 1 :]
            if spill:
                rest, buffers, sems = rest[: -spill - 1], rest[-spill - 1 : -1], rest[-1]
                kernel(*ins, *results[:far], *buffers, *results[main:], *rest)
                copies = [
                    pltpu.make_async_copy(buffers[i], results[far + i], sems.at[i]) for i in range(spill)
                ]
                for copy in copies:
                    copy.start()
                for copy in copies:
                    copy.wait()
            else:
                kernel(*ins, *results, *rest)

        *results, self.token = pl.pallas_call(
            body,
            grid=(1,),
            out_shape=[pltpu.HBM(o.shape, o.dtype) if i < main else o for i, o in enumerate(outs)]
            + [pltpu.HBM((8, 128), f32)],
            in_specs=specs + [FAR] * len(tokens),
            out_specs=out_specs + [MAIN],
            scratch_shapes=scratch,
            compiler_params=pltpu.CompilerParams(vmem_limit_bytes=held + SPARE_MB * 1024 * 1024),
            cost_estimate=pl.CostEstimate(flops=1, bytes_accessed=1, transcendentals=0),
            name=name,
        )(*arrays, *tokens)
        return results


def unit_of(values):
    center = values - jnp.mean(values, axis=-1, keepdims=True)
    spread = jnp.mean(center * center, axis=-1, keepdims=True)
    rstd = lax.rsqrt(spread + norm_eps)
    return center * rstd, rstd


def row_tiles(count, size=32):
    return [slice(i * size, (i + 1) * size) for i in range(count // size)]


def stay(x):
    return pltpu.with_memory_space_constraint(x, pltpu.HBM)


def first_norm_kernel(scal, mine, other, gain, shift, cot, low_a, low_b, res_a, res_b, cot_out):
    chip = scal[2]
    cot_out[...] = cot[...]
    for rows in row_tiles(mine.shape[0]):
        a, b = mine[rows, :].astype(f32), other[rows, :].astype(f32)
        for values, res, low in (
            (jnp.where(chip == 0, a, b), res_a, low_a),
            (jnp.where(chip == 0, b, a), res_b, low_b),
        ):
            res[rows, :] = values
            unit, _ = unit_of(values)
            low[rows, :] = (unit * gain[0:1, :] + shift[0:1, :]).astype(bf16)


def first_norm(run, scal, mine, other, gain, shift, cot):
    block = mine.shape[0]
    return run(
        first_norm_kernel,
        [(scal, SMALL)] + [(a, None) for a in (mine, other, gain, shift, cot)],
        [struct((block, D), bf16)] * 2 + [struct((block, D), f32)] * 2 + [struct((block, D), bf16)],
        spill=2,
        name="first_norm",
    )


def first_grad_kernel(scal, mine, other, sums, low_a, low_b):
    chip = scal[2]
    total = jnp.zeros((8, D), f32)
    for rows in row_tiles(mine.shape[0]):
        a, b = mine[rows, :], other[rows, :]
        low_a[rows, :] = jnp.where(chip == 0, a, b)
        low_b[rows, :] = jnp.where(chip == 0, b, a)
        total = total + fold(a.astype(f32)) + fold(b.astype(f32))
    sums[...] = 0.5 * jnp.sum(total, axis=0, keepdims=True)


def first_grad(run, scal, mine, other):
    block = mine.shape[0]
    return run(
        first_grad_kernel,
        [(scal, SMALL), (mine, None), (other, None)],
        [struct((1, D), f32)] + [struct((block, D), bf16)] * 2,
        spill=1,
        name="first_grad",
    )


def add_kernel(keep, got, out):
    for rows in row_tiles(keep.shape[0], 64):
        out[rows, :] = (keep[rows, :] + got[rows, :].astype(f32)).astype(out.dtype)


def add_low(run, keep, got, after=()):
    out = [struct(keep.shape, bf16)]
    return run(add_kernel, [(keep, None), (got, None)], out, name="add_low", after=after)[0]


def last_pick_kernel(scal, keep_a, got_a, val_a, keep_b, got_b, val_b, send, mine, sums):
    totals = [jnp.zeros((8, D), f32) for _ in range(2)]
    near_a = scal[2] == 0
    for rows in row_tiles(mine.shape[0]):
        parts = []
        for keep, got, values in ((keep_a, got_a, val_a), (keep_b, got_b, val_b)):
            total = keep[rows, :] + got[rows, :].astype(f32)
            unit, _ = unit_of(values[rows, :])
            totals[0] = totals[0] + fold(total * unit)
            totals[1] = totals[1] + fold(total)
            parts.append(total)
        mine[rows, :] = jnp.where(near_a, parts[0], parts[1])
        send[rows, :] = jnp.where(near_a, parts[1], parts[0]).astype(bf16)
    for i, total in enumerate(totals):
        sums[i : i + 1, :] = jnp.sum(total, axis=0, keepdims=True)
    sums[2:8, :] = jnp.zeros((6, D), f32)


def last_pick(run, scal, keeps, gots, entry):
    shape = keeps[0].shape
    operands = [a for i in range(2) for a in (keeps[i], gots[i], entry[i])]
    return run(
        last_pick_kernel,
        [(scal, SMALL)] + [(a, None) for a in operands],
        [struct(shape, bf16), struct(shape, f32), struct((8, D), f32)],
        name="last_pick",
    )


def add_norm_kernel(layer, norm_layer, here, there, residual, bias, gain, shift, low, out):
    for rows in row_tiles(here.shape[0]):
        values = residual[rows, :] + here[rows, :].astype(f32) + there[rows, :].astype(f32)
        values = values + bias[layer : layer + 1, :]
        out[rows, :] = values
        unit, _ = unit_of(values)
        low[rows, :] = (
            unit * gain[norm_layer : norm_layer + 1, :] + shift[norm_layer : norm_layer + 1, :]
        ).astype(bf16)


def add_norm(run, layer, norm_layer, here, there, residual, bias, gain, shift, spill=0):
    shape = here.shape
    return run(
        functools.partial(add_norm_kernel, layer, norm_layer),
        [(a, None) for a in (here, there, residual, bias, gain, shift)],
        [struct(shape, bf16), struct(shape, f32)],
        spill=spill,
        name="add_norm",
    )


def pick_kernel(layer, scal, keep_a, got_a, keep_b, got_b, mid_a, mid_b, bias, send, mine):
    def pick(near, far_away):
        keep, got, middle = near
        for rows in row_tiles(mine.shape[0]):
            values = keep[rows, :] + got[rows, :].astype(f32) + middle[rows, :]
            mine[rows, :] = values + bias[layer : layer + 1, :]
            send[rows, :] = (far_away[0][rows, :] + far_away[1][rows, :].astype(f32)).astype(bf16)

    @pl.when(scal[2] == 0)
    def _():
        pick((keep_a, got_a, mid_a), (keep_b, got_b))

    @pl.when(scal[2] != 0)
    def _():
        pick((keep_b, got_b, mid_b), (keep_a, got_a))


def pick_outputs(run, layer, scal, keeps, gots, middles, bias):
    shape = keeps[0].shape
    operands = (keeps[0], gots[0], keeps[1], gots[1], *middles, bias)
    return run(
        functools.partial(pick_kernel, layer),
        [(scal, SMALL)] + [(a, None) for a in operands],
        [struct(shape, bf16), struct(shape, f32)],
        name="pick_outputs",
    )


def last_add_kernel(mine, there, out):
    for rows in row_tiles(out.shape[0], 64):
        out[rows, :] = mine[rows, :] + there[rows, :].astype(f32)


def last_add(run, mine, there):
    return run(last_add_kernel, [(mine, None), (there, None)], [struct(mine.shape, f32)], name="last_add")[0]


def fold(x):
    return sum(x[8 * i : 8 * i + 8, :] for i in range(x.shape[0] // 8))


def norm_back_kernel(layer, here, there, values, grad, gain, out, sums, low):
    totals = [jnp.zeros((8, D), f32) for _ in range(3)]
    for rows in row_tiles(here.shape[0], 16):
        dy = here[rows, :].astype(f32) + there[rows, :].astype(f32)
        unit, rstd = unit_of(values[rows, :])
        scaled = dy * gain[layer : layer + 1, :]
        into = rstd * (
            scaled
            - jnp.mean(scaled, axis=-1, keepdims=True)
            - unit * jnp.mean(scaled * unit, axis=-1, keepdims=True)
        )
        new = grad[rows, :].astype(f32) + into
        out[rows, :] = new
        low[rows, :] = new.astype(bf16)
        for k, part in enumerate((dy * unit, dy, new)):
            totals[k] = totals[k] + fold(part)
    for k, total in enumerate(totals):
        sums[k : k + 1, :] = 0.5 * jnp.sum(total, axis=0, keepdims=True)
    sums[3:8, :] = jnp.zeros((5, D), f32)


def norm_back(run, layer, here, there, values, grad, gain, spill=0):
    shape = here.shape
    return run(
        functools.partial(norm_back_kernel, layer),
        [(a, None) for a in (here, there, values, grad, gain)],
        [struct(shape, f32), struct((8, D), f32), struct(shape, bf16)],
        spill=2 + spill,
        name="norm_back",
    )


def last_back_kernel(layer, scal, mine, there, val_a, val_b, grad_a, grad_b, gain, out):
    near_a = scal[2] == 0
    for rows in row_tiles(out.shape[0], 16):
        dy = mine[rows, :] + there[rows, :].astype(f32)
        unit, rstd = unit_of(jnp.where(near_a, val_a[rows, :], val_b[rows, :]))
        scaled = dy * gain[layer : layer + 1, :]
        into = rstd * (
            scaled
            - jnp.mean(scaled, axis=-1, keepdims=True)
            - unit * jnp.mean(scaled * unit, axis=-1, keepdims=True)
        )
        out[rows, :] = jnp.where(near_a, grad_a[rows, :], grad_b[rows, :]) + into


def last_back(run, layer, scal, mine, there, entry, grad, gain):
    return run(
        functools.partial(last_back_kernel, layer),
        [(scal, SMALL), (mine, None), (there, None)]
        + [(a, None) for a in (*entry, *grad, gain)],
        [struct(mine.shape, f32)],
        name="last_back",
    )[0]


def ffn_fwd_kernel(
    layer, own, got, up_far, up_bias, down_far, pre_far, hid_far, sent, keep, both, pre, hid, up, down, sems
):
    copy_up = pltpu.make_async_copy(up_far.at[layer], up, sems.at[2])
    copy_down = pltpu.make_async_copy(down_far.at[layer], down, sems.at[3])
    copy_up.start()
    copy_down.start()
    half = own.shape[0]
    both[:half, :] = own[...]
    both[half:, :] = got[...]
    copy_up.wait()
    v = dot(both[...], up[...]) + up_bias[layer : layer + 1, :]
    pre[...] = v.astype(bf16)
    hid[...] = (0.5 * v * (1.0 + jnp.tanh(GELU_A * (v + GELU_B * v * v * v)))).astype(bf16)
    copies = [
        pltpu.make_async_copy(a, b, sems.at[i]) for i, (a, b) in enumerate(((pre, pre_far), (hid, hid_far)))
    ]
    for copy in copies:
        copy.start()
    copy_down.wait()
    total = dot(hid[...], down[...])
    keep[...] = total[:half, :]
    sent[...] = total[half:, :].astype(bf16)
    for copy in copies:
        copy.wait()


def ffn_fwd(run, layer, own, got, up, up_bias, down):
    half, width = own.shape[0], up.shape[2]
    return run(
        functools.partial(ffn_fwd_kernel, layer),
        [(own, None), (got, None), (up, FAR), (up_bias, None), (down, FAR)],
        [
            struct((2 * half, width), bf16),
            struct((2 * half, width), bf16),
            struct((half, D), bf16),
            struct((half, D), f32),
        ],
        scratch=[
            pltpu.VMEM((2 * half, D), bf16),
            pltpu.VMEM((2 * half, width), bf16),
            pltpu.VMEM((2 * half, width), bf16),
            pltpu.VMEM((D, width), bf16),
            pltpu.VMEM((width, D), bf16),
            pltpu.SemaphoreType.DMA((4,)),
        ],
        far=2,
        name="ffn_fwd",
    )


def ffn_bwd_kernel(
    layer, own, got, up_far, down_far, pre_far, up_low_far, bias_sum, sent, keep,
    both, up, down, pre, up_low, sems,
):
    ins = ((down_far.at[layer], down), (pre_far, pre), (up_far.at[layer], up))
    copies = [pltpu.make_async_copy(a, b, sems.at[i]) for i, (a, b) in enumerate(ins)]
    for copy in copies:
        copy.start()
    half = own.shape[0]
    both[:half, :] = own[...]
    both[half:, :] = got[...]
    copies[0].wait()
    copies[1].wait()
    v = pre[...].astype(f32)
    t = jnp.tanh(GELU_A * (v + GELU_B * v * v * v))
    slope = 0.5 * (1.0 + t) + 0.5 * v * (1.0 - t * t) * (GELU_A * (1.0 + 3.0 * GELU_B * v * v))
    g = dot_cols(both[...], down[...]) * slope
    bias_sum[...] = jnp.sum(g, axis=0, keepdims=True)
    up_low[...] = g.astype(bf16)
    copy_low = pltpu.make_async_copy(up_low, up_low_far, sems.at[3])
    copy_low.start()
    copies[2].wait()
    total = dot_cols(up_low[...], up[...])
    keep[...] = total[:half, :]
    sent[...] = total[half:, :].astype(bf16)
    copy_low.wait()


def ffn_bwd(run, layer, own, got, up, down, pre, near):
    half, width = own.shape[0], up.shape[2]
    if not near:
        up, down = stay(up), stay(down)
    up_low, bias_sum, sent, keep = run(
        functools.partial(ffn_bwd_kernel, layer),
        [(own, None), (got, None), (up, FAR), (down, FAR), (stay(pre), FAR)],
        [
            struct((2 * half, width), bf16),
            struct((1, width), f32),
            struct((half, D), bf16),
            struct((half, D), f32),
        ],
        scratch=[
            pltpu.VMEM((2 * half, D), bf16),
            pltpu.VMEM((D, width), bf16),
            pltpu.VMEM((width, D), bf16),
            pltpu.VMEM((2 * half, width), bf16),
            pltpu.VMEM((2 * half, width), bf16),
            pltpu.SemaphoreType.DMA((4,)),
        ],
        far=1,
        spill=1,
        name="ffn_bwd",
    )
    return bias_sum, up_low, sent, keep


def sine(x, both=False):
    turns = jnp.floor(x * (1.0 / math.pi) + 0.5)
    rest = (x - turns * 3.140625) - turns * 9.67653589793e-4
    sign = 1.0 - 2.0 * (turns - 2.0 * jnp.floor(turns * 0.5))
    sq = rest * rest
    odd = -1.0 / 39916800.0
    for c in (1.0 / 362880.0, -1.0 / 5040.0, 1.0 / 120.0, -1.0 / 6.0, 1.0):
        odd = odd * sq + c
    value = sign * rest * odd
    if not both:
        return value
    even = 1.0 / 479001600.0
    for c in (-1.0 / 3628800.0, 1.0 / 40320.0, -1.0 / 720.0, 1.0 / 24.0, -0.5, 1.0):
        even = even * sq + c
    return value, sign * even


def decay(spot, channels, length):
    lane = lax.broadcasted_iota(jnp.int32, (1, channels), 1) + spot * channels
    row = lax.broadcasted_iota(jnp.int32, (REACH, channels), 0).astype(f32)
    rate = slow_rate + (fast_rate - slow_rate) * lane.astype(f32) / (D - 1)
    return jnp.exp(-(row * (1.0 / (length - 1))) * rate)


def columns(layer, *refs):
    rows = [r[layer : layer + 1, :] for r in refs] + [jnp.zeros((8 - len(refs), FILT), f32)]
    wide = jnp.concatenate([jnp.concatenate(rows, axis=0), jnp.zeros((8, 128 - FILT), f32)], axis=1).T
    return [wide[:FILT, i : i + 1] for i in range(len(refs))]


def filter_fwd_kernel(
    layer, length, scal, pos, w_in, b_in, f_in, w_mid, b_mid, f_mid, w_out, waves, spec, kept
):
    channels = w_out.shape[1]
    b_in, f_in, b_mid, f_mid = columns(layer, b_in, f_in, b_mid, f_mid)
    z = fine(w_in[...], pos[:POS, :], ((0,), (0,))) + b_in
    h, c = sine(f_in * z, both=True)
    kept[0] = z
    kept[1] = h
    kept[2] = c
    z = fine(w_mid[...], h, ((0,), (0,))) + b_mid
    h, c = sine(f_mid * z, both=True)
    kept[3] = z
    kept[4] = h
    kept[5] = c
    taps = fine(h, w_out[...], ((0,), (0,))) * decay(scal[4], channels, length)
    spec[...] = dot(waves[:, :REACH], taps.astype(bf16)) * (2.0 / WAVES)


def filter_fwd(run, layer, length, scal, pos, weights, waves):
    channels = weights[-1].shape[2]
    return run(
        functools.partial(filter_fwd_kernel, layer, length),
        [(scal, SMALL), (pos, None)]
        + [(a, layer_of(a, layer) if a.ndim == 3 else None) for a in weights]
        + [(waves, None)],
        [struct((WAVES, channels), f32), struct((6, FILT, REACH), f32)],
        spill=2,
        name="filter_fwd",
    )


def filter_bwd_kernel(layer, length, scal, taps_grad, pos, f_in, w_mid, f_mid, w_out, kept, by_chan, narrow):
    channels = w_out.shape[1]
    dt = taps_grad[...] * decay(scal[4], channels, length)
    by_chan[...] = fine(kept[4], dt, ((1,), (0,)))
    f_in, f_mid = columns(layer, f_in, f_mid)
    dh = fine(w_out[...], dt, ((1,), (1,)))
    c = kept[5] * dh
    dz = c * f_mid
    narrow[NW_MID : NW_MID + FILT, :] = fine(kept[1], dz, ((1,), (1,)))
    mid_sums = jnp.concatenate(
        [jnp.sum(dz, axis=1, keepdims=True), jnp.sum(c * kept[3], axis=1, keepdims=True)], axis=1
    )
    dh = fine(w_mid[...], dz, ((1,), (0,)))
    c = kept[2] * dh
    dz = c * f_in
    narrow[:POS, :] = fine(pos[...], dz, ((1,), (1,)))[:POS, :]
    in_sums = jnp.concatenate(
        [jnp.sum(dz, axis=1, keepdims=True), jnp.sum(c * kept[0], axis=1, keepdims=True)], axis=1
    )
    sums = jnp.concatenate([in_sums, mid_sums, jnp.zeros((FILT, 124), f32)], axis=1).T
    narrow[NB_IN : NB_IN + 2, :] = sums[0:2, :]
    narrow[NB_MID : NB_MID + 2, :] = sums[2:4, :]
    narrow[NF_MID + 1 :, :] = jnp.zeros((NARROW_ROWS - NF_MID - 1, FILT), f32)


def filter_bwd(run, layer, length, scal, taps_grad, pos, weights, kept):
    _, _, f_in, w_mid, _, f_mid, w_out = weights
    return run(
        functools.partial(filter_bwd_kernel, layer, length),
        [(scal, SMALL), (taps_grad, None), (pos, None)]
        + [(a, layer_of(a, layer) if a.ndim == 3 else None) for a in (f_in, w_mid, f_mid, w_out)]
        + [(kept, None)],
        [struct((FILT, w_out.shape[2]), f32), struct((NARROW_ROWS, FILT), f32)],
        name="filter_bwd",
    )


def lagged(ref, tile, cols, lag, before=None):
    if tile:
        return ref[tile * TILE - lag : (tile + 1) * TILE - lag, cols]
    if before is None:
        head = jnp.zeros((lag, cols.stop - cols.start), f32)
    else:
        head = before[before.shape[0] - lag :, cols]
    return jnp.concatenate([head, ref[: TILE - lag, cols]], axis=0)


def ahead(ref, tile, cols, lag, last):
    if tile < last:
        return ref[tile * TILE + lag : (tile + 1) * TILE + lag, cols]
    empty = jnp.zeros((lag, cols.stop - cols.start), f32)
    return jnp.concatenate([ref[tile * TILE + lag : (tile + 1) * TILE, cols], empty], axis=0)


def place(tile, first, shift=0):
    row = lax.broadcasted_iota(jnp.int32, (TILE, 1), 0) + (tile * TILE + shift)
    in_first = row < first
    return in_first, jnp.where(in_first, row, row - first)


def short_tile(proj, conv_w, conv_b, layer, tile, stream, offset, channels, before=None):
    cols = slice(stream * channels, (stream + 1) * channels)
    row = slice(layer, layer + 1)
    total = proj[tile * TILE : (tile + 1) * TILE, cols] * conv_w[stream, 0, row, :]
    total = total + conv_b[stream, row, :]
    for lag in range(1, SHORT):
        weight = conv_w[stream, lag, row, :]
        total = total + jnp.where(offset >= lag, lagged(proj, tile, cols, lag, before) * weight, 0.0)
    return total


def tile_rows(tile):
    return slice(tile * TILE, (tile + 1) * TILE)


def halves(own_a, own_b, got_a, got_b, core):
    block = own_a.shape[0]
    out = []
    for half, (own, got) in enumerate(((own_a, got_a), (own_b, got_b))):
        for rows, side in ((own, core), (got, 1 - core)):
            out.append((rows, pl.multiple_of(2 * block * half + side * block, block)))
    return out


def mix_fwd_kernel(layer, half, *refs):
    (scal, in_b, conv_w, conv_b, skip, own_far, got_far, in_w_far, taps_far, out_w_far, waves_far, waves_t_far), refs = (
        refs[:12],
        refs[12:],
    )
    before, prev = None, None
    if half:
        (before, prev), refs = refs[:2], refs[2:]
    (proj_far, longc_far, mixed_far, spec, tail, sent, keep), refs = refs[:7], refs[7:]
    own, got, in_w, waves, waves_t, taps, out_w, proj, gated, mixed, s0, pieces, prod, sems = refs
    block = own.shape[0]
    length = 2 * block
    first_ins = ((own_far, own), (got_far, got), (in_w_far.at[layer], in_w))
    first_copies = [pltpu.make_async_copy(a, b, sems.at[8 + i]) for i, (a, b) in enumerate(first_ins)]
    for copy in first_copies:
        copy.start()
    places = slice(half * length, (half + 1) * length)
    ins = [
        (waves_far.at[:, places], waves),
        (taps_far, taps),
        (waves_t_far.at[places, :], waves_t),
        (out_w_far.at[layer], out_w),
    ]
    copies = [pltpu.make_async_copy(a, b, sems.at[i]) for i, (a, b) in enumerate(ins)]
    outs = ((proj, proj_far), (gated, longc_far), (mixed, mixed_far))
    copy_proj, copy_long, copy_mixed = [
        pltpu.make_async_copy(a, b, sems.at[4 + i]) for i, (a, b) in enumerate(outs)
    ]
    for copy in copies:
        copy.start()
    for copy in first_copies:
        copy.wait()
    first, core = scal[0], scal[1]
    channels = skip.shape[1]
    row = slice(layer, layer + 1)
    sides = [pl.multiple_of(side * block, block) for side in (core, 1 - core)]
    for rows, at in zip((own, got), sides):
        for stream in range(STREAMS):
            cols = slice(stream * channels, (stream + 1) * channels)
            proj[pl.ds(at, block), cols] = dot(rows[...], in_w[stream]) + in_b[stream, row, :]
    copy_proj.start()
    tail[...] = proj[length - 8 :, :]
    for tile in range(length // TILE):
        rows = tile_rows(tile)
        in_first, offset = place(tile, first, half * length)
        one, two, zero = [
            short_tile(proj, conv_w, conv_b, layer, tile, stream, offset, channels, before)
            for stream in (1, 2, 0)
        ]
        g = one * two
        gated[rows, :] = g
        s0[rows, :] = zero
        pieces[rows, :channels] = jnp.where(in_first, g, 0.0).astype(bf16)
        pieces[rows, channels:] = jnp.where(in_first, 0.0, g).astype(bf16)
    copies[0].wait()
    copies[1].wait()
    steps = 2
    part = REACH // steps
    for step in range(steps):
        lo = slice(step * part, (step + 1) * part)
        hi = slice(REACH + step * part, REACH + (step + 1) * part)
        for seg in range(2):
            cols = slice(seg * channels, (seg + 1) * channels)
            re = dot(waves[lo, :], pieces[:, cols])
            im = dot(waves[hi, :], pieces[:, cols])
            if half:
                re = re + prev[lo, cols].astype(f32)
                im = im + prev[hi, cols].astype(f32)
            t_re, t_im = taps[lo, :], taps[hi, :]
            spec[lo, cols] = re.astype(bf16)
            spec[hi, cols] = im.astype(bf16)
            prod[lo, cols] = (re * t_re - im * t_im).astype(bf16)
            prod[hi, cols] = (re * t_im + im * t_re).astype(bf16)
    copies[2].wait()
    in_first = lax.broadcasted_iota(jnp.int32, (length, 1), 0) + half * length < first
    a = dot(waves_t[...], prod[:, :channels])
    b = dot(waves_t[...], prod[:, channels:])
    total = jnp.where(in_first, a, b) + skip[row, :] * gated[...]
    gated[...] = total
    mixed[...] = (total * s0[...]).astype(bf16)
    copy_long.start()
    copy_mixed.start()
    copies[3].wait()
    keep[...] = dot(mixed[pl.ds(sides[0], block), :], out_w[...])
    sent[...] = dot(mixed[pl.ds(sides[1], block), :], out_w[...]).astype(bf16)
    for copy in (copy_proj, copy_long, copy_mixed):
        copy.wait()


def mix_fwd(run, layer, half, scal, own, got, in_w, in_b, conv_w, conv_b, skip, taps, out_w, waves, waves_t, prev):
    block, channels = own.shape[0], skip.shape[1]
    length = 2 * block
    extra = [] if prev is None else [(a, None) for a in prev]
    proj, longc, mixed, spec, tail, sent, keep = run(
        functools.partial(mix_fwd_kernel, layer, half),
        [(scal, SMALL)]
        + [(a, None) for a in (in_b, conv_w, conv_b, skip)]
        + [(stay(own), FAR), (got, FAR)]
        + [(stay(a), FAR) for a in (in_w, taps, out_w, waves, waves_t)]
        + extra,
        [
            struct((length, STREAMS * channels), f32),
            struct((length, channels), f32),
            struct((length, channels), bf16),
            struct((WAVES, 2 * channels), bf16),
            struct((8, STREAMS * channels), f32),
            struct((block, D), bf16),
            struct((block, D), f32),
        ],
        scratch=[
            pltpu.VMEM((block, D), bf16),
            pltpu.VMEM((block, D), bf16),
            pltpu.VMEM((STREAMS, D, channels), bf16),
            pltpu.VMEM((WAVES, length), bf16),
            pltpu.VMEM((length, WAVES), bf16),
            pltpu.VMEM((WAVES, channels), f32),
            pltpu.VMEM((channels, D), bf16),
            pltpu.VMEM((length, STREAMS * channels), f32),
            pltpu.VMEM((length, channels), f32),
            pltpu.VMEM((length, channels), bf16),
            pltpu.VMEM((length, channels), f32),
            pltpu.VMEM((length, 2 * channels), bf16),
            pltpu.VMEM((WAVES, 2 * channels), bf16),
            pltpu.SemaphoreType.DMA((11,)),
        ],
        far=3,
        spill=half,
        name="mix_fwd",
    )
    return (proj, longc, mixed), (tail, spec), sent, keep


def mix_bwd_kernel(
    layer, scal, conv_w, conv_b, skip, own_a_far, own_b_far, got_a_far, got_b_far, out_w_far,
    proj_a_far, proj_b_far, longc_a_far, longc_b_far, waves_far, spec_far, taps_far, waves_t_far, in_w_far,
    in_low, taps_grad, sums, sent_a, sent_b, keep_a, keep_b,
    own_a, own_b, got_a, got_b, out_w, proj, longc, waves, spec, taps, waves_t, in_w, mgrad, ds, pieces, prod,
    corr, sems,
):
    first_ins = (
        (own_a_far, own_a),
        (own_b_far, own_b),
        (got_a_far, got_a),
        (got_b_far, got_b),
        (out_w_far.at[layer], out_w),
    )
    first_copies = [pltpu.make_async_copy(a, b, sems.at[9 + i]) for i, (a, b) in enumerate(first_ins)]
    for copy in first_copies:
        copy.start()
    half_rows = proj_a_far.shape[0]
    near, later = pl.ds(0, half_rows), pl.ds(half_rows, half_rows)
    ins = (
        (proj_a_far, proj.at[near, :]),
        (longc_a_far, longc.at[near, :]),
        (proj_b_far, proj.at[later, :]),
        (longc_b_far, longc.at[later, :]),
        (waves_far, waves),
        (spec_far, spec),
        (taps_far, taps),
        (waves_t_far, waves_t),
        (in_w_far.at[layer], in_w),
    )
    copies = [pltpu.make_async_copy(a, b, sems.at[i]) for i, (a, b) in enumerate(ins)]
    for copy in copies[:4]:
        copy.start()
    first, core = scal[0], scal[1]
    block = own_a.shape[0]
    channels = skip.shape[1]
    row = slice(layer, layer + 1)
    length = 4 * block
    tiles = length // TILE
    for copy in first_copies:
        copy.wait()
    for copy in copies[4:]:
        copy.start()
    for rows, at in halves(own_a, own_b, got_a, got_b, core):
        mgrad[pl.ds(at, block), :] = dot_cols(rows[...], out_w[...])
    skip_sum = jnp.zeros((1, channels), f32)
    for copy in copies[:4]:
        copy.wait()
    mid, end = slice(channels, 2 * channels), slice(2 * channels, 3 * channels)
    for tile in range(tiles):
        rows = tile_rows(tile)
        in_first, offset = place(tile, first)
        one = short_tile(proj, conv_w, conv_b, layer, tile, 1, offset, channels)
        two = short_tile(proj, conv_w, conv_b, layer, tile, 2, offset, channels)
        ds[rows, mid] = one
        ds[rows, end] = two
        m = mgrad[rows, :]
        r = m * short_tile(proj, conv_w, conv_b, layer, tile, 0, offset, channels)
        mgrad[rows, :] = r
        ds[rows, :channels] = m * longc[rows, :]
        skip_sum = skip_sum + jnp.sum(r * one * two, axis=0, keepdims=True)
        pieces[rows, :channels] = jnp.where(in_first, r, 0.0).astype(bf16)
        pieces[rows, channels:] = jnp.where(in_first, 0.0, r).astype(bf16)
    sums[ROW_SKIP : ROW_SKIP + 1, :] = skip_sum
    for copy in copies[4:7]:
        copy.wait()
    steps = 2
    part = REACH // steps
    for step in range(steps):
        lo = slice(step * part, (step + 1) * part)
        hi = slice(REACH + step * part, REACH + (step + 1) * part)
        corr_re, corr_im = None, None
        for seg in range(2):
            cols = slice(seg * channels, (seg + 1) * channels)
            re = dot(waves[lo, :], pieces[:, cols])
            im = dot(waves[hi, :], pieces[:, cols])
            t_re, t_im = taps[lo, :], taps[hi, :]
            prod[lo, cols] = (re * t_re + im * t_im).astype(bf16)
            prod[hi, cols] = (im * t_re - re * t_im).astype(bf16)
            g_re, g_im = spec[lo, cols].astype(f32), spec[hi, cols].astype(f32)
            c_re = g_re * re + g_im * im
            c_im = g_re * im - g_im * re
            corr_re = c_re if corr_re is None else corr_re + c_re
            corr_im = c_im if corr_im is None else corr_im + c_im
        corr[lo, :] = corr_re.astype(bf16)
        corr[hi, :] = corr_im.astype(bf16)
    copies[7].wait()
    big = 512
    for r in range(length // big):
        rows = slice(r * big, (r + 1) * big)
        in_first = lax.broadcasted_iota(jnp.int32, (big, 1), 0) + r * big < first
        a = dot(waves_t[rows, :], prod[:, :channels])
        b = dot(waves_t[rows, :], prod[:, channels:])
        total = jnp.where(in_first, a, b) + skip[row, :] * mgrad[rows, :]
        one, two = ds[rows, mid], ds[rows, end]
        ds[rows, mid] = total * two
        ds[rows, end] = total * one
    for stream in range(STREAMS):
        cols = slice(stream * channels, (stream + 1) * channels)
        at = stream * SHORT
        bias_sum = jnp.zeros((1, channels), f32)
        in_sum = jnp.zeros((1, channels), f32)
        lag_sums = [jnp.zeros((1, channels), f32) for _ in range(SHORT)]
        for tile in range(tiles):
            rows = tile_rows(tile)
            _, offset = place(tile, first)
            d = ds[rows, cols]
            p = proj[rows, cols]
            total = d * conv_w[stream, 0, row, :]
            bias_sum = bias_sum + jnp.sum(d, axis=0, keepdims=True)
            lag_sums[0] = lag_sums[0] + jnp.sum(d * p, axis=0, keepdims=True)
            for lag in range(1, SHORT):
                _, later = place(tile, first, lag)
                moved = jnp.where(later >= lag, ahead(ds, tile, cols, lag, tiles - 1), 0.0)
                total = total + moved * conv_w[stream, lag, row, :]
                lag_sums[lag] = lag_sums[lag] + jnp.sum(moved * p, axis=0, keepdims=True)
            in_sum = in_sum + jnp.sum(total, axis=0, keepdims=True)
            in_low[rows, cols] = total.astype(bf16)
        sums[ROW_IN_BIAS + stream : ROW_IN_BIAS + stream + 1, :] = in_sum
        sums[ROW_CONV_B + stream : ROW_CONV_B + stream + 1, :] = bias_sum
        for lag in range(SHORT):
            sums[ROW_CONV_W + at + lag : ROW_CONV_W + at + lag + 1, :] = lag_sums[lag]

    def into(at):
        rows = pl.ds(at, block)
        total = dot_cols(in_low[rows, :channels], in_w[0])
        for stream in range(1, STREAMS):
            cols = slice(stream * channels, (stream + 1) * channels)
            total = total + dot_cols(in_low[rows, cols], in_w[stream])
        return total

    copies[8].wait()
    for half, (sent, keep) in enumerate(((sent_a, keep_a), (sent_b, keep_b))):
        at = pl.multiple_of(2 * block * half + (1 - core) * block, block)
        sent[...] = into(at).astype(bf16)
        at = pl.multiple_of(2 * block * half + core * block, block)
        keep[...] = into(at)
    taps_grad[...] = dot(waves_t[:REACH, :], corr[...]) * (2.0 / WAVES)


def mix_bwd(run, layer, scal, rows, out_w, saved, spec, in_w, conv_w, conv_b, skip, taps, waves, waves_t):
    block, channels = rows[0].shape[0], skip.shape[1]
    length = 4 * block
    return run(
        functools.partial(mix_bwd_kernel, layer),
        [(scal, SMALL)]
        + [(a, None) for a in (conv_w, conv_b, skip)]
        + [(stay(a), FAR) for a in rows[:2]]
        + [(a, FAR) for a in rows[2:]]
        + [(stay(out_w), FAR)]
        + [(stay(a), FAR) for a in (saved[0][0], saved[1][0], saved[0][1], saved[1][1], waves, spec, taps, waves_t, in_w)],
        [
            struct((length, STREAMS * channels), bf16),
            struct((REACH, channels), f32),
            struct((16, channels), f32),
            struct((block, D), bf16),
            struct((block, D), bf16),
            struct((block, D), f32),
            struct((block, D), f32),
        ],
        scratch=[
            pltpu.VMEM((block, D), bf16),
            pltpu.VMEM((block, D), bf16),
            pltpu.VMEM((block, D), bf16),
            pltpu.VMEM((block, D), bf16),
            pltpu.VMEM((channels, D), bf16),
            pltpu.VMEM((length, STREAMS * channels), f32),
            pltpu.VMEM((length, channels), f32),
            pltpu.VMEM((WAVES, length), bf16),
            pltpu.VMEM((WAVES, 2 * channels), bf16),
            pltpu.VMEM((WAVES, channels), f32),
            pltpu.VMEM((length, WAVES), bf16),
            pltpu.VMEM((STREAMS, D, channels), bf16),
            pltpu.VMEM((length, channels), f32),
            pltpu.VMEM((length, STREAMS * channels), f32),
            pltpu.VMEM((length, 2 * channels), bf16),
            pltpu.VMEM((WAVES, 2 * channels), bf16),
            pltpu.VMEM((WAVES, channels), bf16),
            pltpu.SemaphoreType.DMA((14,)),
        ],
        name="mix_bwd",
    )


def parts_order(strides):
    bits = len(strides)
    return [sum(((part >> (bits - 1 - i)) & 1) * s for i, s in enumerate(strides)) for part in range(1 << bits)]


def spread_columns(source, target, at, index, order):
    for part, step in enumerate(order):
        cols = pl.ds(pl.multiple_of((index ^ step) * CHUNK, CHUNK), CHUNK)
        target[at, part * CHUNK : (part + 1) * CHUNK] = source[:, cols]


def ffn_grad_kernel(orders, scal, *refs):
    feeds, lows = refs[0:4], refs[4:8]
    (up_a, up_b, hid_a, hid_b), outs, (left, right) = refs[8:12], refs[12:16], refs[16:18]
    block = feeds[0].shape[0]
    index = scal[3]
    for k, (source, (rhs_a, rhs_b)) in enumerate(((feeds, (up_a, up_b)), (lows, (hid_a, hid_b)))):
        right[: 2 * block, :] = rhs_a[...]
        right[2 * block :, :] = rhs_b[...]
        for i in range(4):
            spread_columns(source[i], left, slice(i * block, (i + 1) * block), index, orders[k])
        for half in range(2):
            out = outs[2 * k + half]
            wide = PARTS // 2 * CHUNK
            got = dot_rows(left[:, half * wide : (half + 1) * wide], right[...]).astype(bf16)
            for part in range(PARTS // 2):
                out[part] = got[part * CHUNK : (part + 1) * CHUNK, :]


def ffn_whole_kernel(*refs):
    feeds, lows = refs[0:4], refs[4:8]
    (up_a, up_b, hid_a, hid_b), out, (left, right) = refs[8:12], refs[12], refs[13:15]
    block = feeds[0].shape[0]
    for k, (source, (rhs_a, rhs_b)) in enumerate(((feeds, (up_a, up_b)), (lows, (hid_a, hid_b)))):
        right[: 2 * block, :] = rhs_a[...]
        right[2 * block :, :] = rhs_b[...]
        for i in range(4):
            left[i * block : (i + 1) * block, :] = source[i][...]
        for half in range(2):
            rows = slice(half * D // 2, (half + 1) * D // 2)
            out[k, rows, :] = dot_rows(left[:, rows], right[...]).astype(bf16)


def ffn_whole(run, feeds, lows, ups, hids):
    block, width = feeds[0].shape[0], ups[0].shape[1]
    return run(
        ffn_whole_kernel,
        [(a, None) for a in (*feeds, *lows, *ups, *hids)],
        [struct((2, D, width), bf16)],
        scratch=[pltpu.VMEM((4 * block, D), bf16), pltpu.VMEM((4 * block, width), bf16)],
        spill=1,
        name="ffn_whole",
    )[0]


def ffn_grad(run, orders, scal, feeds, lows, ups, hids):
    block, width = feeds[0].shape[0], ups[0].shape[1]
    out = struct((PARTS // 2, CHUNK, width), bf16)
    return run(
        functools.partial(ffn_grad_kernel, orders),
        [(scal, SMALL)] + [(a, None) for a in (*feeds, *lows, *ups, *hids)],
        [out] * 4,
        scratch=[pltpu.VMEM((4 * block, D), bf16), pltpu.VMEM((4 * block, width), bf16)],
        spill=4,
        name="ffn_grad",
    )


def join(target, a, b):
    rows = a.shape[0]
    target[:rows, :] = a[...]
    target[rows:, :] = b[...]


def mix_grad_kernel(orders, scal, *refs):
    normed, lows = refs[0:4], refs[4:8]
    in_low, mixed_a, mixed_b = refs[8:11]
    outs, (left, mixed) = refs[11:-2], refs[-2:]
    joined = len(outs) == 2
    channels = mixed.shape[1]
    join(mixed, mixed_a, mixed_b)
    core, index = scal[1], scal[3]
    groups = (
        (normed, in_low, slice(0, 2 * channels), 0, 0),
        (normed, in_low, slice(2 * channels, 3 * channels), 1, 0),
        (lows, mixed, slice(0, channels), 1, 1),
    )
    for source, rhs, cols, group, base in groups:
        own_a, own_b, got_a, got_b = source
        block = own_a.shape[0]
        for rows, at in halves(own_a, own_b, got_a, got_b, core):
            spread_columns(rows, left, pl.ds(at, block), index, orders[group])
        for half in range(2):
            out = outs[half if joined else 2 * group + half]
            first = base + 2 * group if joined else base
            wide = PARTS // 2 * CHUNK
            got = dot_rows(left[:, half * wide : (half + 1) * wide], rhs[:, cols]).astype(bf16)
            for part in range(PARTS // 2):
                for i in range(got.shape[1] // channels):
                    block_cols = slice(i * channels, (i + 1) * channels)
                    out[part, first + i] = got[part * CHUNK : (part + 1) * CHUNK, block_cols]


def mix_grad(run, orders, scal, normed, lows, in_low, mixed, joined):
    block, channels = normed[0].shape[0], mixed[0].shape[1]
    if joined:
        outs = [struct((PARTS // 2, 4, CHUNK, channels), bf16)] * 2
    else:
        outs = [struct((PARTS // 2, 2, CHUNK, channels), bf16)] * 4
    return run(
        functools.partial(mix_grad_kernel, orders),
        [(scal, SMALL)]
        + [(a, None) for a in (*normed, *lows, in_low, *mixed)],
        outs,
        scratch=[pltpu.VMEM((4 * block, D), bf16), pltpu.VMEM((4 * block, channels), bf16)],
        spill=len(outs),
        name="mix_grad",
    )


def halve_kernel(keep, got, sent, kept):
    count = keep.shape[0] // 2
    for i in range(count):
        kept[i] = (keep[i].astype(f32) + got[i].astype(f32)).astype(bf16)
        sent[i] = (keep[count + i].astype(f32) + got[count + i].astype(f32)).astype(bf16)


def halve(run, keep, got):
    out = struct((keep.shape[0] // 2, *keep.shape[1:]), bf16)
    return run(halve_kernel, [(keep, None), (got, None)], [out, out], spill=2, name="halve")


def total_of(refs, leads):
    return sum(ref[lead].astype(f32) for ref, lead in zip(refs, leads))


def finish_kernel(leads, turned, *refs):
    out, refs = refs[-1], list(refs[:-1])
    for layer, lead in enumerate(leads):
        total = total_of([refs.pop(0) for _ in lead], lead)
        out[layer] = total.T if turned else total


def ffn_finish(run, terms, turned):
    _, rows, cols = terms[0][0][0].shape
    shape = (cols, rows) if turned else (rows, cols)
    leads = [[lead for _, lead in pairs] for pairs in terms]
    return run(
        functools.partial(finish_kernel, leads, turned),
        [(a, None) for pairs in terms for a, _ in pairs],
        [struct((len(terms), *shape), f32)],
        name="ffn_finish",
    )[0]


def mix_finish_kernel(plan, *refs):
    into, out = refs[-2:]
    for layer, streams in enumerate(plan):
        for stream, parts in enumerate(streams):
            total = sum(refs[k][lead].astype(f32) for k, lead in parts)
            if stream < STREAMS:
                into[layer, stream] = total
            else:
                out[layer] = total.T


def mix_finish(run, arrays, plan):
    rows, channels = arrays[0].shape[-2:]
    return run(
        functools.partial(mix_finish_kernel, plan),
        [(a, None) for a in arrays],
        [struct((len(plan), STREAMS, rows, channels), f32), struct((len(plan), channels, rows), f32)],
        name="mix_finish",
    )


def pack_kernel(mix, filt, narrow, up_a, up_b, feed_a, feed_b, in_a, in_b, own, down, out):
    channels = mix.shape[1]
    out[:16, :] = mix[...]
    out[ROW_FILTER : ROW_FILTER + FILT, :] = filt[...]
    for q in range(D // channels):
        cols = slice(q * channels, (q + 1) * channels)
        out[ROW_UP_BIAS + q : ROW_UP_BIAS + q + 1, :] = up_a[:, cols] + up_b[:, cols]
        wide = [feed_a[i : i + 1, cols] + feed_b[i : i + 1, cols] for i in range(3)]
        wide.append(down[:, cols])
        wide += [in_a[i : i + 1, cols] + in_b[i : i + 1, cols] for i in range(2)]
        wide += [own[i : i + 1, cols] for i in range(2)]
        for i, value in enumerate(wide):
            at = ROW_WIDE + 4 * i + q
            out[at : at + 1, :] = value
    groups = [
        narrow[i * NARROW_GROUP : (i + 1) * NARROW_GROUP, :] for i in range(channels // FILT)
    ]
    out[ROW_NARROW:, :] = jnp.concatenate(groups, axis=1)


def pack(run, mix, filt, narrow, ups, feeds, ins, own, down):
    return run(
        pack_kernel,
        [(a, None) for a in (mix, filt, narrow, *ups, *feeds, *ins, own, down)],
        [struct((PACK_ROWS, mix.shape[1]), f32)],
        name="pack_small",
    )[0]


def gate(run, after=()):
    run(lambda: None, [], [], name="gate", after=after)


def stack_kernel(*refs):
    size = refs[0].shape[0]
    total, low = refs[-2:]
    for i, ref in enumerate(refs[:-2]):
        total[i * size : (i + 1) * size, :] = ref[...]
        low[i * size : (i + 1) * size, :] = ref[...].astype(bf16)


def stack_packs(run, packs):
    rows, cols = packs[0].shape
    shape = (len(packs) * rows, cols)
    return run(
        stack_kernel, [(a, None) for a in packs], [struct(shape, f32), struct(shape, bf16)], name="stack_packs"
    )


def add_small_kernel(value, got, total, low):
    added = value[...] + got[...].astype(f32)
    total[...] = added
    low[...] = added.astype(bf16)


def add_small(run, value, got):
    outs = [struct(value.shape, f32), struct(value.shape, bf16)]
    return run(add_small_kernel, [(value, None), (got, None)], outs, name="add_small")


def last_small_kernel(value, got, total, wide):
    added = value[...] + got[...].astype(f32)
    total[...] = added
    size = PACK_ROWS - ROW_WIDE
    for i in range(value.shape[0] // PACK_ROWS):
        wide[i * size : (i + 1) * size, :] = added[i * PACK_ROWS + ROW_WIDE : (i + 1) * PACK_ROWS, :]


def last_small(run, value, got):
    rows, cols = value.shape
    wide = struct((rows // PACK_ROWS * (PACK_ROWS - ROW_WIDE), cols), f32)
    return run(
        last_small_kernel, [(value, None), (got, None)], [struct(value.shape, f32), wide], name="last_small"
    )


def sum_kernel(a, b, out):
    out[...] = a[...] + b[...]


def add_pair(run, a, b):
    return run(sum_kernel, [(a, None), (b, None)], [struct(a.shape, f32)], name="add_pair")[0]


def unpack_kernel(layers, *refs):
    (chans, wides), outs = refs[:2], refs[2:]
    (gain, shift, out_bias, feed_gain, feed_shift, down_bias, in_bias, conv_w, conv_b, skip, filt, up_bias,
     w_in, b_in, f_in, w_mid, b_mid, f_mid) = outs
    channels = chans.shape[1]
    size = PACK_ROWS - ROW_WIDE
    for layer in range(layers):
        chan = chans[layer * PACK_ROWS : (layer + 1) * PACK_ROWS, :]
        wide = wides[layer * size : (layer + 1) * size, :]
        row = slice(layer, layer + 1)

        def spread(target, ref, at, row=row):
            for q in range(D // channels):
                target[row, q * channels : (q + 1) * channels] = ref[at + q : at + q + 1, :]

        spread(feed_gain, wide, 0)
        spread(feed_shift, wide, 4)
        spread(out_bias, wide, 8)
        spread(down_bias, wide, 12)
        if layer + 1 < layers:
            spread(gain, wide, 16, slice(layer + 1, layer + 2))
            spread(shift, wide, 20, slice(layer + 1, layer + 2))
        if layer == 0:
            spread(gain, wide, 24)
            spread(shift, wide, 28)
        spread(up_bias, chan, ROW_UP_BIAS)
        for stream in range(STREAMS):
            in_bias[stream, row, :] = chan[ROW_IN_BIAS + stream : ROW_IN_BIAS + stream + 1, :]
            conv_b[stream, row, :] = chan[ROW_CONV_B + stream : ROW_CONV_B + stream + 1, :]
            for lag in range(SHORT):
                at = ROW_CONV_W + stream * SHORT + lag
                conv_w[stream, lag, row, :] = chan[at : at + 1, :]
        skip[row, :] = chan[ROW_SKIP : ROW_SKIP + 1, :]
        filt[layer] = chan[ROW_FILTER : ROW_FILTER + FILT, :]
        base = ROW_NARROW - ROW_WIDE
        rows = slice(base, base + NARROW_GROUP)
        narrow = jnp.concatenate(
            [wide[rows, i * FILT : (i + 1) * FILT] for i in range(channels // FILT)], axis=0
        )
        for target, at in ((b_in, NB_IN), (f_in, NF_IN), (b_mid, NB_MID), (f_mid, NF_MID)):
            target[row, :] = narrow[at : at + 1, :]
        w_in[layer] = narrow[:POS, :]
        w_mid[layer] = narrow[NW_MID : NW_MID + FILT, :]


def unpack(run, chans, wides, up_width):
    layers, channels = chans.shape[0] // PACK_ROWS, chans.shape[1]
    return run(
        functools.partial(unpack_kernel, layers),
        [(chans, None), (wides, None)],
        [struct((layers, D), f32)] * 6
        + [
            struct((STREAMS, layers, channels), f32),
            struct((STREAMS, SHORT, layers, channels), f32),
            struct((STREAMS, layers, channels), f32),
            struct((layers, channels), f32),
            struct((layers, FILT, channels), f32),
            struct((layers, up_width), f32),
            struct((layers, POS, FILT), f32),
            struct((layers, FILT), f32),
            struct((layers, FILT), f32),
            struct((layers, FILT, FILT), f32),
            struct((layers, FILT), f32),
            struct((layers, FILT), f32),
        ],
        name="unpack_small",
    )


def dp_swap(x, stride):
    size = lax.axis_size("dp")
    return lax.ppermute(x, "dp", [(i, i ^ stride) for i in range(size)])


class Scatter:
    def __init__(self, run, sent, keep, strides):
        self.run, self.keep = run, keep
        self.strides = list(strides)
        self.got = dp_swap(sent, self.strides.pop(0))

    def step(self):
        sent, self.keep = halve(self.run, self.keep, self.got)
        self.got = dp_swap(sent, self.strides.pop(0))

    def pair(self):
        while self.strides:
            self.step()
        return self.keep, self.got


class SmallSum:
    def __init__(self, run, packs, strides):
        self.run, self.strides = run, list(strides)
        self.value, low = stack_packs(run, packs)
        self.got = dp_swap(low, self.strides.pop(0))

    def step(self):
        self.value, low = add_small(self.run, self.value, self.got)
        self.got = dp_swap(low, self.strides.pop(0))

    def sums(self):
        return last_small(self.run, self.value, self.got)


def share_out(pair):
    keep, got = pair
    total = (keep[0].astype(f32) + got[0].astype(f32)).reshape(-1, CHUNK, keep.shape[-1])
    left = lax.axis_size("dp") // PARTS
    index = lax.axis_index("dp")
    stride = 1
    total = total.reshape(total.shape[0], left, CHUNK // left, -1)
    while left > 1:
        total = total.reshape(total.shape[0], left // 2, 2, total.shape[2], -1)
        bit = (index // stride) % 2
        mine = lax.dynamic_index_in_dim(total, bit, 2, keepdims=False)
        other = lax.dynamic_index_in_dim(total, 1 - bit, 2, keepdims=False)
        total = mine + dp_swap(other.astype(bf16), stride).astype(f32)
        left, stride = left // 2, stride * 2
    return total[:, 0]


def shards(
    tokens,
    seg_lengths,
    cotangent,
    mixer_norm_gain,
    mixer_norm_bias,
    in_weight,
    in_bias,
    conv_weight,
    conv_bias,
    filter_in,
    filter_in_bias,
    filter_in_freq,
    filter_mid,
    filter_mid_bias,
    filter_mid_freq,
    filter_out,
    skip_bias,
    out_weight,
    out_bias,
    feed_norm_gain,
    feed_norm_bias,
    feed_up,
    feed_up_bias,
    feed_down,
    feed_down_bias,
):
    block = tokens.shape[1]
    length = block * lax.axis_size("mp")
    channels = in_weight.shape[3]
    layers = in_weight.shape[0]
    spot = lax.axis_index("mp").astype(jnp.int32)
    left = lax.axis_size("dp") // PARTS
    chunk = (lax.axis_index("dp") // left).astype(jnp.int32)
    scal = jnp.stack([seg_lengths[0, 0], spot % 2, spot // 2, chunk, spot])
    table = wave_table(length)
    waves = jnp.asarray(table)
    waves_t = jnp.asarray(np.ascontiguousarray(table.T))
    pos = jnp.asarray(position_table(length))
    run = Chain()

    in_w = in_weight.transpose(0, 2, 1, 3)
    in_b = in_bias.transpose(1, 0, 2)
    conv_w = conv_weight.transpose(1, 2, 0, 3)
    conv_b = conv_bias.transpose(1, 0, 2)
    filter_weights = (
        filter_in, filter_in_bias, filter_in_freq, filter_mid, filter_mid_bias, filter_mid_freq, filter_out
    )
    both = range(2)

    def start_sum(ends):
        got = [core_swap(ends[i]) for i in both]
        out = []
        for i in both:
            here = add_low(run, ends[2 + i], got[i])
            out.append((here, chip_swap(here)))
        return out

    def one_sum(sent, keep):
        here = add_low(run, keep, core_swap(sent))
        return here, chip_swap(here)

    def in_turn(first, pace=None):
        gate(run, [first[1]])
        if pace is None:
            gate(run)
        else:
            pace.step()

    mine = tokens[0]
    other = chip_swap(mine)
    filt = [None] * layers
    early = tuple(stay(a) for a in filter_weights)
    filt[0] = filter_fwd(run, 0, length, scal, stay(pos), early, stay(waves))
    low_a, low_b, res_a, res_b, cot = first_norm(
        run, scal, stay(mine), other, stay(mixer_norm_gain), stay(mixer_norm_bias), stay(cotangent[0])
    )
    res, low = [res_a, res_b], [low_a, low_b]

    def in_halves(prepare, work, sums):
        out = []
        for i in both:
            prepare(i)
            sent, keep = work(i)
            if i == 0 and sums is not None:
                in_turn(sums[1])
            if i == 1:
                in_turn(out[0])
            out.append(one_sum(sent, keep))
        return out

    stored, cot_parts = [], []
    back = [None, None]
    got = [core_swap(x) for x in low]
    cot_other = chip_swap(cot)
    sums = None
    for layer in range(layers):
        last = layer + 1 == layers
        saved, passed, middle, feed, feed_got, ffn = [], [None], [], [], [], []
        if layer:
            res, low, got = [], [], []

        def mix_prepare(i):
            if layer:
                b, a = add_norm(
                    run, layer - 1, layer, *sums[i], stored[layer - 1][5][i],
                    feed_down_bias, mixer_norm_gain, mixer_norm_bias, 1,
                )
                res.append(a)
                low.append(b)
                got.append(core_swap(b))

        def mix_work(i):
            kept, on, sent, keep = mix_fwd(
                run, layer, i, scal, low[i], got[i], in_w, in_b, conv_w, conv_b, skip_bias, filt[layer][0],
                out_weight, waves, waves_t, passed[-1],
            )
            saved.append(kept)
            passed.append(on)
            if layer == 0 and i == 0:
                cot_parts.extend(first_grad(run, scal, cot, cot_other))
            return sent, keep

        def feed_prepare(i):
            b, a = add_norm(run, layer, layer, *sums[i], res[i], out_bias, feed_norm_gain, feed_norm_bias)
            middle.append(a)
            feed.append(b)
            feed_got.append(core_swap(b))

        def feed_work(i):
            ffn.append(ffn_fwd(run, layer, feed[i], feed_got[i], feed_up, feed_up_bias, feed_down))
            if i == 0 and not last:
                filt[layer + 1] = filter_fwd(
                    run, layer + 1, length, scal, pos, filter_weights, waves
                )
            if not last:
                return ffn[i][2], ffn[i][3]
            back[i] = ffn_bwd(run, layer, cot_low[i], cot_got[i], feed_up, feed_down, ffn[i][0], True)
            return back[i][2], back[i][3]

        sums = in_halves(mix_prepare, mix_work, sums)
        if layer == 0:
            cot_sum, *cot_low = cot_parts
            cot_got = [core_swap(x) for x in cot_low]
        stored.append(
            (res, (*low, *got), saved, passed[2][1], [kept[2] for kept in saved], middle, feed, feed_got, ffn)
        )
        sums = in_halves(feed_prepare, feed_work, sums)
    back_sums = sums

    rising, turned = (1, 2, 4), (2, 4, 1)
    feed_orders, mix_orders = (rising, turned), (rising, rising)

    def scatter_pair(sends, orders):
        return [
            Scatter(run, sends[2 * k + 1], sends[2 * k], [left * o for o in orders[k]]) for k in range(2)
        ]

    def scatter_rows(whole_grad):
        return lax.psum_scatter(whole_grad, "dp", scatter_dimension=1, tiled=True)

    def grad_args(layer, low, got, back):
        feed, feed_got, ffn = stored[layer][6:]
        return (
            (feed[0], feed_got[0], feed[1], feed_got[1]),
            (low[0], got[0], low[1], got[1]),
            [back[i][1] for i in both],
            [ffn[i][1] for i in both],
        )

    grad, low, got = cot_low, cot_low, cot_got
    down_sum = cot_sum
    moves = back_sums
    feed_shares, mix_rest, packs = ([None] * layers for _ in range(3))
    no_sums = jnp.zeros((8, D), f32)
    in_sums = [no_sums, no_sums]
    for layer in reversed(range(layers)):
        above = layer + 1
        entry, normed, saved, spec, mixed, middle, feed, feed_got, ffn = stored[layer]
        if layer:
            feed_whole = ffn_whole(run, *grad_args(layer, low, got, back))
        else:
            feed_sends = ffn_grad(
                run, [parts_order(o) for o in feed_orders], scal, *grad_args(layer, low, got, back)
            )
        if above == layers:
            out_got = [core_swap(ffn[i][2]) for i in both]
            out_send, out_mine = pick_outputs(
                run, layer, scal, [ffn[i][3] for i in both], out_got, middle, feed_down_bias
            )
        new_grad, low, feed_sums = [], [], []
        for i in both:
            a, c, b = norm_back(run, layer, *moves[i], middle[i], grad[i], feed_norm_gain, 1)
            new_grad.append(a)
            low.append(b)
            feed_sums.append(c)
        grad = new_grad
        got = [core_swap(x) for x in low]
        rows = (*low, *got)
        if layer:
            feed_shares[layer] = scatter_rows(run.release([feed_whole])[0])
        else:
            feed_sends[1], feed_sends[3] = run.release([feed_sends[1], feed_sends[3]])
            up_big, down_big = scatter_pair(feed_sends, feed_orders)
        in_low, taps_grad, mix_sums, *ends = mix_bwd(
            run, layer, scal, rows, out_weight, saved, spec, in_w, conv_w, conv_b, skip_bias,
            filt[layer][0], waves, waves_t,
        )
        if layer:
            if above == layers:
                outputs = last_add(run, out_mine, chip_swap(out_send))
            moves = start_sum(ends)
            own_sums = no_sums
            mix_keep, mix_sent = mix_grad(
                run, [parts_order(rising)] * 2, scal, normed, rows, in_low, mixed, True
            )
        else:
            for x in mix_rest[1:]:
                x.step()
            swapped = [core_swap(ends[i]) for i in both]
        filt_out, narrow = filter_bwd(run, layer, length, scal, taps_grad, pos, filter_weights, filt[layer][1])
        if layer == 0:
            up_big.step()
            send, own, own_sums = last_pick(run, scal, ends[2:], swapped, entry)
            there = chip_swap(send)
            down_big.step()
        packs[layer] = pack(
            run, mix_sums, filt_out, narrow, [back[i][0] for i in both], feed_sums, in_sums, own_sums, down_sum
        )
        if layer == 0:
            small = SmallSum(
                run, packs, [1 << i for i in range(left.bit_length() - 1)] + [left * o for o in rising]
            )
            sends = mix_grad(
                run, [parts_order(o) for o in mix_orders], scal, normed, rows, in_low, mixed, False
            )
            small.step()
            sends[1], sends[3] = run.release([sends[1], sends[3]])
            mix_bigs = scatter_pair(sends, mix_orders)
            up_big.step()
            for x in mix_rest[1:]:
                x.step()
            break
        new_grad, new_low, in_sums, new_got, new_back, back_sums = [], [], [], [], [], []

        def norm_half(i):
            a, c, b = norm_back(run, layer, *moves[i], entry[i], grad[i], mixer_norm_gain)
            new_grad.append(a)
            new_low.append(b)
            in_sums.append(c)
            new_got.append(core_swap(b))

        def ffn_half(i):
            below = stored[layer - 1][8]
            new_back.append(
                ffn_bwd(run, layer - 1, new_low[i], new_got[i], feed_up, feed_down, below[i][0], False)
            )

        def sum_half(i):
            back_sums.append(one_sum(new_back[i][2], new_back[i][3]))

        norm_half(0)
        mix_rest[layer] = Scatter(run, run.release([mix_sent])[0], mix_keep, [left * o for o in rising])
        ffn_half(0)
        in_turn(moves[1])
        sum_half(0)
        norm_half(1)
        ffn_half(1)
        in_turn(back_sums[0])
        sum_half(1)
        moves = back_sums
        back = new_back
        down_sum = (in_sums[0] + in_sums[1])[2:3]
        grad, low, got = new_grad, new_low, new_got
    token_grad = last_back(run, 0, scal, own, there, entry, grad, mixer_norm_gain)
    while small.strides:
        small.step()
    down_big.step()
    mix_bigs[0].step()
    small_sums, wide = small.sums()
    wide_got = chip_swap(wide)
    mix_bigs[1].step()
    wide = add_pair(run, wide, wide_got)
    wide_got = core_swap(wide)
    mix_bigs[0].step()
    mix_bigs[1].step()
    (gain, shift, out_bias_g, feed_gain, feed_shift, down_bias_g, in_bias_g, conv_w_g, conv_b_g, skip_g, filt_g,
     up_bias_g, w_in_g, b_in_g, f_in_g, w_mid_g, b_mid_g, f_mid_g) = unpack(
        run, small_sums, add_pair(run, wide, wide_got), feed_up.shape[2]
    )
    up_pair, down_pair = up_big.pair(), down_big.pair()
    if left == 1:
        up_first, down_first = [[(a, 0) for a in pair] for pair in (up_pair, down_pair)]
    else:
        up_first, down_first = [[(share_out(pair), 0)] for pair in (up_pair, down_pair)]
    up_g = ffn_finish(run, [up_first] + [[(a, 0)] for a in feed_shares[1:]], False)
    down_g = ffn_finish(run, [down_first] + [[(a, 1)] for a in feed_shares[1:]], True)
    mix_pairs = [x.pair() for x in mix_bigs]
    if left == 1:
        arrays = [a for pair in mix_pairs for a in pair]
        first = [[(2 * k, (0, i)), (2 * k + 1, (0, i))] for k in both for i in both]
    else:
        arrays = [share_out(pair) for pair in mix_pairs]
        first = [[(k, i)] for k in both for i in both]
    plan = [first]
    for x in mix_rest[1:]:
        pair = x.pair()
        if left == 1:
            plan.append([[(len(arrays), (0, i)), (len(arrays) + 1, (0, i))] for i in range(STREAMS + 1)])
            arrays += pair
        else:
            plan.append([[(len(arrays), i)] for i in range(STREAMS + 1)])
            arrays.append(share_out(pair))
    in_g, out_g = mix_finish(run, arrays, plan)
    return (
        outputs[None],
        token_grad[None],
        gain,
        shift,
        in_g.transpose(0, 2, 1, 3),
        in_bias_g.transpose(1, 0, 2),
        conv_w_g.transpose(2, 0, 1, 3),
        conv_b_g.transpose(1, 0, 2),
        w_in_g,
        b_in_g,
        f_in_g,
        w_mid_g,
        b_mid_g,
        f_mid_g,
        filt_g,
        skip_g,
        out_g,
        out_bias_g,
        feed_gain,
        feed_shift,
        up_g,
        up_bias_g,
        down_g,
        down_bias_g,
    )


def solution(mesh):
    in_specs = (
        P("dp", "mp", None),
        P("dp", None),
        P("dp", "mp", None),
        P(),
        P(),
        P(None, None, None, "mp"),
        P(None, None, "mp"),
        P(None, None, None, "mp"),
        P(None, None, "mp"),
        P(),
        P(),
        P(),
        P(),
        P(),
        P(),
        P(None, None, "mp"),
        P(None, "mp"),
        P(None, "mp", None),
        P(),
        P(),
        P(),
        P(None, None, "mp"),
        P(None, "mp"),
        P(None, "mp", None),
        P(),
    )
    out_specs = (
        P("dp", "mp", None),
        P("dp", "mp", None),
        P(),
        P(),
        P(None, "dp", None, "mp"),
        P(None, None, "mp"),
        P(None, None, None, "mp"),
        P(None, None, "mp"),
        P(),
        P(),
        P(),
        P(),
        P(),
        P(),
        P(None, None, "mp"),
        P(None, "mp"),
        P(None, "mp", "dp"),
        P(),
        P(),
        P(),
        P(None, "dp", "mp"),
        P(None, "mp"),
        P(None, "mp", "dp"),
        P(),
    )
    return jax.shard_map(shards, mesh=mesh, in_specs=in_specs, out_specs=out_specs, check_vma=False)
```

```python
import functools
import math

import jax
import jax.numpy as jnp
import ml_dtypes
import numpy as np
from jax import lax
from jax.experimental import pallas as pl
from jax.experimental.pallas import tpu as pltpu
from jax.sharding import PartitionSpec as P

D = 1024
POS = 33
FILT = 64
REACH = 896
WAVES = 2 * REACH
SHORT = 3
STREAMS = 3
TILE = 128
CHUNK = 128
PARTS = D // CHUNK

f32 = jnp.float32
bf16 = jnp.bfloat16
highest = lax.Precision.HIGHEST
norm_eps = 1e-05
slow_rate = math.log(100.0) / 1.5
fast_rate = math.log(100.0) / 0.3
GELU_A = math.sqrt(2.0 / math.pi)
GELU_B = 0.044715
SPARE_MB = 3

ROW_IN_BIAS = 0
ROW_CONV_W = 3
ROW_CONV_B = 12
ROW_SKIP = 15
ROW_FILTER = 16
ROW_UP_BIAS = 80
ROW_WIDE = 84
ROW_NARROW = 116
PACK_ROWS = 144
NARROW_ROWS = 112
NARROW_GROUP = 28
NB_IN, NF_IN, NW_MID, NB_MID, NF_MID = 33, 34, 35, 99, 100


def wave_table(length):
    freq = 2 * np.arange(REACH, dtype=np.int64) + 1
    phase = (freq[:, None] * np.arange(length, dtype=np.int64)[None, :]) % (2 * WAVES)
    angle = phase.astype(np.float64) * (math.pi / WAVES)
    return np.concatenate([np.cos(angle), -np.sin(angle)], axis=0).astype(ml_dtypes.bfloat16)


def position_table(length):
    places = np.arange(REACH, dtype=np.float64)
    count = (POS - 1) // 2
    bands = 0.0001 + np.arange(count, dtype=np.float64) * ((count - 1 - 0.0001) / (count - 1))
    phases = bands[:, None] * places[None, :] * (2.0 * math.pi / length)
    table = np.zeros((64, REACH), np.float32)
    table[0] = places / (length - 1)
    table[1 : 1 + count] = np.cos(phases)
    table[1 + count : POS] = -np.sin(phases)
    return table


def core_swap(x):
    size = lax.axis_size("mp")
    return lax.ppermute(x, "mp", [(i, i ^ 1) for i in range(size)])


def chip_swap(x):
    size = lax.axis_size("mp")
    return lax.ppermute(x, "mp", [(i, i ^ 2) for i in range(size)])


def dot(a, b):
    return jnp.dot(a, b, preferred_element_type=f32)


def dot_rows(a, b):
    return lax.dot_general(a, b, (((0,), (0,)), ((), ())), preferred_element_type=f32)


def dot_cols(a, b):
    return lax.dot_general(a, b, (((1,), (1,)), ((), ())), preferred_element_type=f32)


def fine(a, b, dims):
    return lax.dot_general(a, b, (dims, ((), ())), precision=highest, preferred_element_type=f32)


def whole(shape):
    return pl.BlockSpec(tuple(shape), lambda *_: (0,) * len(shape))


def layer_of(stacked, layer):
    shape = stacked.shape[1:]
    return pl.BlockSpec((None, *shape), lambda *_: (layer,) + (0,) * len(shape))


SMALL = pl.BlockSpec(memory_space=pltpu.SMEM)
FAR = pl.BlockSpec(memory_space=pl.ANY)
MAIN = pl.BlockSpec(memory_space=pltpu.HBM)


def struct(shape, dtype):
    return jax.ShapeDtypeStruct(tuple(shape), dtype)


class Chain:
    def __init__(self):
        self.token = None

    def release(self, arrays):
        *results, self.token = pl.pallas_call(
            lambda *refs: None,
            grid=(1,),
            out_shape=[pltpu.HBM(a.shape, a.dtype) for a in arrays] + [pltpu.HBM((8, 128), f32)],
            in_specs=[FAR] * (len(arrays) + 1),
            out_specs=[MAIN] * (len(arrays) + 1),
            input_output_aliases={i: i for i in range(len(arrays))},
            cost_estimate=pl.CostEstimate(flops=1, bytes_accessed=1, transcendentals=0),
            name="release",
        )(*[stay(a) for a in arrays], stay(self.token))
        return results

    def __call__(self, kernel, operands, outs, scratch=(), far=0, spill=0, name=None, after=()):
        arrays = [a for a, _ in operands]
        specs = [whole(a.shape) if s is None else s for a, s in operands]
        main = far + spill
        out_specs = [MAIN if i < main else whole(o.shape) for i, o in enumerate(outs)]
        spilled = [pltpu.VMEM(o.shape, o.dtype) for o in outs[far:main]]
        scratch = [*scratch, *spilled] + ([pltpu.SemaphoreType.DMA((spill,))] if spill else [])
        held = 0
        for a, s in list(zip(arrays, specs)) + list(zip(outs, out_specs)):
            if s is not SMALL and s is not FAR and s is not MAIN:
                held += math.prod(x for x in s.block_shape if x is not None) * a.dtype.itemsize
        for s in scratch:
            if getattr(s, "memory_space", None) == pltpu.VMEM:
                held += math.prod(s.shape) * jnp.dtype(s.dtype).itemsize
        count, given = len(arrays), len(outs)
        tokens = ([] if self.token is None else [stay(self.token)]) + list(after)

        def body(*refs):
            ins, refs = refs[:count], refs[count + len(tokens) :]
            results, rest = refs[:given], refs[given + 1 :]
            if spill:
                rest, buffers, sems = rest[: -spill - 1], rest[-spill - 1 : -1], rest[-1]
                kernel(*ins, *results[:far], *buffers, *results[main:], *rest)
                copies = [
                    pltpu.make_async_copy(buffers[i], results[far + i], sems.at[i]) for i in range(spill)
                ]
                for copy in copies:
                    copy.start()
                for copy in copies:
                    copy.wait()
            else:
                kernel(*ins, *results, *rest)

        *results, self.token = pl.pallas_call(
            body,
            grid=(1,),
            out_shape=[pltpu.HBM(o.shape, o.dtype) if i < main else o for i, o in enumerate(outs)]
            + [pltpu.HBM((8, 128), f32)],
            in_specs=specs + [FAR] * len(tokens),
            out_specs=out_specs + [MAIN],
            scratch_shapes=scratch,
            compiler_params=pltpu.CompilerParams(vmem_limit_bytes=held + SPARE_MB * 1024 * 1024),
            cost_estimate=pl.CostEstimate(flops=1, bytes_accessed=1, transcendentals=0),
            name=name,
        )(*arrays, *tokens)
        return results


def unit_of(values):
    center = values - jnp.mean(values, axis=-1, keepdims=True)
    spread = jnp.mean(center * center, axis=-1, keepdims=True)
    rstd = lax.rsqrt(spread + norm_eps)
    return center * rstd, rstd


def row_tiles(count, size=32):
    return [slice(i * size, (i + 1) * size) for i in range(count // size)]


def stay(x):
    return pltpu.with_memory_space_constraint(x, pltpu.HBM)


def first_norm_kernel(scal, mine, other, gain, shift, cot, low_a, low_b, res_a, res_b, cot_out):
    chip = scal[2]
    cot_out[...] = cot[...]
    for rows in row_tiles(mine.shape[0]):
        a, b = mine[rows, :].astype(f32), other[rows, :].astype(f32)
        for values, res, low in (
            (jnp.where(chip == 0, a, b), res_a, low_a),
            (jnp.where(chip == 0, b, a), res_b, low_b),
        ):
            res[rows, :] = values
            unit, _ = unit_of(values)
            low[rows, :] = (unit * gain[0:1, :] + shift[0:1, :]).astype(bf16)


def first_norm(run, scal, mine, other, gain, shift, cot):
    block = mine.shape[0]
    return run(
        first_norm_kernel,
        [(scal, SMALL)] + [(a, None) for a in (mine, other, gain, shift, cot)],
        [struct((block, D), bf16)] * 2 + [struct((block, D), f32)] * 2 + [struct((block, D), bf16)],
        spill=2,
        name="first_norm",
    )


def first_grad_kernel(scal, mine, other, sums, low_a, low_b):
    chip = scal[2]
    total = jnp.zeros((8, D), f32)
    for rows in row_tiles(mine.shape[0]):
        a, b = mine[rows, :], other[rows, :]
        low_a[rows, :] = jnp.where(chip == 0, a, b)
        low_b[rows, :] = jnp.where(chip == 0, b, a)
        total = total + fold(a.astype(f32)) + fold(b.astype(f32))
    sums[...] = 0.5 * jnp.sum(total, axis=0, keepdims=True)


def first_grad(run, scal, mine, other):
    block = mine.shape[0]
    return run(
        first_grad_kernel,
        [(scal, SMALL), (mine, None), (other, None)],
        [struct((1, D), f32)] + [struct((block, D), bf16)] * 2,
        spill=1,
        name="first_grad",
    )


def add_kernel(keep, got, out):
    for rows in row_tiles(keep.shape[0], 64):
        out[rows, :] = (keep[rows, :] + got[rows, :].astype(f32)).astype(out.dtype)


def add_low(run, keep, got, after=()):
    out = [struct(keep.shape, bf16)]
    return run(add_kernel, [(keep, None), (got, None)], out, name="add_low", after=after)[0]


def last_pick_kernel(scal, keep_a, got_a, val_a, keep_b, got_b, val_b, send, mine, sums):
    totals = [jnp.zeros((8, D), f32) for _ in range(2)]
    near_a = scal[2] == 0
    for rows in row_tiles(mine.shape[0]):
        parts = []
        for keep, got, values in ((keep_a, got_a, val_a), (keep_b, got_b, val_b)):
            total = keep[rows, :] + got[rows, :].astype(f32)
            unit, _ = unit_of(values[rows, :])
            totals[0] = totals[0] + fold(total * unit)
            totals[1] = totals[1] + fold(total)
            parts.append(total)
        mine[rows, :] = jnp.where(near_a, parts[0], parts[1])
        send[rows, :] = jnp.where(near_a, parts[1], parts[0]).astype(bf16)
    for i, total in enumerate(totals):
        sums[i : i + 1, :] = jnp.sum(total, axis=0, keepdims=True)
    sums[2:8, :] = jnp.zeros((6, D), f32)


def last_pick(run, scal, keeps, gots, entry):
    shape = keeps[0].shape
    operands = [a for i in range(2) for a in (keeps[i], gots[i], entry[i])]
    return run(
        last_pick_kernel,
        [(scal, SMALL)] + [(a, None) for a in operands],
        [struct(shape, bf16), struct(shape, f32), struct((8, D), f32)],
        name="last_pick",
    )


def add_norm_kernel(layer, norm_layer, here, there, residual, bias, gain, shift, low, out):
    for rows in row_tiles(here.shape[0]):
        values = residual[rows, :] + here[rows, :].astype(f32) + there[rows, :].astype(f32)
        values = values + bias[layer : layer + 1, :]
        out[rows, :] = values
        unit, _ = unit_of(values)
        low[rows, :] = (
            unit * gain[norm_layer : norm_layer + 1, :] + shift[norm_layer : norm_layer + 1, :]
        ).astype(bf16)


def add_norm(run, layer, norm_layer, here, there, residual, bias, gain, shift, spill=0):
    shape = here.shape
    return run(
        functools.partial(add_norm_kernel, layer, norm_layer),
        [(a, None) for a in (here, there, residual, bias, gain, shift)],
        [struct(shape, bf16), struct(shape, f32)],
        spill=spill,
        name="add_norm",
    )


def pick_kernel(layer, scal, keep_a, got_a, keep_b, got_b, mid_a, mid_b, bias, send, mine):
    def pick(near, far_away):
        keep, got, middle = near
        for rows in row_tiles(mine.shape[0]):
            values = keep[rows, :] + got[rows, :].astype(f32) + middle[rows, :]
            mine[rows, :] = values + bias[layer : layer + 1, :]
            send[rows, :] = (far_away[0][rows, :] + far_away[1][rows, :].astype(f32)).astype(bf16)

    @pl.when(scal[2] == 0)
    def _():
        pick((keep_a, got_a, mid_a), (keep_b, got_b))

    @pl.when(scal[2] != 0)
    def _():
        pick((keep_b, got_b, mid_b), (keep_a, got_a))


def pick_outputs(run, layer, scal, keeps, gots, middles, bias):
    shape = keeps[0].shape
    operands = (keeps[0], gots[0], keeps[1], gots[1], *middles, bias)
    return run(
        functools.partial(pick_kernel, layer),
        [(scal, SMALL)] + [(a, None) for a in operands],
        [struct(shape, bf16), struct(shape, f32)],
        name="pick_outputs",
    )


def last_add_kernel(mine, there, out):
    for rows in row_tiles(out.shape[0], 64):
        out[rows, :] = mine[rows, :] + there[rows, :].astype(f32)


def last_add(run, mine, there):
    return run(last_add_kernel, [(mine, None), (there, None)], [struct(mine.shape, f32)], name="last_add")[0]


def fold(x):
    return sum(x[8 * i : 8 * i + 8, :] for i in range(x.shape[0] // 8))


def norm_back_kernel(layer, here, there, values, grad, gain, out, sums, low):
    totals = [jnp.zeros((8, D), f32) for _ in range(3)]
    for rows in row_tiles(here.shape[0], 16):
        dy = here[rows, :].astype(f32) + there[rows, :].astype(f32)
        unit, rstd = unit_of(values[rows, :])
        scaled = dy * gain[layer : layer + 1, :]
        into = rstd * (
            scaled
            - jnp.mean(scaled, axis=-1, keepdims=True)
            - unit * jnp.mean(scaled * unit, axis=-1, keepdims=True)
        )
        new = grad[rows, :].astype(f32) + into
        out[rows, :] = new
        low[rows, :] = new.astype(bf16)
        for k, part in enumerate((dy * unit, dy, new)):
            totals[k] = totals[k] + fold(part)
    for k, total in enumerate(totals):
        sums[k : k + 1, :] = 0.5 * jnp.sum(total, axis=0, keepdims=True)
    sums[3:8, :] = jnp.zeros((5, D), f32)


def norm_back(run, layer, here, there, values, grad, gain, spill=0):
    shape = here.shape
    return run(
        functools.partial(norm_back_kernel, layer),
        [(a, None) for a in (here, there, values, grad, gain)],
        [struct(shape, f32), struct((8, D), f32), struct(shape, bf16)],
        spill=2 + spill,
        name="norm_back",
    )


def last_back_kernel(layer, scal, mine, there, val_a, val_b, grad_a, grad_b, gain, out):
    near_a = scal[2] == 0
    for rows in row_tiles(out.shape[0], 16):
        dy = mine[rows, :] + there[rows, :].astype(f32)
        unit, rstd = unit_of(jnp.where(near_a, val_a[rows, :], val_b[rows, :]))
        scaled = dy * gain[layer : layer + 1, :]
        into = rstd * (
            scaled
            - jnp.mean(scaled, axis=-1, keepdims=True)
            - unit * jnp.mean(scaled * unit, axis=-1, keepdims=True)
        )
        out[rows, :] = jnp.where(near_a, grad_a[rows, :], grad_b[rows, :]) + into


def last_back(run, layer, scal, mine, there, entry, grad, gain):
    return run(
        functools.partial(last_back_kernel, layer),
        [(scal, SMALL), (mine, None), (there, None)]
        + [(a, None) for a in (*entry, *grad, gain)],
        [struct(mine.shape, f32)],
        name="last_back",
    )[0]


def ffn_fwd_kernel(
    layer, own, got, up_far, up_bias, down_far, pre_far, hid_far, sent, keep, both, pre, hid, up, down, sems
):
    copy_up = pltpu.make_async_copy(up_far.at[layer], up, sems.at[2])
    copy_down = pltpu.make_async_copy(down_far.at[layer], down, sems.at[3])
    copy_up.start()
    copy_down.start()
    half = own.shape[0]
    both[:half, :] = own[...]
    both[half:, :] = got[...]
    copy_up.wait()
    v = dot(both[...], up[...]) + up_bias[layer : layer + 1, :]
    pre[...] = v.astype(bf16)
    hid[...] = (0.5 * v * (1.0 + jnp.tanh(GELU_A * (v + GELU_B * v * v * v)))).astype(bf16)
    copies = [
        pltpu.make_async_copy(a, b, sems.at[i]) for i, (a, b) in enumerate(((pre, pre_far), (hid, hid_far)))
    ]
    for copy in copies:
        copy.start()
    copy_down.wait()
    total = dot(hid[...], down[...])
    keep[...] = total[:half, :]
    sent[...] = total[half:, :].astype(bf16)
    for copy in copies:
        copy.wait()


def ffn_fwd(run, layer, own, got, up, up_bias, down):
    half, width = own.shape[0], up.shape[2]
    return run(
        functools.partial(ffn_fwd_kernel, layer),
        [(own, None), (got, None), (up, FAR), (up_bias, None), (down, FAR)],
        [
            struct((2 * half, width), bf16),
            struct((2 * half, width), bf16),
            struct((half, D), bf16),
            struct((half, D), f32),
        ],
        scratch=[
            pltpu.VMEM((2 * half, D), bf16),
            pltpu.VMEM((2 * half, width), bf16),
            pltpu.VMEM((2 * half, width), bf16),
            pltpu.VMEM((D, width), bf16),
            pltpu.VMEM((width, D), bf16),
            pltpu.SemaphoreType.DMA((4,)),
        ],
        far=2,
        name="ffn_fwd",
    )


def ffn_bwd_kernel(
    layer, own, got, up_far, down_far, pre_far, up_low_far, bias_sum, sent, keep,
    both, up, down, pre, up_low, sems,
):
    ins = ((down_far.at[layer], down), (pre_far, pre), (up_far.at[layer], up))
    copies = [pltpu.make_async_copy(a, b, sems.at[i]) for i, (a, b) in enumerate(ins)]
    for copy in copies:
        copy.start()
    half = own.shape[0]
    both[:half, :] = own[...]
    both[half:, :] = got[...]
    copies[0].wait()
    copies[1].wait()
    v = pre[...].astype(f32)
    t = jnp.tanh(GELU_A * (v + GELU_B * v * v * v))
    slope = 0.5 * (1.0 + t) + 0.5 * v * (1.0 - t * t) * (GELU_A * (1.0 + 3.0 * GELU_B * v * v))
    g = dot_cols(both[...], down[...]) * slope
    bias_sum[...] = jnp.sum(g, axis=0, keepdims=True)
    up_low[...] = g.astype(bf16)
    copy_low = pltpu.make_async_copy(up_low, up_low_far, sems.at[3])
    copy_low.start()
    copies[2].wait()
    total = dot_cols(up_low[...], up[...])
    keep[...] = total[:half, :]
    sent[...] = total[half:, :].astype(bf16)
    copy_low.wait()


def ffn_bwd(run, layer, own, got, up, down, pre, near):
    half, width = own.shape[0], up.shape[2]
    if not near:
        up, down = stay(up), stay(down)
    up_low, bias_sum, sent, keep = run(
        functools.partial(ffn_bwd_kernel, layer),
        [(own, None), (got, None), (up, FAR), (down, FAR), (stay(pre), FAR)],
        [
            struct((2 * half, width), bf16),
            struct((1, width), f32),
            struct((half, D), bf16),
            struct((half, D), f32),
        ],
        scratch=[
            pltpu.VMEM((2 * half, D), bf16),
            pltpu.VMEM((D, width), bf16),
            pltpu.VMEM((width, D), bf16),
            pltpu.VMEM((2 * half, width), bf16),
            pltpu.VMEM((2 * half, width), bf16),
            pltpu.SemaphoreType.DMA((4,)),
        ],
        far=1,
        spill=1,
        name="ffn_bwd",
    )
    return bias_sum, up_low, sent, keep


def sine(x, both=False):
    turns = jnp.floor(x * (1.0 / math.pi) + 0.5)
    rest = (x - turns * 3.140625) - turns * 9.67653589793e-4
    sign = 1.0 - 2.0 * (turns - 2.0 * jnp.floor(turns * 0.5))
    sq = rest * rest
    odd = -1.0 / 39916800.0
    for c in (1.0 / 362880.0, -1.0 / 5040.0, 1.0 / 120.0, -1.0 / 6.0, 1.0):
        odd = odd * sq + c
    value = sign * rest * odd
    if not both:
        return value
    even = 1.0 / 479001600.0
    for c in (-1.0 / 3628800.0, 1.0 / 40320.0, -1.0 / 720.0, 1.0 / 24.0, -0.5, 1.0):
        even = even * sq + c
    return value, sign * even


def decay(spot, channels, length):
    lane = lax.broadcasted_iota(jnp.int32, (1, channels), 1) + spot * channels
    row = lax.broadcasted_iota(jnp.int32, (REACH, channels), 0).astype(f32)
    rate = slow_rate + (fast_rate - slow_rate) * lane.astype(f32) / (D - 1)
    return jnp.exp(-(row * (1.0 / (length - 1))) * rate)


def columns(layer, *refs):
    rows = [r[layer : layer + 1, :] for r in refs] + [jnp.zeros((8 - len(refs), FILT), f32)]
    wide = jnp.concatenate([jnp.concatenate(rows, axis=0), jnp.zeros((8, 128 - FILT), f32)], axis=1).T
    return [wide[:FILT, i : i + 1] for i in range(len(refs))]


def filter_fwd_kernel(
    layer, length, scal, pos, w_in, b_in, f_in, w_mid, b_mid, f_mid, w_out, waves, spec, kept
):
    channels = w_out.shape[1]
    b_in, f_in, b_mid, f_mid = columns(layer, b_in, f_in, b_mid, f_mid)
    z = fine(w_in[...], pos[:POS, :], ((0,), (0,))) + b_in
    h, c = sine(f_in * z, both=True)
    kept[0] = z
    kept[1] = h
    kept[2] = c
    z = fine(w_mid[...], h, ((0,), (0,))) + b_mid
    h, c = sine(f_mid * z, both=True)
    kept[3] = z
    kept[4] = h
    kept[5] = c
    taps = fine(h, w_out[...], ((0,), (0,))) * decay(scal[4], channels, length)
    spec[...] = dot(waves[:, :REACH], taps.astype(bf16)) * (2.0 / WAVES)


def filter_fwd(run, layer, length, scal, pos, weights, waves):
    channels = weights[-1].shape[2]
    return run(
        functools.partial(filter_fwd_kernel, layer, length),
        [(scal, SMALL), (pos, None)]
        + [(a, layer_of(a, layer) if a.ndim == 3 else None) for a in weights]
        + [(waves, None)],
        [struct((WAVES, channels), f32), struct((6, FILT, REACH), f32)],
        spill=2,
        name="filter_fwd",
    )


def filter_bwd_kernel(layer, length, scal, taps_grad, pos, f_in, w_mid, f_mid, w_out, kept, by_chan, narrow):
    channels = w_out.shape[1]
    dt = taps_grad[...] * decay(scal[4], channels, length)
    by_chan[...] = fine(kept[4], dt, ((1,), (0,)))
    f_in, f_mid = columns(layer, f_in, f_mid)
    dh = fine(w_out[...], dt, ((1,), (1,)))
    c = kept[5] * dh
    dz = c * f_mid
    narrow[NW_MID : NW_MID + FILT, :] = fine(kept[1], dz, ((1,), (1,)))
    mid_sums = jnp.concatenate(
        [jnp.sum(dz, axis=1, keepdims=True), jnp.sum(c * kept[3], axis=1, keepdims=True)], axis=1
    )
    dh = fine(w_mid[...], dz, ((1,), (0,)))
    c = kept[2] * dh
    dz = c * f_in
    narrow[:POS, :] = fine(pos[...], dz, ((1,), (1,)))[:POS, :]
    in_sums = jnp.concatenate(
        [jnp.sum(dz, axis=1, keepdims=True), jnp.sum(c * kept[0], axis=1, keepdims=True)], axis=1
    )
    sums = jnp.concatenate([in_sums, mid_sums, jnp.zeros((FILT, 124), f32)], axis=1).T
    narrow[NB_IN : NB_IN + 2, :] = sums[0:2, :]
    narrow[NB_MID : NB_MID + 2, :] = sums[2:4, :]
    narrow[NF_MID + 1 :, :] = jnp.zeros((NARROW_ROWS - NF_MID - 1, FILT), f32)


def filter_bwd(run, layer, length, scal, taps_grad, pos, weights, kept):
    _, _, f_in, w_mid, _, f_mid, w_out = weights
    return run(
        functools.partial(filter_bwd_kernel, layer, length),
        [(scal, SMALL), (taps_grad, None), (pos, None)]
        + [(a, layer_of(a, layer) if a.ndim == 3 else None) for a in (f_in, w_mid, f_mid, w_out)]
        + [(kept, None)],
        [struct((FILT, w_out.shape[2]), f32), struct((NARROW_ROWS, FILT), f32)],
        name="filter_bwd",
    )


def lagged(ref, tile, cols, lag, before=None):
    if tile:
        return ref[tile * TILE - lag : (tile + 1) * TILE - lag, cols]
    if before is None:
        head = jnp.zeros((lag, cols.stop - cols.start), f32)
    else:
        head = before[before.shape[0] - lag :, cols]
    return jnp.concatenate([head, ref[: TILE - lag, cols]], axis=0)


def ahead(ref, tile, cols, lag, last):
    if tile < last:
        return ref[tile * TILE + lag : (tile + 1) * TILE + lag, cols]
    empty = jnp.zeros((lag, cols.stop - cols.start), f32)
    return jnp.concatenate([ref[tile * TILE + lag : (tile + 1) * TILE, cols], empty], axis=0)


def place(tile, first, shift=0):
    row = lax.broadcasted_iota(jnp.int32, (TILE, 1), 0) + (tile * TILE + shift)
    in_first = row < first
    return in_first, jnp.where(in_first, row, row - first)


def short_tile(proj, conv_w, conv_b, layer, tile, stream, offset, channels, before=None):
    cols = slice(stream * channels, (stream + 1) * channels)
    row = slice(layer, layer + 1)
    total = proj[tile * TILE : (tile + 1) * TILE, cols] * conv_w[stream, 0, row, :]
    total = total + conv_b[stream, row, :]
    for lag in range(1, SHORT):
        weight = conv_w[stream, lag, row, :]
        total = total + jnp.where(offset >= lag, lagged(proj, tile, cols, lag, before) * weight, 0.0)
    return total


def tile_rows(tile):
    return slice(tile * TILE, (tile + 1) * TILE)


def halves(own_a, own_b, got_a, got_b, core):
    block = own_a.shape[0]
    out = []
    for half, (own, got) in enumerate(((own_a, got_a), (own_b, got_b))):
        for rows, side in ((own, core), (got, 1 - core)):
            out.append((rows, pl.multiple_of(2 * block * half + side * block, block)))
    return out


def mix_fwd_kernel(layer, half, *refs):
    (scal, in_b, conv_w, conv_b, skip, own_far, got_far, in_w_far, taps_far, out_w_far, waves_far, waves_t_far), refs = (
        refs[:12],
        refs[12:],
    )
    before, prev = None, None
    if half:
        (before, prev), refs = refs[:2], refs[2:]
    (proj_far, longc_far, mixed_far, spec, tail, sent, keep), refs = refs[:7], refs[7:]
    own, got, in_w, waves, waves_t, taps, out_w, proj, gated, mixed, s0, pieces, prod, sems = refs
    block = own.shape[0]
    length = 2 * block
    first_ins = ((own_far, own), (got_far, got), (in_w_far.at[layer], in_w))
    first_copies = [pltpu.make_async_copy(a, b, sems.at[8 + i]) for i, (a, b) in enumerate(first_ins)]
    for copy in first_copies:
        copy.start()
    places = slice(half * length, (half + 1) * length)
    ins = [
        (waves_far.at[:, places], waves),
        (taps_far, taps),
        (waves_t_far.at[places, :], waves_t),
        (out_w_far.at[layer], out_w),
    ]
    copies = [pltpu.make_async_copy(a, b, sems.at[i]) for i, (a, b) in enumerate(ins)]
    outs = ((proj, proj_far), (gated, longc_far), (mixed, mixed_far))
    copy_proj, copy_long, copy_mixed = [
        pltpu.make_async_copy(a, b, sems.at[4 + i]) for i, (a, b) in enumerate(outs)
    ]
    for copy in copies:
        copy.start()
    for copy in first_copies:
        copy.wait()
    first, core = scal[0], scal[1]
    channels = skip.shape[1]
    row = slice(layer, layer + 1)
    sides = [pl.multiple_of(side * block, block) for side in (core, 1 - core)]
    for rows, at in zip((own, got), sides):
        for stream in range(STREAMS):
            cols = slice(stream * channels, (stream + 1) * channels)
            proj[pl.ds(at, block), cols] = dot(rows[...], in_w[stream]) + in_b[stream, row, :]
    copy_proj.start()
    tail[...] = proj[length - 8 :, :]
    for tile in range(length // TILE):
        rows = tile_rows(tile)
        in_first, offset = place(tile, first, half * length)
        one, two, zero = [
            short_tile(proj, conv_w, conv_b, layer, tile, stream, offset, channels, before)
            for stream in (1, 2, 0)
        ]
        g = one * two
        gated[rows, :] = g
        s0[rows, :] = zero
        pieces[rows, :channels] = jnp.where(in_first, g, 0.0).astype(bf16)
        pieces[rows, channels:] = jnp.where(in_first, 0.0, g).astype(bf16)
    copies[0].wait()
    copies[1].wait()
    steps = 2
    part = REACH // steps
    for step in range(steps):
        lo = slice(step * part, (step + 1) * part)
        hi = slice(REACH + step * part, REACH + (step + 1) * part)
        for seg in range(2):
            cols = slice(seg * channels, (seg + 1) * channels)
            re = dot(waves[lo, :], pieces[:, cols])
            im = dot(waves[hi, :], pieces[:, cols])
            if half:
                re = re + prev[lo, cols].astype(f32)
                im = im + prev[hi, cols].astype(f32)
            t_re, t_im = taps[lo, :], taps[hi, :]
            spec[lo, cols] = re.astype(bf16)
            spec[hi, cols] = im.astype(bf16)
            prod[lo, cols] = (re * t_re - im * t_im).astype(bf16)
            prod[hi, cols] = (re * t_im + im * t_re).astype(bf16)
    copies[2].wait()
    in_first = lax.broadcasted_iota(jnp.int32, (length, 1), 0) + half * length < first
    a = dot(waves_t[...], prod[:, :channels])
    b = dot(waves_t[...], prod[:, channels:])
    total = jnp.where(in_first, a, b) + skip[row, :] * gated[...]
    gated[...] = total
    mixed[...] = (total * s0[...]).astype(bf16)
    copy_long.start()
    copy_mixed.start()
    copies[3].wait()
    keep[...] = dot(mixed[pl.ds(sides[0], block), :], out_w[...])
    sent[...] = dot(mixed[pl.ds(sides[1], block), :], out_w[...]).astype(bf16)
    for copy in (copy_proj, copy_long, copy_mixed):
        copy.wait()


def mix_fwd(run, layer, half, scal, own, got, in_w, in_b, conv_w, conv_b, skip, taps, out_w, waves, waves_t, prev):
    block, channels = own.shape[0], skip.shape[1]
    length = 2 * block
    extra = [] if prev is None else [(a, None) for a in prev]
    proj, longc, mixed, spec, tail, sent, keep = run(
        functools.partial(mix_fwd_kernel, layer, half),
        [(scal, SMALL)]
        + [(a, None) for a in (in_b, conv_w, conv_b, skip)]
        + [(stay(own), FAR), (got, FAR)]
        + [(stay(a), FAR) for a in (in_w, taps, out_w, waves, waves_t)]
        + extra,
        [
            struct((length, STREAMS * channels), f32),
            struct((length, channels), f32),
            struct((length, channels), bf16),
            struct((WAVES, 2 * channels), bf16),
            struct((8, STREAMS * channels), f32),
            struct((block, D), bf16),
            struct((block, D), f32),
        ],
        scratch=[
            pltpu.VMEM((block, D), bf16),
            pltpu.VMEM((block, D), bf16),
            pltpu.VMEM((STREAMS, D, channels), bf16),
            pltpu.VMEM((WAVES, length), bf16),
            pltpu.VMEM((length, WAVES), bf16),
            pltpu.VMEM((WAVES, channels), f32),
            pltpu.VMEM((channels, D), bf16),
            pltpu.VMEM((length, STREAMS * channels), f32),
            pltpu.VMEM((length, channels), f32),
            pltpu.VMEM((length, channels), bf16),
            pltpu.VMEM((length, channels), f32),
            pltpu.VMEM((length, 2 * channels), bf16),
            pltpu.VMEM((WAVES, 2 * channels), bf16),
            pltpu.SemaphoreType.DMA((11,)),
        ],
        far=3,
        spill=half,
        name="mix_fwd",
    )
    return (proj, longc, mixed), (tail, spec), sent, keep


def mix_bwd_kernel(
    layer, scal, conv_w, conv_b, skip, own_a_far, own_b_far, got_a_far, got_b_far, out_w_far,
    proj_a_far, proj_b_far, longc_a_far, longc_b_far, waves_far, spec_far, taps_far, waves_t_far, in_w_far,
    in_low, taps_grad, sums, sent_a, sent_b, keep_a, keep_b,
    own_a, own_b, got_a, got_b, out_w, proj, longc, waves, spec, taps, waves_t, in_w, mgrad, ds, pieces, prod,
    corr, sems,
):
    first_ins = (
        (own_a_far, own_a),
        (own_b_far, own_b),
        (got_a_far, got_a),
        (got_b_far, got_b),
        (out_w_far.at[layer], out_w),
    )
    first_copies = [pltpu.make_async_copy(a, b, sems.at[9 + i]) for i, (a, b) in enumerate(first_ins)]
    for copy in first_copies:
        copy.start()
    half_rows = proj_a_far.shape[0]
    near, later = pl.ds(0, half_rows), pl.ds(half_rows, half_rows)
    ins = (
        (proj_a_far, proj.at[near, :]),
        (longc_a_far, longc.at[near, :]),
        (proj_b_far, proj.at[later, :]),
        (longc_b_far, longc.at[later, :]),
        (waves_far, waves),
        (spec_far, spec),
        (taps_far, taps),
        (waves_t_far, waves_t),
        (in_w_far.at[layer], in_w),
    )
    copies = [pltpu.make_async_copy(a, b, sems.at[i]) for i, (a, b) in enumerate(ins)]
    for copy in copies[:4]:
        copy.start()
    first, core = scal[0], scal[1]
    block = own_a.shape[0]
    channels = skip.shape[1]
    row = slice(layer, layer + 1)
    length = 4 * block
    tiles = length // TILE
    for copy in first_copies:
        copy.wait()
    for copy in copies[4:]:
        copy.start()
    for rows, at in halves(own_a, own_b, got_a, got_b, core):
        mgrad[pl.ds(at, block), :] = dot_cols(rows[...], out_w[...])
    skip_sum = jnp.zeros((1, channels), f32)
    for copy in copies[:4]:
        copy.wait()
    mid, end = slice(channels, 2 * channels), slice(2 * channels, 3 * channels)
    for tile in range(tiles):
        rows = tile_rows(tile)
        in_first, offset = place(tile, first)
        one = short_tile(proj, conv_w, conv_b, layer, tile, 1, offset, channels)
        two = short_tile(proj, conv_w, conv_b, layer, tile, 2, offset, channels)
        ds[rows, mid] = one
        ds[rows, end] = two
        m = mgrad[rows, :]
        r = m * short_tile(proj, conv_w, conv_b, layer, tile, 0, offset, channels)
        mgrad[rows, :] = r
        ds[rows, :channels] = m * longc[rows, :]
        skip_sum = skip_sum + jnp.sum(r * one * two, axis=0, keepdims=True)
        pieces[rows, :channels] = jnp.where(in_first, r, 0.0).astype(bf16)
        pieces[rows, channels:] = jnp.where(in_first, 0.0, r).astype(bf16)
    sums[ROW_SKIP : ROW_SKIP + 1, :] = skip_sum
    for copy in copies[4:7]:
        copy.wait()
    steps = 2
    part = REACH // steps
    for step in range(steps):
        lo = slice(step * part, (step + 1) * part)
        hi = slice(REACH + step * part, REACH + (step + 1) * part)
        corr_re, corr_im = None, None
        for seg in range(2):
            cols = slice(seg * channels, (seg + 1) * channels)
            re = dot(waves[lo, :], pieces[:, cols])
            im = dot(waves[hi, :], pieces[:, cols])
            t_re, t_im = taps[lo, :], taps[hi, :]
            prod[lo, cols] = (re * t_re + im * t_im).astype(bf16)
            prod[hi, cols] = (im * t_re - re * t_im).astype(bf16)
            g_re, g_im = spec[lo, cols].astype(f32), spec[hi, cols].astype(f32)
            c_re = g_re * re + g_im * im
            c_im = g_re * im - g_im * re
            corr_re = c_re if corr_re is None else corr_re + c_re
            corr_im = c_im if corr_im is None else corr_im + c_im
        corr[lo, :] = corr_re.astype(bf16)
        corr[hi, :] = corr_im.astype(bf16)
    copies[7].wait()
    big = 512
    for r in range(length // big):
        rows = slice(r * big, (r + 1) * big)
        in_first = lax.broadcasted_iota(jnp.int32, (big, 1), 0) + r * big < first
        a = dot(waves_t[rows, :], prod[:, :channels])
        b = dot(waves_t[rows, :], prod[:, channels:])
        total = jnp.where(in_first, a, b) + skip[row, :] * mgrad[rows, :]
        one, two = ds[rows, mid], ds[rows, end]
        ds[rows, mid] = total * two
        ds[rows, end] = total * one
    for stream in range(STREAMS):
        cols = slice(stream * channels, (stream + 1) * channels)
        at = stream * SHORT
        bias_sum = jnp.zeros((1, channels), f32)
        in_sum = jnp.zeros((1, channels), f32)
        lag_sums = [jnp.zeros((1, channels), f32) for _ in range(SHORT)]
        for tile in range(tiles):
            rows = tile_rows(tile)
            _, offset = place(tile, first)
            d = ds[rows, cols]
            p = proj[rows, cols]
            total = d * conv_w[stream, 0, row, :]
            bias_sum = bias_sum + jnp.sum(d, axis=0, keepdims=True)
            lag_sums[0] = lag_sums[0] + jnp.sum(d * p, axis=0, keepdims=True)
            for lag in range(1, SHORT):
                _, later = place(tile, first, lag)
                moved = jnp.where(later >= lag, ahead(ds, tile, cols, lag, tiles - 1), 0.0)
                total = total + moved * conv_w[stream, lag, row, :]
                lag_sums[lag] = lag_sums[lag] + jnp.sum(moved * p, axis=0, keepdims=True)
            in_sum = in_sum + jnp.sum(total, axis=0, keepdims=True)
            in_low[rows, cols] = total.astype(bf16)
        sums[ROW_IN_BIAS + stream : ROW_IN_BIAS + stream + 1, :] = in_sum
        sums[ROW_CONV_B + stream : ROW_CONV_B + stream + 1, :] = bias_sum
        for lag in range(SHORT):
            sums[ROW_CONV_W + at + lag : ROW_CONV_W + at + lag + 1, :] = lag_sums[lag]

    def into(at):
        rows = pl.ds(at, block)
        total = dot_cols(in_low[rows, :channels], in_w[0])
        for stream in range(1, STREAMS):
            cols = slice(stream * channels, (stream + 1) * channels)
            total = total + dot_cols(in_low[rows, cols], in_w[stream])
        return total

    copies[8].wait()
    for half, (sent, keep) in enumerate(((sent_a, keep_a), (sent_b, keep_b))):
        at = pl.multiple_of(2 * block * half + (1 - core) * block, block)
        sent[...] = into(at).astype(bf16)
        at = pl.multiple_of(2 * block * half + core * block, block)
        keep[...] = into(at)
    taps_grad[...] = dot(waves_t[:REACH, :], corr[...]) * (2.0 / WAVES)


def mix_bwd(run, layer, scal, rows, out_w, saved, spec, in_w, conv_w, conv_b, skip, taps, waves, waves_t):
    block, channels = rows[0].shape[0], skip.shape[1]
    length = 4 * block
    return run(
        functools.partial(mix_bwd_kernel, layer),
        [(scal, SMALL)]
        + [(a, None) for a in (conv_w, conv_b, skip)]
        + [(stay(a), FAR) for a in rows[:2]]
        + [(a, FAR) for a in rows[2:]]
        + [(stay(out_w), FAR)]
        + [(stay(a), FAR) for a in (saved[0][0], saved[1][0], saved[0][1], saved[1][1], waves, spec, taps, waves_t, in_w)],
        [
            struct((length, STREAMS * channels), bf16),
            struct((REACH, channels), f32),
            struct((16, channels), f32),
            struct((block, D), bf16),
            struct((block, D), bf16),
            struct((block, D), f32),
            struct((block, D), f32),
        ],
        scratch=[
            pltpu.VMEM((block, D), bf16),
            pltpu.VMEM((block, D), bf16),
            pltpu.VMEM((block, D), bf16),
            pltpu.VMEM((block, D), bf16),
            pltpu.VMEM((channels, D), bf16),
            pltpu.VMEM((length, STREAMS * channels), f32),
            pltpu.VMEM((length, channels), f32),
            pltpu.VMEM((WAVES, length), bf16),
            pltpu.VMEM((WAVES, 2 * channels), bf16),
            pltpu.VMEM((WAVES, channels), f32),
            pltpu.VMEM((length, WAVES), bf16),
            pltpu.VMEM((STREAMS, D, channels), bf16),
            pltpu.VMEM((length, channels), f32),
            pltpu.VMEM((length, STREAMS * channels), f32),
            pltpu.VMEM((length, 2 * channels), bf16),
            pltpu.VMEM((WAVES, 2 * channels), bf16),
            pltpu.VMEM((WAVES, channels), bf16),
            pltpu.SemaphoreType.DMA((14,)),
        ],
        name="mix_bwd",
    )


def parts_order(strides):
    bits = len(strides)
    return [sum(((part >> (bits - 1 - i)) & 1) * s for i, s in enumerate(strides)) for part in range(1 << bits)]


def spread_columns(source, target, at, index, order):
    for part, step in enumerate(order):
        cols = pl.ds(pl.multiple_of((index ^ step) * CHUNK, CHUNK), CHUNK)
        target[at, part * CHUNK : (part + 1) * CHUNK] = source[:, cols]


def ffn_grad_kernel(orders, scal, *refs):
    feeds, lows = refs[0:4], refs[4:8]
    (up_a, up_b, hid_a, hid_b), outs, (left, right) = refs[8:12], refs[12:16], refs[16:18]
    block = feeds[0].shape[0]
    index = scal[3]
    for k, (source, (rhs_a, rhs_b)) in enumerate(((feeds, (up_a, up_b)), (lows, (hid_a, hid_b)))):
        right[: 2 * block, :] = rhs_a[...]
        right[2 * block :, :] = rhs_b[...]
        for i in range(4):
            spread_columns(source[i], left, slice(i * block, (i + 1) * block), index, orders[k])
        for half in range(2):
            out = outs[2 * k + half]
            wide = PARTS // 2 * CHUNK
            got = dot_rows(left[:, half * wide : (half + 1) * wide], right[...]).astype(bf16)
            for part in range(PARTS // 2):
                out[part] = got[part * CHUNK : (part + 1) * CHUNK, :]


def ffn_whole_kernel(*refs):
    feeds, lows = refs[0:4], refs[4:8]
    (up_a, up_b, hid_a, hid_b), out, (left, right) = refs[8:12], refs[12], refs[13:15]
    block = feeds[0].shape[0]
    for k, (source, (rhs_a, rhs_b)) in enumerate(((feeds, (up_a, up_b)), (lows, (hid_a, hid_b)))):
        right[: 2 * block, :] = rhs_a[...]
        right[2 * block :, :] = rhs_b[...]
        for i in range(4):
            left[i * block : (i + 1) * block, :] = source[i][...]
        for half in range(2):
            rows = slice(half * D // 2, (half + 1) * D // 2)
            out[k, rows, :] = dot_rows(left[:, rows], right[...]).astype(bf16)


def ffn_whole(run, feeds, lows, ups, hids):
    block, width = feeds[0].shape[0], ups[0].shape[1]
    return run(
        ffn_whole_kernel,
        [(a, None) for a in (*feeds, *lows, *ups, *hids)],
        [struct((2, D, width), bf16)],
        scratch=[pltpu.VMEM((4 * block, D), bf16), pltpu.VMEM((4 * block, width), bf16)],
        spill=1,
        name="ffn_whole",
    )[0]


def ffn_grad(run, orders, scal, feeds, lows, ups, hids):
    block, width = feeds[0].shape[0], ups[0].shape[1]
    out = struct((PARTS // 2, CHUNK, width), bf16)
    return run(
        functools.partial(ffn_grad_kernel, orders),
        [(scal, SMALL)] + [(a, None) for a in (*feeds, *lows, *ups, *hids)],
        [out] * 4,
        scratch=[pltpu.VMEM((4 * block, D), bf16), pltpu.VMEM((4 * block, width), bf16)],
        spill=4,
        name="ffn_grad",
    )


def join(target, a, b):
    rows = a.shape[0]
    target[:rows, :] = a[...]
    target[rows:, :] = b[...]


def mix_grad_kernel(orders, scal, *refs):
    normed, lows = refs[0:4], refs[4:8]
    in_low, mixed_a, mixed_b = refs[8:11]
    outs, (left, mixed) = refs[11:-2], refs[-2:]
    joined = len(outs) == 2
    channels = mixed.shape[1]
    join(mixed, mixed_a, mixed_b)
    core, index = scal[1], scal[3]
    groups = (
        (normed, in_low, slice(0, 2 * channels), 0, 0),
        (normed, in_low, slice(2 * channels, 3 * channels), 1, 0),
        (lows, mixed, slice(0, channels), 1, 1),
    )
    for source, rhs, cols, group, base in groups:
        own_a, own_b, got_a, got_b = source
        block = own_a.shape[0]
        for rows, at in halves(own_a, own_b, got_a, got_b, core):
            spread_columns(rows, left, pl.ds(at, block), index, orders[group])
        for half in range(2):
            out = outs[half if joined else 2 * group + half]
            first = base + 2 * group if joined else base
            wide = PARTS // 2 * CHUNK
            got = dot_rows(left[:, half * wide : (half + 1) * wide], rhs[:, cols]).astype(bf16)
            for part in range(PARTS // 2):
                for i in range(got.shape[1] // channels):
                    block_cols = slice(i * channels, (i + 1) * channels)
                    out[part, first + i] = got[part * CHUNK : (part + 1) * CHUNK, block_cols]


def mix_grad(run, orders, scal, normed, lows, in_low, mixed, joined):
    block, channels = normed[0].shape[0], mixed[0].shape[1]
    if joined:
        outs = [struct((PARTS // 2, 4, CHUNK, channels), bf16)] * 2
    else:
        outs = [struct((PARTS // 2, 2, CHUNK, channels), bf16)] * 4
    return run(
        functools.partial(mix_grad_kernel, orders),
        [(scal, SMALL)]
        + [(a, None) for a in (*normed, *lows, in_low, *mixed)],
        outs,
        scratch=[pltpu.VMEM((4 * block, D), bf16), pltpu.VMEM((4 * block, channels), bf16)],
        spill=len(outs),
        name="mix_grad",
    )


def halve_kernel(keep, got, sent, kept):
    count = keep.shape[0] // 2
    for i in range(count):
        kept[i] = (keep[i].astype(f32) + got[i].astype(f32)).astype(bf16)
        sent[i] = (keep[count + i].astype(f32) + got[count + i].astype(f32)).astype(bf16)


def halve(run, keep, got):
    out = struct((keep.shape[0] // 2, *keep.shape[1:]), bf16)
    return run(halve_kernel, [(keep, None), (got, None)], [out, out], spill=2, name="halve")


def total_of(refs, leads):
    return sum(ref[lead].astype(f32) for ref, lead in zip(refs, leads))


def finish_kernel(leads, turned, *refs):
    out, refs = refs[-1], list(refs[:-1])
    for layer, lead in enumerate(leads):
        total = total_of([refs.pop(0) for _ in lead], lead)
        out[layer] = total.T if turned else total


def ffn_finish(run, terms, turned):
    _, rows, cols = terms[0][0][0].shape
    shape = (cols, rows) if turned else (rows, cols)
    leads = [[lead for _, lead in pairs] for pairs in terms]
    return run(
        functools.partial(finish_kernel, leads, turned),
        [(a, None) for pairs in terms for a, _ in pairs],
        [struct((len(terms), *shape), f32)],
        name="ffn_finish",
    )[0]


def mix_finish_kernel(plan, *refs):
    into, out = refs[-2:]
    for layer, streams in enumerate(plan):
        for stream, parts in enumerate(streams):
            total = sum(refs[k][lead].astype(f32) for k, lead in parts)
            if stream < STREAMS:
                into[layer, stream] = total
            else:
                out[layer] = total.T


def mix_finish(run, arrays, plan):
    rows, channels = arrays[0].shape[-2:]
    return run(
        functools.partial(mix_finish_kernel, plan),
        [(a, None) for a in arrays],
        [struct((len(plan), STREAMS, rows, channels), f32), struct((len(plan), channels, rows), f32)],
        name="mix_finish",
    )


def pack_kernel(mix, filt, narrow, up_a, up_b, feed_a, feed_b, in_a, in_b, own, down, out):
    channels = mix.shape[1]
    out[:16, :] = mix[...]
    out[ROW_FILTER : ROW_FILTER + FILT, :] = filt[...]
    for q in range(D // channels):
        cols = slice(q * channels, (q + 1) * channels)
        out[ROW_UP_BIAS + q : ROW_UP_BIAS + q + 1, :] = up_a[:, cols] + up_b[:, cols]
        wide = [feed_a[i : i + 1, cols] + feed_b[i : i + 1, cols] for i in range(3)]
        wide.append(down[:, cols])
        wide += [in_a[i : i + 1, cols] + in_b[i : i + 1, cols] for i in range(2)]
        wide += [own[i : i + 1, cols] for i in range(2)]
        for i, value in enumerate(wide):
            at = ROW_WIDE + 4 * i + q
            out[at : at + 1, :] = value
    groups = [
        narrow[i * NARROW_GROUP : (i + 1) * NARROW_GROUP, :] for i in range(channels // FILT)
    ]
    out[ROW_NARROW:, :] = jnp.concatenate(groups, axis=1)


def pack(run, mix, filt, narrow, ups, feeds, ins, own, down):
    return run(
        pack_kernel,
        [(a, None) for a in (mix, filt, narrow, *ups, *feeds, *ins, own, down)],
        [struct((PACK_ROWS, mix.shape[1]), f32)],
        name="pack_small",
    )[0]


def gate(run, after=()):
    run(lambda: None, [], [], name="gate", after=after)


def stack_kernel(*refs):
    size = refs[0].shape[0]
    total, low = refs[-2:]
    for i, ref in enumerate(refs[:-2]):
        total[i * size : (i + 1) * size, :] = ref[...]
        low[i * size : (i + 1) * size, :] = ref[...].astype(bf16)


def stack_packs(run, packs):
    rows, cols = packs[0].shape
    shape = (len(packs) * rows, cols)
    return run(
        stack_kernel, [(a, None) for a in packs], [struct(shape, f32), struct(shape, bf16)], name="stack_packs"
    )


def add_small_kernel(value, got, total, low):
    added = value[...] + got[...].astype(f32)
    total[...] = added
    low[...] = added.astype(bf16)


def add_small(run, value, got):
    outs = [struct(value.shape, f32), struct(value.shape, bf16)]
    return run(add_small_kernel, [(value, None), (got, None)], outs, name="add_small")


def last_small_kernel(value, got, total, wide):
    added = value[...] + got[...].astype(f32)
    total[...] = added
    size = PACK_ROWS - ROW_WIDE
    for i in range(value.shape[0] // PACK_ROWS):
        wide[i * size : (i + 1) * size, :] = added[i * PACK_ROWS + ROW_WIDE : (i + 1) * PACK_ROWS, :]


def last_small(run, value, got):
    rows, cols = value.shape
    wide = struct((rows // PACK_ROWS * (PACK_ROWS - ROW_WIDE), cols), f32)
    return run(
        last_small_kernel, [(value, None), (got, None)], [struct(value.shape, f32), wide], name="last_small"
    )


def sum_kernel(a, b, out):
    out[...] = a[...] + b[...]


def add_pair(run, a, b):
    return run(sum_kernel, [(a, None), (b, None)], [struct(a.shape, f32)], name="add_pair")[0]


def unpack_kernel(layers, *refs):
    (chans, wides), outs = refs[:2], refs[2:]
    (gain, shift, out_bias, feed_gain, feed_shift, down_bias, in_bias, conv_w, conv_b, skip, filt, up_bias,
     w_in, b_in, f_in, w_mid, b_mid, f_mid) = outs
    channels = chans.shape[1]
    size = PACK_ROWS - ROW_WIDE
    for layer in range(layers):
        chan = chans[layer * PACK_ROWS : (layer + 1) * PACK_ROWS, :]
        wide = wides[layer * size : (layer + 1) * size, :]
        row = slice(layer, layer + 1)

        def spread(target, ref, at, row=row):
            for q in range(D // channels):
                target[row, q * channels : (q + 1) * channels] = ref[at + q : at + q + 1, :]

        spread(feed_gain, wide, 0)
        spread(feed_shift, wide, 4)
        spread(out_bias, wide, 8)
        spread(down_bias, wide, 12)
        if layer + 1 < layers:
            spread(gain, wide, 16, slice(layer + 1, layer + 2))
            spread(shift, wide, 20, slice(layer + 1, layer + 2))
        if layer == 0:
            spread(gain, wide, 24)
            spread(shift, wide, 28)
        spread(up_bias, chan, ROW_UP_BIAS)
        for stream in range(STREAMS):
            in_bias[stream, row, :] = chan[ROW_IN_BIAS + stream : ROW_IN_BIAS + stream + 1, :]
            conv_b[stream, row, :] = chan[ROW_CONV_B + stream : ROW_CONV_B + stream + 1, :]
            for lag in range(SHORT):
                at = ROW_CONV_W + stream * SHORT + lag
                conv_w[stream, lag, row, :] = chan[at : at + 1, :]
        skip[row, :] = chan[ROW_SKIP : ROW_SKIP + 1, :]
        filt[layer] = chan[ROW_FILTER : ROW_FILTER + FILT, :]
        base = ROW_NARROW - ROW_WIDE
        rows = slice(base, base + NARROW_GROUP)
        narrow = jnp.concatenate(
            [wide[rows, i * FILT : (i + 1) * FILT] for i in range(channels // FILT)], axis=0
        )
        for target, at in ((b_in, NB_IN), (f_in, NF_IN), (b_mid, NB_MID), (f_mid, NF_MID)):
            target[row, :] = narrow[at : at + 1, :]
        w_in[layer] = narrow[:POS, :]
        w_mid[layer] = narrow[NW_MID : NW_MID + FILT, :]


def unpack(run, chans, wides, up_width):
    layers, channels = chans.shape[0] // PACK_ROWS, chans.shape[1]
    return run(
        functools.partial(unpack_kernel, layers),
        [(chans, None), (wides, None)],
        [struct((layers, D), f32)] * 6
        + [
            struct((STREAMS, layers, channels), f32),
            struct((STREAMS, SHORT, layers, channels), f32),
            struct((STREAMS, layers, channels), f32),
            struct((layers, channels), f32),
            struct((layers, FILT, channels), f32),
            struct((layers, up_width), f32),
            struct((layers, POS, FILT), f32),
            struct((layers, FILT), f32),
            struct((layers, FILT), f32),
            struct((layers, FILT, FILT), f32),
            struct((layers, FILT), f32),
            struct((layers, FILT), f32),
        ],
        name="unpack_small",
    )


def dp_swap(x, stride):
    size = lax.axis_size("dp")
    return lax.ppermute(x, "dp", [(i, i ^ stride) for i in range(size)])


class Scatter:
    def __init__(self, run, sent, keep, strides):
        self.run, self.keep = run, keep
        self.strides = list(strides)
        self.got = dp_swap(sent, self.strides.pop(0))

    def step(self):
        sent, self.keep = halve(self.run, self.keep, self.got)
        self.got = dp_swap(sent, self.strides.pop(0))

    def pair(self):
        while self.strides:
            self.step()
        return self.keep, self.got


class SmallSum:
    def __init__(self, run, packs, strides):
        self.run, self.strides = run, list(strides)
        self.value, low = stack_packs(run, packs)
        self.got = dp_swap(low, self.strides.pop(0))

    def step(self):
        self.value, low = add_small(self.run, self.value, self.got)
        self.got = dp_swap(low, self.strides.pop(0))

    def sums(self):
        return last_small(self.run, self.value, self.got)


def share_out(pair):
    keep, got = pair
    total = (keep[0].astype(f32) + got[0].astype(f32)).reshape(-1, CHUNK, keep.shape[-1])
    left = lax.axis_size("dp") // PARTS
    index = lax.axis_index("dp")
    stride = 1
    total = total.reshape(total.shape[0], left, CHUNK // left, -1)
    while left > 1:
        total = total.reshape(total.shape[0], left // 2, 2, total.shape[2], -1)
        bit = (index // stride) % 2
        mine = lax.dynamic_index_in_dim(total, bit, 2, keepdims=False)
        other = lax.dynamic_index_in_dim(total, 1 - bit, 2, keepdims=False)
        total = mine + dp_swap(other.astype(bf16), stride).astype(f32)
        left, stride = left // 2, stride * 2
    return total[:, 0]


def shards(
    tokens,
    seg_lengths,
    cotangent,
    mixer_norm_gain,
    mixer_norm_bias,
    in_weight,
    in_bias,
    conv_weight,
    conv_bias,
    filter_in,
    filter_in_bias,
    filter_in_freq,
    filter_mid,
    filter_mid_bias,
    filter_mid_freq,
    filter_out,
    skip_bias,
    out_weight,
    out_bias,
    feed_norm_gain,
    feed_norm_bias,
    feed_up,
    feed_up_bias,
    feed_down,
    feed_down_bias,
):
    block = tokens.shape[1]
    length = block * lax.axis_size("mp")
    channels = in_weight.shape[3]
    layers = in_weight.shape[0]
    spot = lax.axis_index("mp").astype(jnp.int32)
    left = lax.axis_size("dp") // PARTS
    chunk = (lax.axis_index("dp") // left).astype(jnp.int32)
    scal = jnp.stack([seg_lengths[0, 0], spot % 2, spot // 2, chunk, spot])
    table = wave_table(length)
    waves = jnp.asarray(table)
    waves_t = jnp.asarray(np.ascontiguousarray(table.T))
    pos = jnp.asarray(position_table(length))
    run = Chain()

    in_w = in_weight.transpose(0, 2, 1, 3)
    in_b = in_bias.transpose(1, 0, 2)
    conv_w = conv_weight.transpose(1, 2, 0, 3)
    conv_b = conv_bias.transpose(1, 0, 2)
    filter_weights = (
        filter_in, filter_in_bias, filter_in_freq, filter_mid, filter_mid_bias, filter_mid_freq, filter_out
    )
    both = range(2)

    def start_sum(ends):
        got = [core_swap(ends[i]) for i in both]
        out = []
        for i in both:
            here = add_low(run, ends[2 + i], got[i])
            out.append((here, chip_swap(here)))
        return out

    def one_sum(sent, keep):
        here = add_low(run, keep, core_swap(sent))
        return here, chip_swap(here)

    def in_turn(first, pace=None):
        gate(run, [first[1]])
        if pace is None:
            gate(run)
        else:
            pace.step()

    mine = tokens[0]
    other = chip_swap(mine)
    filt = [None] * layers
    early = tuple(stay(a) for a in filter_weights)
    filt[0] = filter_fwd(run, 0, length, scal, stay(pos), early, stay(waves))
    low_a, low_b, res_a, res_b, cot = first_norm(
        run, scal, stay(mine), other, stay(mixer_norm_gain), stay(mixer_norm_bias), stay(cotangent[0])
    )
    res, low = [res_a, res_b], [low_a, low_b]

    def in_halves(prepare, work, sums):
        out = []
        for i in both:
            prepare(i)
            sent, keep = work(i)
            if i == 0 and sums is not None:
                in_turn(sums[1])
            if i == 1:
                in_turn(out[0])
            out.append(one_sum(sent, keep))
        return out

    stored, cot_parts = [], []
    back = [None, None]
    got = [core_swap(x) for x in low]
    cot_other = chip_swap(cot)
    sums = None
    for layer in range(layers):
        last = layer + 1 == layers
        saved, passed, middle, feed, feed_got, ffn = [], [None], [], [], [], []
        if layer:
            res, low, got = [], [], []

        def mix_prepare(i):
            if layer:
                b, a = add_norm(
                    run, layer - 1, layer, *sums[i], stored[layer - 1][5][i],
                    feed_down_bias, mixer_norm_gain, mixer_norm_bias, 1,
                )
                res.append(a)
                low.append(b)
                got.append(core_swap(b))

        def mix_work(i):
            kept, on, sent, keep = mix_fwd(
                run, layer, i, scal, low[i], got[i], in_w, in_b, conv_w, conv_b, skip_bias, filt[layer][0],
                out_weight, waves, waves_t, passed[-1],
            )
            saved.append(kept)
            passed.append(on)
            if layer == 0 and i == 0:
                cot_parts.extend(first_grad(run, scal, cot, cot_other))
            return sent, keep

        def feed_prepare(i):
            b, a = add_norm(run, layer, layer, *sums[i], res[i], out_bias, feed_norm_gain, feed_norm_bias)
            middle.append(a)
            feed.append(b)
            feed_got.append(core_swap(b))

        def feed_work(i):
            ffn.append(ffn_fwd(run, layer, feed[i], feed_got[i], feed_up, feed_up_bias, feed_down))
            if i == 0 and not last:
                filt[layer + 1] = filter_fwd(
                    run, layer + 1, length, scal, pos, filter_weights, waves
                )
            if not last:
                return ffn[i][2], ffn[i][3]
            back[i] = ffn_bwd(run, layer, cot_low[i], cot_got[i], feed_up, feed_down, ffn[i][0], True)
            return back[i][2], back[i][3]

        sums = in_halves(mix_prepare, mix_work, sums)
        if layer == 0:
            cot_sum, *cot_low = cot_parts
            cot_got = [core_swap(x) for x in cot_low]
        stored.append(
            (res, (*low, *got), saved, passed[2][1], [kept[2] for kept in saved], middle, feed, feed_got, ffn)
        )
        sums = in_halves(feed_prepare, feed_work, sums)
    back_sums = sums

    rising, turned = (1, 2, 4), (2, 4, 1)
    feed_orders, mix_orders = (rising, turned), (rising, rising)

    def scatter_pair(sends, orders):
        return [
            Scatter(run, sends[2 * k + 1], sends[2 * k], [left * o for o in orders[k]]) for k in range(2)
        ]

    def scatter_rows(whole_grad):
        return lax.psum_scatter(whole_grad, "dp", scatter_dimension=1, tiled=True)

    def grad_args(layer, low, got, back):
        feed, feed_got, ffn = stored[layer][6:]
        return (
            (feed[0], feed_got[0], feed[1], feed_got[1]),
            (low[0], got[0], low[1], got[1]),
            [back[i][1] for i in both],
            [ffn[i][1] for i in both],
        )

    grad, low, got = cot_low, cot_low, cot_got
    down_sum = cot_sum
    moves = back_sums
    feed_shares, mix_rest, packs = ([None] * layers for _ in range(3))
    no_sums = jnp.zeros((8, D), f32)
    in_sums = [no_sums, no_sums]
    for layer in reversed(range(layers)):
        above = layer + 1
        entry, normed, saved, spec, mixed, middle, feed, feed_got, ffn = stored[layer]
        if layer:
            feed_whole = ffn_whole(run, *grad_args(layer, low, got, back))
        else:
            feed_sends = ffn_grad(
                run, [parts_order(o) for o in feed_orders], scal, *grad_args(layer, low, got, back)
            )
        if above == layers:
            out_got = [core_swap(ffn[i][2]) for i in both]
            out_send, out_mine = pick_outputs(
                run, layer, scal, [ffn[i][3] for i in both], out_got, middle, feed_down_bias
            )
        new_grad, low, feed_sums = [], [], []
        for i in both:
            a, c, b = norm_back(run, layer, *moves[i], middle[i], grad[i], feed_norm_gain, 1)
            new_grad.append(a)
            low.append(b)
            feed_sums.append(c)
        grad = new_grad
        got = [core_swap(x) for x in low]
        rows = (*low, *got)
        if layer:
            feed_shares[layer] = scatter_rows(run.release([feed_whole])[0])
        else:
            feed_sends[1], feed_sends[3] = run.release([feed_sends[1], feed_sends[3]])
            up_big, down_big = scatter_pair(feed_sends, feed_orders)
        in_low, taps_grad, mix_sums, *ends = mix_bwd(
            run, layer, scal, rows, out_weight, saved, spec, in_w, conv_w, conv_b, skip_bias,
            filt[layer][0], waves, waves_t,
        )
        if layer:
            if above == layers:
                outputs = last_add(run, out_mine, chip_swap(out_send))
            moves = start_sum(ends)
            own_sums = no_sums
            mix_keep, mix_sent = mix_grad(
                run, [parts_order(rising)] * 2, scal, normed, rows, in_low, mixed, True
            )
        else:
            swapped = [core_swap(ends[i]) for i in both]
        filt_out, narrow = filter_bwd(run, layer, length, scal, taps_grad, pos, filter_weights, filt[layer][1])
        if layer == 0:
            for x in mix_rest[1:]:
                x.step()
            up_big.step()
            send, own, own_sums = last_pick(run, scal, ends[2:], swapped, entry)
            there = chip_swap(send)
            down_big.step()
        packs[layer] = pack(
            run, mix_sums, filt_out, narrow, [back[i][0] for i in both], feed_sums, in_sums, own_sums, down_sum
        )
        if layer == 0:
            small = SmallSum(
                run, packs, [1 << i for i in range(left.bit_length() - 1)] + [left * o for o in rising]
            )
            sends = mix_grad(
                run, [parts_order(o) for o in mix_orders], scal, normed, rows, in_low, mixed, False
            )
            small.step()
            sends[1], sends[3] = run.release([sends[1], sends[3]])
            mix_bigs = scatter_pair(sends, mix_orders)
            up_big.step()
            for x in mix_rest[1:]:
                x.step()
            break
        new_grad, new_low, in_sums, new_got, new_back, back_sums = [], [], [], [], [], []

        def norm_half(i):
            a, c, b = norm_back(run, layer, *moves[i], entry[i], grad[i], mixer_norm_gain)
            new_grad.append(a)
            new_low.append(b)
            in_sums.append(c)
            new_got.append(core_swap(b))

        def ffn_half(i):
            below = stored[layer - 1][8]
            new_back.append(
                ffn_bwd(run, layer - 1, new_low[i], new_got[i], feed_up, feed_down, below[i][0], False)
            )

        def sum_half(i):
            back_sums.append(one_sum(new_back[i][2], new_back[i][3]))

        norm_half(0)
        mix_rest[layer] = Scatter(run, run.release([mix_sent])[0], mix_keep, [left * o for o in rising])
        ffn_half(0)
        in_turn(moves[1])
        sum_half(0)
        norm_half(1)
        ffn_half(1)
        in_turn(back_sums[0])
        sum_half(1)
        moves = back_sums
        back = new_back
        down_sum = (in_sums[0] + in_sums[1])[2:3]
        grad, low, got = new_grad, new_low, new_got
    token_grad = last_back(run, 0, scal, own, there, entry, grad, mixer_norm_gain)
    while small.strides:
        small.step()
    down_big.step()
    mix_bigs[0].step()
    small_sums, wide = small.sums()
    wide_got = chip_swap(wide)
    mix_bigs[1].step()
    wide = add_pair(run, wide, wide_got)
    wide_got = core_swap(wide)
    mix_bigs[0].step()
    mix_bigs[1].step()
    (gain, shift, out_bias_g, feed_gain, feed_shift, down_bias_g, in_bias_g, conv_w_g, conv_b_g, skip_g, filt_g,
     up_bias_g, w_in_g, b_in_g, f_in_g, w_mid_g, b_mid_g, f_mid_g) = unpack(
        run, small_sums, add_pair(run, wide, wide_got), feed_up.shape[2]
    )
    up_pair, down_pair = up_big.pair(), down_big.pair()
    if left == 1:
        up_first, down_first = [[(a, 0) for a in pair] for pair in (up_pair, down_pair)]
    else:
        up_first, down_first = [[(share_out(pair), 0)] for pair in (up_pair, down_pair)]
    up_g = ffn_finish(run, [up_first] + [[(a, 0)] for a in feed_shares[1:]], False)
    down_g = ffn_finish(run, [down_first] + [[(a, 1)] for a in feed_shares[1:]], True)
    mix_pairs = [x.pair() for x in mix_bigs]
    if left == 1:
        arrays = [a for pair in mix_pairs for a in pair]
        first = [[(2 * k, (0, i)), (2 * k + 1, (0, i))] for k in both for i in both]
    else:
        arrays = [share_out(pair) for pair in mix_pairs]
        first = [[(k, i)] for k in both for i in both]
    plan = [first]
    for x in mix_rest[1:]:
        pair = x.pair()
        if left == 1:
            plan.append([[(len(arrays), (0, i)), (len(arrays) + 1, (0, i))] for i in range(STREAMS + 1)])
            arrays += pair
        else:
            plan.append([[(len(arrays), i)] for i in range(STREAMS + 1)])
            arrays.append(share_out(pair))
    in_g, out_g = mix_finish(run, arrays, plan)
    return (
        outputs[None],
        token_grad[None],
        gain,
        shift,
        in_g.transpose(0, 2, 1, 3),
        in_bias_g.transpose(1, 0, 2),
        conv_w_g.transpose(2, 0, 1, 3),
        conv_b_g.transpose(1, 0, 2),
        w_in_g,
        b_in_g,
        f_in_g,
        w_mid_g,
        b_mid_g,
        f_mid_g,
        filt_g,
        skip_g,
        out_g,
        out_bias_g,
        feed_gain,
        feed_shift,
        up_g,
        up_bias_g,
        down_g,
        down_bias_g,
    )


def solution(mesh):
    in_specs = (
        P("dp", "mp", None),
        P("dp", None),
        P("dp", "mp", None),
        P(),
        P(),
        P(None, None, None, "mp"),
        P(None, None, "mp"),
        P(None, None, None, "mp"),
        P(None, None, "mp"),
        P(),
        P(),
        P(),
        P(),
        P(),
        P(),
        P(None, None, "mp"),
        P(None, "mp"),
        P(None, "mp", None),
        P(),
        P(),
        P(),
        P(None, None, "mp"),
        P(None, "mp"),
        P(None, "mp", None),
        P(),
    )
    out_specs = (
        P("dp", "mp", None),
        P("dp", "mp", None),
        P(),
        P(),
        P(None, "dp", None, "mp"),
        P(None, None, "mp"),
        P(None, None, None, "mp"),
        P(None, None, "mp"),
        P(),
        P(),
        P(),
        P(),
        P(),
        P(),
        P(None, None, "mp"),
        P(None, "mp"),
        P(None, "mp", "dp"),
        P(),
        P(),
        P(),
        P(None, "dp", "mp"),
        P(None, "mp"),
        P(None, "mp", "dp"),
        P(),
    )
    return jax.shard_map(shards, mesh=mesh, in_specs=in_specs, out_specs=out_specs, check_vma=False)
```
